32 devices in a mesh: row: 4 (over y, core), col: 8 (over z, x).
Axes of the slice: x: 2, y: 2, z: 4, core: 2. Of those that a mesh axis runs over, the one named last changes fastest.
Arguments:
- points: float32 [16, 16384], P(None, ('row', 'col')), may hold values from -0.125 to 1.125
- lengthscale: float32 [16], replicated, may hold values from 2 to 6, as said below
- noise_var: float32 [128], replicated, may hold values from 0.2 to 2
- groups: int32 [32], replicated, may hold values from 0 to 63
- targets: float32 [16384, 128], P(('row', 'col')), may hold values from -162 to 162, as said below
Outputs:
- solution_field: float32 [16384, 128], P(('row', 'col'))
- residual: float32 [16384, 128], P(('row', 'col'))
The draws below stay inside these ranges and needn't reach their ends.
Inputs may be any that keep to these rules, and one draw needn't show every extreme that they name: Observed targets, real-valued. `lengthscale`: length scales, positive.
All inputs are finite; a program needn't handle non-finite values.
Results may differ from the reference program's by a relative error of at most 0.029.
Values may be sent and summed in bfloat16 or wider, within the bound.
A program may use at most 64 MiB of HBM per device.

```python
import math
import jax
import jax.numpy as jnp
from jax import lax

DIMS = 16
RHS = 128
TILE = 512
GROUPS = 64
ITERS = 2
BPD = 1
NB = 32
ROWS = 16384
N_ROW = 4
N_COL = 8


def group_draw(key):
    level_key, place_key = jax.random.split(key)
    raw_level = jax.random.randint(level_key, (NB,), 0, 32768, dtype=jnp.int32)
    picked = raw_level * raw_level // 16777216
    placed = jax.random.permutation(place_key, NB).astype(jnp.int32)
    blocks = jnp.arange(NB, dtype=jnp.int32)
    picked = jnp.where(blocks == placed[0], 0, picked)
    picked = jnp.where(blocks == placed[1], GROUPS - 1, picked)
    return picked.astype(jnp.int32)


def draw_groups(key, part):
    return group_draw(key)


def draw_points(key, part):
    group_ids = group_draw(key)
    key = jax.random.fold_in(key, 7)
    center_key, jitter_key = jax.random.split(key)
    blocks = jnp.arange(NB, dtype=jnp.int32)
    same_group = group_ids[:, None] == group_ids[None, :]
    before = (blocks[None, :] < blocks[:, None]) & same_group
    ordinal = jnp.sum(before.astype(jnp.int32), axis=1)
    leader = ordinal - ordinal % 4
    matched = same_group & (ordinal[None, :] == leader[:, None])
    anchor = jnp.sum(jnp.where(matched, blocks[None, :], 0), axis=1).astype(jnp.int32)
    centers = jax.random.uniform(center_key, (DIMS, NB, TILE), jnp.float32, 0.0, 1.0)
    shared = jnp.take(centers, anchor, axis=1)
    jitter = jax.random.uniform(jitter_key, (DIMS, NB, TILE), jnp.float32, -0.115, 0.115)
    return (shared + jitter).reshape(DIMS, ROWS).astype(jnp.float32)


def draw_lengthscale(key, part):
    key = jax.random.fold_in(key, 5)
    order_key, jitter_key = jax.random.split(key)
    ranks = jax.random.permutation(order_key, DIMS).astype(jnp.float32)
    jitter = jax.random.uniform(jitter_key, (DIMS,), jnp.float32, 0.0, 1.0)
    exponent = (ranks + jitter) / DIMS
    return (2.0 * jnp.exp(math.log(3.0) * exponent)).astype(jnp.float32)


def draw_targets(key, part):
    key = jax.random.fold_in(key, 11)
    base_key, row_key, col_key = jax.random.split(key, 3)
    position = jnp.arange(ROWS, dtype=jnp.float32) / ROWS
    trend = (1.0 + 2.0 * position)[:, None]
    row_scale = jnp.exp(jax.random.uniform(row_key, (ROWS, 1), jnp.float32, math.log(0.3), math.log(3.0)))
    col_scale = jnp.exp(jax.random.uniform(col_key, (1, RHS), jnp.float32, math.log(0.3), math.log(3.0)))
    values = jnp.clip(jax.random.normal(base_key, (ROWS, RHS), jnp.float32), -6.0, 6.0)
    return (values * row_scale * col_scale * trend).astype(jnp.float32)


def setup_inputs(seed: int = 0) -> dict:
    streams_of = jax.random.split(jax.random.key(seed), 6)
    points = draw_points(jax.random.fold_in(streams_of[5], 71), 0)
    lengthscale = draw_lengthscale(jax.random.fold_in(streams_of[5], 71), 0)
    noise_var = jnp.clip(jnp.exp(jax.random.uniform(streams_of[2], (RHS,), jnp.float32, math.log(0.2), math.log(2.0))), 0.2, 2.0)
    groups = draw_groups(jax.random.fold_in(streams_of[5], 71), 0)
    targets = draw_targets(jax.random.fold_in(streams_of[5], 71), 0)
    return {"points": points, "lengthscale": lengthscale, "noise_var": noise_var, "groups": groups, "targets": targets}


def kernel_tile(row_coords, col_coords):
    row_norms = lax.optimization_barrier(jnp.sum(row_coords * row_coords, axis=0))
    col_norms = lax.optimization_barrier(jnp.sum(col_coords * col_coords, axis=0))
    crossed = lax.dot_general(row_coords, col_coords, (((0,), (0,)), ((), ())), precision=lax.Precision.HIGHEST, preferred_element_type=jnp.float32)
    squared = jnp.maximum(row_norms[:, None] + col_norms[None, :] - 2.0 * crossed, 0.0)
    radius = jnp.sqrt(squared)
    support = jnp.maximum(1.0 - radius, 0.0)
    return (support ** 11 * (11.0 * radius + 1.0)).astype(jnp.bfloat16)

def kernel_product(narrow, scaled, groups):
    blocks = N_ROW * N_COL * BPD
    vec_blocks = narrow.reshape(blocks, TILE, RHS)
    coord_blocks = jnp.transpose(scaled.reshape(DIMS, blocks, TILE), (1, 0, 2))

    def row_block(row_id):

        def per_class(class_col, running):

            def per_block(member, partial_value):
                col_id = ((member // BPD * N_COL + class_col) * BPD + member % BPD).astype(jnp.int32)

                def add_tile(summed):
                    values = kernel_tile(coord_blocks[row_id], coord_blocks[col_id])
                    return summed + jnp.dot(values, vec_blocks[col_id], preferred_element_type=jnp.float32)

                def keep_tile(summed):
                    return summed
                return lax.cond(groups[row_id] == groups[col_id], add_tile, keep_tile, partial_value)
            partial_value = lax.fori_loop(0, N_ROW * BPD, per_block, jnp.zeros((TILE, RHS), jnp.float32))
            rounded = lax.optimization_barrier(partial_value.astype(jnp.bfloat16))
            return running + rounded.astype(jnp.float32)
        return lax.fori_loop(0, N_COL, per_class, jnp.zeros((TILE, RHS), jnp.float32))
    return lax.map(row_block, jnp.arange(blocks, dtype=jnp.int32)).reshape(blocks * TILE, RHS)

def reference(points, lengthscale, noise_var, groups, targets):
    scaled = points / lengthscale[:, None]

    def operator_apply(vector):
        return noise_var[None, :] * vector + kernel_product(vector.astype(jnp.bfloat16), scaled, groups)
    solution_field = jnp.zeros_like(targets)
    residual = targets
    direction = targets
    norm_now = lax.optimization_barrier(jnp.sum(residual * residual, axis=0))
    for iteration in range(ITERS):
        image = operator_apply(direction)
        step_size = norm_now / lax.optimization_barrier(jnp.sum(direction * image, axis=0))
        solution_field = solution_field + step_size[None, :] * direction
        residual = residual - step_size[None, :] * image
        if iteration + 1 < ITERS:
            norm_next = lax.optimization_barrier(jnp.sum(residual * residual, axis=0))
            direction = residual + (norm_next / norm_now)[None, :] * direction
            norm_now = norm_next
    return (solution_field, residual)
```

```python
import functools

import jax
import jax.numpy as jnp
from jax import lax
from jax.experimental import pallas as pl
from jax.experimental.pallas import tpu as pltpu
from jax.sharding import PartitionSpec as P

TILE = 512
ITERS = 2
RHS = 128
CHUNK = 128
GATHER_LIMIT = 64
VMEM_LIMIT = 48 * 1024 * 1024


def split3(value):
    first = value.astype(jnp.bfloat16).astype(jnp.float32)
    rest = value - first
    second = rest.astype(jnp.bfloat16).astype(jnp.float32)
    return first, second, rest - second


def lifted(coords, factor, norm_at, one_at):
    wide = coords.astype(jnp.float32)
    parts = split3(jnp.sum(wide * wide, axis=0, keepdims=True))
    row = lax.broadcasted_iota(jnp.int32, wide.shape, 0)
    tail = jnp.where((row >= one_at) & (row < one_at + 3), 1.0, 0.0)
    for place, part in enumerate(parts):
        tail = jnp.where(row == norm_at + place, part, tail)
    return jnp.concatenate([wide * factor, tail], axis=0).astype(jnp.bfloat16)


def wendland(squared):
    safe = jnp.maximum(squared, 1e-30)
    radius = safe * lax.rsqrt(safe)
    support = jnp.maximum(1.0 - radius, 0.0)
    second = support * support
    third = second * support
    fourth = second * second
    eighth = fourth * fourth
    return ((eighth * third) * (12.0 - 11.0 * support)).astype(jnp.bfloat16)


def first_kernel(order, count, own, coords, source, field, tiles, image, narrow, sums,
                 left, right, built, vectors, vec_sems, tile_sems):
    total = count[0]

    def vector_copy(slot):
        return pltpu.make_async_copy(
            source.at[order[slot]], vectors.at[slot], vec_sems.at[slot]
        )

    def tile_copy(slot):
        return pltpu.make_async_copy(built.at[slot], tiles.at[slot], tile_sems.at[slot])

    def begin(slot, carry):
        vector_copy(slot).start()
        return carry

    lax.fori_loop(0, total, begin, 0)
    left[...] = lifted(own[...], 1.0, 0, 3).T
    image[...] = jnp.zeros_like(image)

    def one_tile(slot, carry):
        right[...] = lifted(coords[order[slot]], -2.0, 3, 0)
        vector_copy(slot).wait()
        for start in range(0, TILE, CHUNK):
            rows = pl.ds(start, CHUNK)
            squared = jnp.dot(left[rows, :], right[...], preferred_element_type=jnp.float32)
            values = wendland(squared)
            built[slot, rows, :] = values
            image[rows, :] += jnp.dot(values, vectors[slot], preferred_element_type=jnp.float32)
        tile_copy(slot).start()
        return carry

    lax.fori_loop(0, total, one_tile, 0)
    narrow[...] = image[...].astype(jnp.bfloat16)
    sums[0:1, :] = jnp.sum(field[...] * field[...], axis=0, keepdims=True)
    sums[1:2, :] = jnp.sum(field[...] * image[...], axis=0, keepdims=True)

    def finish(slot, carry):
        tile_copy(slot).wait()
        return carry

    lax.fori_loop(0, total, finish, 0)


def second_kernel(order, count, tiles, source, image, field, noise, norms, sums, after, curved,
                  built, vectors, twice, vec_sems, tile_sems):
    total = count[0]

    def vector_copy(slot):
        return pltpu.make_async_copy(
            source.at[order[slot]], vectors.at[slot], vec_sems.at[slot]
        )

    def tile_copy(slot):
        return pltpu.make_async_copy(tiles.at[slot], built.at[slot], tile_sems.at[slot])

    def begin(slot, carry):
        vector_copy(slot).start()
        tile_copy(slot).start()
        return carry

    lax.fori_loop(0, total, begin, 0)
    twice[...] = jnp.zeros_like(twice)

    def one_tile(slot, carry):
        vector_copy(slot).wait()
        tile_copy(slot).wait()
        twice[...] += jnp.dot(built[slot], vectors[slot], preferred_element_type=jnp.float32)
        return carry

    lax.fori_loop(0, total, one_tile, 0)
    variance = noise[...]
    squares = norms[0:1, :]
    step = squares / (variance * squares + norms[1:2, :])
    target = field[...]
    product = image[...]
    applied = variance * target + product
    residual = target - step * applied
    again = variance * residual + product - step * (variance * product + twice[...])
    after[...] = residual
    curved[...] = again
    sums[0:1, :] = jnp.sum(residual * residual, axis=0, keepdims=True)
    sums[1:2, :] = jnp.sum(residual * again, axis=0, keepdims=True)
    sums[2:3, :] = jnp.sum(residual * applied + target * again, axis=0, keepdims=True)


def gathered_plan(points, lengthscale, noise_var, groups, targets):
    blocks = groups.shape[0]
    dims = points.shape[0]
    rhs = targets.shape[1]
    axes = ("row", "col")
    here = lax.axis_index(axes)
    narrow_points = (points / lengthscale[:, None]).astype(jnp.bfloat16)
    coords = lax.all_gather(narrow_points, axes, axis=0, tiled=False)
    source = lax.all_gather(targets.astype(jnp.bfloat16), axes, axis=0, tiled=False)

    same = groups == lax.dynamic_index_in_dim(groups, here, 0, keepdims=False)
    count = jnp.sum(same.astype(jnp.int32)).reshape(1)
    ids = jnp.arange(blocks, dtype=jnp.int32)
    place = jnp.cumsum(same.astype(jnp.int32)) - 1
    order = jnp.sum(
        jnp.where(same[None, :] & (place[None, :] == ids[:, None]), ids[None, :], 0), axis=1
    ).astype(jnp.int32)

    vmem = pl.BlockSpec(memory_space=pltpu.VMEM)
    smem = pl.BlockSpec(memory_space=pltpu.SMEM)
    anywhere = pl.BlockSpec(memory_space=pl.ANY)
    whole = jax.ShapeDtypeStruct((TILE, rhs), jnp.float32)
    few = jax.ShapeDtypeStruct((8, rhs), jnp.float32)
    tiles, image, narrow, sums = pl.pallas_call(
        first_kernel,
        out_shape=[
            jax.ShapeDtypeStruct((blocks, TILE, TILE), jnp.bfloat16),
            whole,
            jax.ShapeDtypeStruct((TILE, rhs), jnp.bfloat16),
            few,
        ],
        in_specs=[smem, smem, vmem, vmem, anywhere, vmem],
        out_specs=[anywhere, vmem, vmem, vmem],
        scratch_shapes=[
            pltpu.VMEM((TILE, 2 * dims), jnp.bfloat16),
            pltpu.VMEM((2 * dims, TILE), jnp.bfloat16),
            pltpu.VMEM((blocks, TILE, TILE), jnp.bfloat16),
            pltpu.VMEM((blocks, TILE, rhs), jnp.bfloat16),
            pltpu.SemaphoreType.DMA((blocks,)),
            pltpu.SemaphoreType.DMA((blocks,)),
        ],
        compiler_params=pltpu.CompilerParams(vmem_limit_bytes=VMEM_LIMIT),
        name="first_product",
    )(order, count, narrow_points, coords, source, targets)

    source = lax.all_gather(narrow, axes, axis=0, tiled=False)
    norms = lax.psum(sums, axes)
    variance = noise_var[None, :]
    sums, residual, again = pl.pallas_call(
        second_kernel,
        out_shape=[few, whole, whole],
        in_specs=[smem, smem, anywhere, anywhere, vmem, vmem, vmem, vmem],
        out_specs=[vmem, vmem, vmem],
        scratch_shapes=[
            pltpu.VMEM((blocks, TILE, TILE), jnp.bfloat16),
            pltpu.VMEM((blocks, TILE, rhs), jnp.bfloat16),
            pltpu.VMEM((TILE, rhs), jnp.float32),
            pltpu.SemaphoreType.DMA((blocks,)),
            pltpu.SemaphoreType.DMA((blocks,)),
        ],
        compiler_params=pltpu.CompilerParams(vmem_limit_bytes=VMEM_LIMIT),
        name="second_product",
    )(order, count, tiles, source, image, targets, variance, norms)

    last = lax.psum(sums, axes)
    squares = norms[0:1]
    curve = variance * squares + norms[1:2]
    step = squares / curve
    ratio = last[0:1] / squares
    second_curve = last[1:2] + ratio * (last[2:3] + ratio * curve)
    second_step = last[0:1] / second_curve
    direction = residual + ratio * targets
    applied = variance * targets + image
    solution_field = step * targets + second_step * direction
    residual = residual - second_step * (again + ratio * applied)
    return (solution_field, residual)


def kernel_tile(row_coords, col_coords):
    row_norms = jnp.sum(row_coords * row_coords, axis=0)
    col_norms = jnp.sum(col_coords * col_coords, axis=0)
    crossed = lax.dot_general(
        row_coords,
        col_coords,
        (((0,), (0,)), ((), ())),
        precision=lax.Precision.HIGHEST,
        preferred_element_type=jnp.float32,
    )
    squared = jnp.maximum(row_norms[:, None] + col_norms[None, :] - 2.0 * crossed, 0.0)
    radius = jnp.sqrt(squared)
    support = jnp.maximum(1.0 - radius, 0.0)
    return (support**11 * (11.0 * radius + 1.0)).astype(jnp.bfloat16)


def per_device(points, lengthscale, noise_var, groups, targets):
    n_row = lax.axis_size("row")
    n_col = lax.axis_size("col")
    own_blocks = targets.shape[0] // TILE
    row_blocks = own_blocks * n_col
    col_blocks = own_blocks * n_row
    scaled = points / lengthscale[:, None]
    row_coords = lax.all_gather(scaled.astype(jnp.bfloat16), "col", axis=1, tiled=True).astype(
        scaled.dtype
    )
    col_coords = lax.all_gather(scaled.astype(jnp.bfloat16), "row", axis=1, tiled=True).astype(
        scaled.dtype
    )
    row_place = lax.axis_index("row")
    col_place = lax.axis_index("col")
    row_groups = lax.dynamic_slice_in_dim(groups, row_place * row_blocks, row_blocks, 0)
    col_groups = lax.dynamic_index_in_dim(
        groups.reshape(n_row, n_col, own_blocks), col_place, 1, keepdims=False
    ).reshape(col_blocks)
    flat_mask = (row_groups[:, None] == col_groups[None, :]).reshape(row_blocks * col_blocks)
    tile_count = jnp.sum(flat_mask.astype(jnp.int32))
    tile_order = jnp.nonzero(flat_mask, size=row_blocks * col_blocks, fill_value=0)[0].astype(
        jnp.int32
    )

    def square_sums(vector):
        return lax.psum(jnp.sum(vector * vector, axis=0), ("row", "col"))

    solution_field = jnp.zeros_like(targets)
    residual = targets
    direction = targets
    norm_now = square_sums(residual)
    for iteration in range(ITERS):
        narrow = direction.astype(jnp.bfloat16)
        operator_source = lax.all_gather(narrow, "row", axis=0, tiled=True)
        source = operator_source
        initial = jnp.zeros((row_blocks * TILE, RHS), jnp.float32)

        def one_tile(position, summed):
            flat_index = tile_order[position]
            row_slot = flat_index // col_blocks
            col_slot = flat_index % col_blocks
            left = lax.dynamic_slice_in_dim(row_coords, row_slot * TILE, TILE, 1)
            right = lax.dynamic_slice_in_dim(col_coords, col_slot * TILE, TILE, 1)
            values = kernel_tile(left, right)
            block_vec = lax.dynamic_slice_in_dim(source, col_slot * TILE, TILE, 0)
            product = jnp.dot(values, block_vec, preferred_element_type=jnp.float32)
            current = lax.dynamic_slice_in_dim(summed, row_slot * TILE, TILE, 0)
            return lax.dynamic_update_slice_in_dim(summed, current + product, row_slot * TILE, 0)

        partial_value = lax.fori_loop(0, tile_count, one_tile, initial)
        outgoing = partial_value.astype(jnp.bfloat16).reshape(n_col, own_blocks * TILE, RHS)
        incoming = lax.all_to_all(outgoing, "col", split_axis=0, concat_axis=0, tiled=True)
        operator_product = jnp.sum(incoming, axis=0, dtype=jnp.float32)
        image = noise_var[None, :] * direction + operator_product
        curve = lax.psum(jnp.sum(direction * image, axis=0), ("row", "col"))
        step_size = norm_now / curve
        solution_field = solution_field + step_size[None, :] * direction
        residual = residual - step_size[None, :] * image
        if iteration + 1 < ITERS:
            norm_next = square_sums(residual)
            direction = residual + (norm_next / norm_now)[None, :] * direction
            norm_now = norm_next
    return (solution_field, residual)


def solution(mesh):
    placed = (P(None, ("row", "col")), P(), P(), P(), P(("row", "col"), None))

    def plan(points, lengthscale, noise_var, groups, targets):
        whole_field = groups.shape[0] <= GATHER_LIMIT and groups.shape[0] == mesh.size
        run = gathered_plan if whole_field else per_device
        return run(points, lengthscale, noise_var, groups, targets)

    return jax.shard_map(
        plan,
        mesh=mesh,
        in_specs=placed,
        out_specs=(P(("row", "col"), None), P(("row", "col"), None)),
        check_vma=False,
    )
```

```python
import functools

import functools

import jax
import jax.numpy as jnp
from jax import lax
from jax.experimental import pallas as pl
from jax.experimental.pallas import tpu as pltpu
from jax.sharding import PartitionSpec as P

TILE = 512
ITERS = 2
RHS = 128
CHUNK = 128
GATHER_LIMIT = 64
VMEM_LIMIT = 48 * 1024 * 1024
MESH = pl.DeviceIdType.MESH


def split3(value):
    first = value.astype(jnp.bfloat16).astype(jnp.float32)
    rest = value - first
    second = rest.astype(jnp.bfloat16).astype(jnp.float32)
    return first, second, rest - second


def lifted(coords, factor, norm_at, one_at):
    wide = coords.astype(jnp.float32)
    parts = split3(jnp.sum(wide * wide, axis=0, keepdims=True))
    row = lax.broadcasted_iota(jnp.int32, wide.shape, 0)
    tail = jnp.where((row >= one_at) & (row < one_at + 3), 1.0, 0.0)
    for place, part in enumerate(parts):
        tail = jnp.where(row == norm_at + place, part, tail)
    return jnp.concatenate([wide * factor, tail], axis=0).astype(jnp.bfloat16)


def wendland(squared):
    safe = jnp.maximum(squared, 1e-30)
    radius = safe * lax.rsqrt(safe)
    support = jnp.maximum(1.0 - radius, 0.0)
    second = support * support
    third = second * support
    fourth = second * second
    eighth = fourth * fourth
    return ((eighth * third) * (12.0 - 11.0 * support)).astype(jnp.bfloat16)


def place():
    row, col = lax.axis_index("row"), lax.axis_index("col")
    return row // 2, lax.rem(row, 2), col // 2, lax.rem(col, 2)


def greet(targets):
    barrier = pltpu.get_barrier_semaphore()
    for target in targets:
        pl.semaphore_signal(barrier, inc=1, device_id=target, device_id_type=MESH)
    pl.semaphore_wait(barrier, len(targets))


def spread(n_col, cut, own, out, send_sems, recv_sems, own_sem):
    y, core, z, x = place()
    depth = n_col // 2
    height = own.shape[0]
    parts = (pl.ds(0, cut), pl.ds(cut, height - cut))

    def device(y, core, z, x):
        return (2 * y + core, 2 * z + x)

    def number(y, core, z, x):
        return (2 * y + core) * n_col + 2 * z + x

    def level(step):
        return lax.rem(z + step, depth)

    over_x, over_y = device(y, core, z, 1 - x), device(1 - y, core, z, x)
    over_core = device(y, 1 - core, z, x)
    over_z = [device(y, core, level(depth - step), x) for step in range(1, depth)]
    greet([over_x, over_y, over_core] + over_z)
    started = []

    def send(block, half, target, first=False):
        spot = out.at[block, parts[half], :]
        copy = pltpu.make_async_remote_copy(
            src_ref=own.at[parts[half], :] if first else spot,
            dst_ref=spot,
            send_sem=send_sems.at[len(started)],
            recv_sem=recv_sems.at[block, half],
            device_id=target,
            device_id_type=MESH,
        )
        copy.start()
        started.append(copy)

    def arrived(block, half):
        spot = out.at[block, parts[half], :]
        pltpu.make_async_copy(spot, spot, recv_sems.at[block, half]).wait()

    def pass_on(block, first=False):
        send(block, 0, over_x, first)
        send(block, 1, over_y, first)
        send(block, 0, over_y, first)
        send(block, 1, over_x, first)
        send(block, 0, over_core, first)
        send(block, 1, over_core, first)

    me = number(y, core, z, x)
    for target in over_z:
        send(me, 0, target, True)
        send(me, 1, target, True)
    pass_on(me, True)
    keep = pltpu.make_async_copy(own, out.at[me], own_sem)
    keep.start()
    for step in range(depth + 2):
        if 0 < step < depth:
            block = number(y, core, level(step), x)
            arrived(block, 0)
            arrived(block, 1)
            pass_on(block)
        if 0 < step <= depth:
            here = level(step - 1)
            block = number(y, core, here, 1 - x)
            arrived(block, 0)
            send(block, 0, over_y)
            send(block, 0, over_core)
            block = number(1 - y, core, here, x)
            arrived(block, 1)
            send(block, 1, over_x)
            send(block, 1, over_core)
        if step >= 2:
            here = level(step - 2)
            for block, half in (
                (number(1 - y, core, here, x), 0),
                (number(y, core, here, 1 - x), 1),
                (number(1 - y, core, here, 1 - x), 0),
                (number(1 - y, core, here, 1 - x), 1),
            ):
                arrived(block, half)
                send(block, half, over_core)
    for step in range(depth):
        for other_y in (y, 1 - y):
            for other_x in (x, 1 - x):
                block = number(other_y, 1 - core, level(step), other_x)
                arrived(block, 0)
                arrived(block, 1)
    keep.wait()
    for copy in started:
        copy.wait_send()


def first_gather(n_col, points, scale, targets, out, own, send_sems, recv_sems, own_sem):
    scaled = (points[...] / scale[...]).astype(jnp.bfloat16)
    own[0:TILE, :] = targets[...].astype(jnp.bfloat16)
    dims, lanes = points.shape[0], targets.shape[1]
    for part in range(TILE // lanes):
        own[TILE + part * dims:TILE + (part + 1) * dims, :] = scaled[:, part * lanes:(part + 1) * lanes]
    spread(n_col, own.shape[0] // 2, own, out, send_sems, recv_sems, own_sem)


def second_gather(n_col, own, out, send_sems, recv_sems, own_sem):
    spread(n_col, TILE // 2 + 16, own, out, send_sems, recv_sems, own_sem)


def total_kernel(n_col, blocks, sums, total, land, send_sems, recv_sems):
    me = lax.axis_index("row") * n_col + lax.axis_index("col")

    def peer(offset):
        other = lax.rem(me + offset, blocks)
        return (other // n_col, lax.rem(other, n_col))

    barrier = pltpu.get_barrier_semaphore()

    def hello(offset, carry):
        pl.semaphore_signal(barrier, inc=1, device_id=peer(offset), device_id_type=MESH)
        return carry

    lax.fori_loop(1, blocks, hello, 0)
    pl.semaphore_wait(barrier, blocks - 1)

    def copy(offset):
        return pltpu.make_async_remote_copy(
            src_ref=sums,
            dst_ref=land.at[offset],
            send_sem=send_sems.at[offset],
            recv_sem=recv_sems.at[offset],
            device_id=peer(offset),
            device_id_type=MESH,
        )

    def begin(offset, carry):
        copy(offset).start()
        return carry

    lax.fori_loop(1, blocks, begin, 0)
    land[0] = sums[...]

    def finish(offset, carry):
        copy(offset).wait()
        return carry

    lax.fori_loop(1, blocks, finish, 0)
    total[...] = jnp.sum(land[...], axis=0)


def find_tiles(blocks, groups, order):
    me = lax.axis_index("row") * lax.axis_size("col") + lax.axis_index("col")
    mine = groups[me]

    def look(block, count):
        order[count] = block
        return count + (groups[block] == mine).astype(jnp.int32)

    return lax.fori_loop(0, blocks, look, 0)


def first_kernel(blocks, groups, points, scale, field, source, tiles, image, narrow,
                 order, left, right, built, vectors, vec_sems, tile_sems):
    total = find_tiles(blocks, groups, order)
    dims, lanes = points.shape[0], field.shape[1]

    def vector_copy(slot):
        return pltpu.make_async_copy(
            source.at[order[slot]], vectors.at[slot], vec_sems.at[slot]
        )

    def tile_copy(slot):
        return pltpu.make_async_copy(built.at[slot], tiles.at[slot], tile_sems.at[slot])

    def begin(slot, carry):
        vector_copy(slot).start()
        return carry

    lax.fori_loop(0, total, begin, 0)
    left[...] = lifted((points[...] / scale[...]).astype(jnp.bfloat16), 1.0, 0, 3).T
    image[...] = jnp.zeros_like(image)

    def one_tile(slot, carry):
        vector_copy(slot).wait()
        coords = jnp.concatenate(
            [vectors[slot, pl.ds(TILE + part * dims, dims), :] for part in range(TILE // lanes)], axis=1
        )
        right[...] = lifted(coords, -2.0, 3, 0)
        for start in range(0, TILE, CHUNK):
            rows = pl.ds(start, CHUNK)
            squared = jnp.dot(left[rows, :], right[...], preferred_element_type=jnp.float32)
            values = wendland(squared)
            built[slot, rows, :] = values
            image[rows, :] += jnp.dot(
                values, vectors[slot, pl.ds(0, TILE), :], preferred_element_type=jnp.float32
            )
        tile_copy(slot).start()
        return carry

    lax.fori_loop(0, total, one_tile, 0)
    narrow[0:TILE, :] = image[...].astype(jnp.bfloat16)
    sums = split3(jnp.sum(field[...] * field[...], axis=0, keepdims=True)) + split3(
        jnp.sum(field[...] * image[...], axis=0, keepdims=True)
    )
    zeros = jnp.zeros((16 - len(sums), lanes), jnp.float32)
    narrow[TILE:TILE + 16, :] = jnp.concatenate(list(sums) + [zeros], axis=0).astype(jnp.bfloat16)

    def finish(slot, carry):
        tile_copy(slot).wait()
        return carry

    lax.fori_loop(0, total, finish, 0)


def second_kernel(blocks, groups, tiles, source, image, field, noise, norms, sums, after, curved,
                  order, built, vectors, twice, tails, vec_sems, tile_sems, tail_sem):
    total = find_tiles(blocks, groups, order)

    def vector_copy(slot):
        return pltpu.make_async_copy(
            source.at[order[slot], pl.ds(0, TILE), :], vectors.at[slot], vec_sems.at[slot]
        )

    def tile_copy(slot):
        return pltpu.make_async_copy(tiles.at[slot], built.at[slot], tile_sems.at[slot])

    tail_copy = pltpu.make_async_copy(source.at[:, pl.ds(TILE, 16), :], tails, tail_sem)
    tail_copy.start()

    def begin(slot, carry):
        vector_copy(slot).start()
        tile_copy(slot).start()
        return carry

    lax.fori_loop(0, total, begin, 0)
    twice[...] = jnp.zeros_like(twice)

    def one_tile(slot, carry):
        vector_copy(slot).wait()
        tile_copy(slot).wait()
        twice[...] += jnp.dot(built[slot], vectors[slot], preferred_element_type=jnp.float32)
        return carry

    tail_copy.wait()
    lax.fori_loop(0, total, one_tile, 0)
    parts = jnp.sum(tails[...].astype(jnp.float32), axis=0)
    variance = noise[...]
    squares = parts[0:1, :] + parts[1:2, :] + parts[2:3, :]
    curve = variance * squares + (parts[3:4, :] + parts[4:5, :] + parts[5:6, :])
    norms[0:1, :] = squares
    norms[1:2, :] = curve
    step = squares / curve
    target = field[...]
    product = image[...]
    applied = variance * target + product
    residual = target - step * applied
    again = variance * residual + product - step * (variance * product + twice[...])
    after[...] = residual
    curved[...] = again
    sums[0:1, :] = jnp.sum(residual * residual, axis=0, keepdims=True)
    sums[1:2, :] = jnp.sum(residual * again, axis=0, keepdims=True)
    sums[2:3, :] = jnp.sum(residual * applied + target * again, axis=0, keepdims=True)
    sums[3:8, :] = jnp.zeros((5, sums.shape[1]), jnp.float32)


def gathered_plan(points, lengthscale, noise_var, groups, targets):
    n_col = lax.axis_size("col")
    blocks = groups.shape[0]
    dims = points.shape[0]
    rhs = targets.shape[1]
    scale = lengthscale[:, None]
    variance = noise_var[None, :]
    first_height = TILE + dims * TILE // rhs
    second_height = TILE + 16
    sends = 6 * (n_col // 2 - 1) * 2 + 6 + n_col // 2 * 8 - (n_col // 2 - 1) * 4

    vmem = pl.BlockSpec(memory_space=pltpu.VMEM)
    smem = pl.BlockSpec(memory_space=pltpu.SMEM)
    anywhere = pl.BlockSpec(memory_space=pl.ANY)
    whole = jax.ShapeDtypeStruct((TILE, rhs), jnp.float32)
    few = jax.ShapeDtypeStruct((8, rhs), jnp.float32)
    gather_sems = [
        pltpu.SemaphoreType.DMA((sends,)),
        pltpu.SemaphoreType.DMA((blocks, 2)),
        pltpu.SemaphoreType.DMA,
    ]

    def remote(number):
        return pltpu.CompilerParams(
            collective_id=number, has_side_effects=True, vmem_limit_bytes=VMEM_LIMIT
        )

    source = pl.pallas_call(
        functools.partial(first_gather, n_col),
        out_shape=jax.ShapeDtypeStruct((blocks, first_height, rhs), jnp.bfloat16),
        in_specs=[vmem, vmem, vmem],
        out_specs=anywhere,
        scratch_shapes=[pltpu.VMEM((first_height, rhs), jnp.bfloat16)] + gather_sems,
        compiler_params=remote(0),
        name="first_gather",
    )(points, scale, targets)

    tiles, image, narrow = pl.pallas_call(
        functools.partial(first_kernel, blocks),
        out_shape=[
            jax.ShapeDtypeStruct((blocks, TILE, TILE), jnp.bfloat16),
            whole,
            jax.ShapeDtypeStruct((second_height, rhs), jnp.bfloat16),
        ],
        in_specs=[smem, vmem, vmem, vmem, anywhere],
        out_specs=[anywhere, vmem, vmem],
        scratch_shapes=[
            pltpu.SMEM((blocks,), jnp.int32),
            pltpu.VMEM((TILE, 2 * dims), jnp.bfloat16),
            pltpu.VMEM((2 * dims, TILE), jnp.bfloat16),
            pltpu.VMEM((blocks, TILE, TILE), jnp.bfloat16),
            pltpu.VMEM((blocks, first_height, rhs), jnp.bfloat16),
            pltpu.SemaphoreType.DMA((blocks,)),
            pltpu.SemaphoreType.DMA((blocks,)),
        ],
        compiler_params=pltpu.CompilerParams(vmem_limit_bytes=VMEM_LIMIT),
        name="first_product",
    )(groups, points, scale, targets, source)

    source = pl.pallas_call(
        functools.partial(second_gather, n_col),
        out_shape=jax.ShapeDtypeStruct((blocks, second_height, rhs), jnp.bfloat16),
        in_specs=[vmem],
        out_specs=anywhere,
        scratch_shapes=gather_sems,
        compiler_params=remote(1),
        name="second_gather",
    )(narrow)

    norms, sums, residual, again = pl.pallas_call(
        functools.partial(second_kernel, blocks),
        out_shape=[few, few, whole, whole],
        in_specs=[smem, anywhere, anywhere, vmem, vmem, vmem],
        out_specs=[vmem, vmem, vmem, vmem],
        scratch_shapes=[
            pltpu.SMEM((blocks,), jnp.int32),
            pltpu.VMEM((blocks, TILE, TILE), jnp.bfloat16),
            pltpu.VMEM((blocks, TILE, rhs), jnp.bfloat16),
            pltpu.VMEM((TILE, rhs), jnp.float32),
            pltpu.VMEM((blocks, 16, rhs), jnp.bfloat16),
            pltpu.SemaphoreType.DMA((blocks,)),
            pltpu.SemaphoreType.DMA((blocks,)),
            pltpu.SemaphoreType.DMA,
        ],
        compiler_params=pltpu.CompilerParams(vmem_limit_bytes=VMEM_LIMIT),
        name="second_product",
    )(groups, tiles, source, image, targets, variance)

    last = pl.pallas_call(
        functools.partial(total_kernel, n_col, blocks),
        out_shape=few,
        in_specs=[vmem],
        out_specs=vmem,
        scratch_shapes=[
            pltpu.VMEM((blocks, 8, rhs), jnp.float32),
            pltpu.SemaphoreType.DMA((blocks,)),
            pltpu.SemaphoreType.DMA((blocks,)),
        ],
        compiler_params=remote(2),
        name="total",
    )(sums)
    squares = norms[0:1]
    curve = norms[1:2]
    step = squares / curve
    ratio = last[0:1] / squares
    second_curve = last[1:2] + ratio * (last[2:3] + ratio * curve)
    second_step = last[0:1] / second_curve
    direction = residual + ratio * targets
    applied = variance * targets + image
    solution_field = step * targets + second_step * direction
    residual = residual - second_step * (again + ratio * applied)
    return (solution_field, residual)


def kernel_tile(row_coords, col_coords):
    row_norms = jnp.sum(row_coords * row_coords, axis=0)
    col_norms = jnp.sum(col_coords * col_coords, axis=0)
    crossed = lax.dot_general(
        row_coords,
        col_coords,
        (((0,), (0,)), ((), ())),
        precision=lax.Precision.HIGHEST,
        preferred_element_type=jnp.float32,
    )
    squared = jnp.maximum(row_norms[:, None] + col_norms[None, :] - 2.0 * crossed, 0.0)
    radius = jnp.sqrt(squared)
    support = jnp.maximum(1.0 - radius, 0.0)
    return (support**11 * (11.0 * radius + 1.0)).astype(jnp.bfloat16)


def per_device(points, lengthscale, noise_var, groups, targets):
    n_row = lax.axis_size("row")
    n_col = lax.axis_size("col")
    own_blocks = targets.shape[0] // TILE
    row_blocks = own_blocks * n_col
    col_blocks = own_blocks * n_row
    scaled = points / lengthscale[:, None]
    row_coords = lax.all_gather(scaled.astype(jnp.bfloat16), "col", axis=1, tiled=True).astype(
        scaled.dtype
    )
    col_coords = lax.all_gather(scaled.astype(jnp.bfloat16), "row", axis=1, tiled=True).astype(
        scaled.dtype
    )
    row_place = lax.axis_index("row")
    col_place = lax.axis_index("col")
    row_groups = lax.dynamic_slice_in_dim(groups, row_place * row_blocks, row_blocks, 0)
    col_groups = lax.dynamic_index_in_dim(
        groups.reshape(n_row, n_col, own_blocks), col_place, 1, keepdims=False
    ).reshape(col_blocks)
    flat_mask = (row_groups[:, None] == col_groups[None, :]).reshape(row_blocks * col_blocks)
    tile_count = jnp.sum(flat_mask.astype(jnp.int32))
    tile_order = jnp.nonzero(flat_mask, size=row_blocks * col_blocks, fill_value=0)[0].astype(
        jnp.int32
    )

    def square_sums(vector):
        return lax.psum(jnp.sum(vector * vector, axis=0), ("row", "col"))

    solution_field = jnp.zeros_like(targets)
    residual = targets
    direction = targets
    norm_now = square_sums(residual)
    for iteration in range(ITERS):
        narrow = direction.astype(jnp.bfloat16)
        operator_source = lax.all_gather(narrow, "row", axis=0, tiled=True)
        source = operator_source
        initial = jnp.zeros((row_blocks * TILE, RHS), jnp.float32)

        def one_tile(position, summed):
            flat_index = tile_order[position]
            row_slot = flat_index // col_blocks
            col_slot = flat_index % col_blocks
            left = lax.dynamic_slice_in_dim(row_coords, row_slot * TILE, TILE, 1)
            right = lax.dynamic_slice_in_dim(col_coords, col_slot * TILE, TILE, 1)
            values = kernel_tile(left, right)
            block_vec = lax.dynamic_slice_in_dim(source, col_slot * TILE, TILE, 0)
            product = jnp.dot(values, block_vec, preferred_element_type=jnp.float32)
            current = lax.dynamic_slice_in_dim(summed, row_slot * TILE, TILE, 0)
            return lax.dynamic_update_slice_in_dim(summed, current + product, row_slot * TILE, 0)

        partial_value = lax.fori_loop(0, tile_count, one_tile, initial)
        outgoing = partial_value.astype(jnp.bfloat16).reshape(n_col, own_blocks * TILE, RHS)
        incoming = lax.all_to_all(outgoing, "col", split_axis=0, concat_axis=0, tiled=True)
        operator_product = jnp.sum(incoming, axis=0, dtype=jnp.float32)
        image = noise_var[None, :] * direction + operator_product
        curve = lax.psum(jnp.sum(direction * image, axis=0), ("row", "col"))
        step_size = norm_now / curve
        solution_field = solution_field + step_size[None, :] * direction
        residual = residual - step_size[None, :] * image
        if iteration + 1 < ITERS:
            norm_next = square_sums(residual)
            direction = residual + (norm_next / norm_now)[None, :] * direction
            norm_now = norm_next
    return (solution_field, residual)


def solution(mesh):
    placed = (P(None, ("row", "col")), P(), P(), P(), P(("row", "col"), None))

    def plan(points, lengthscale, noise_var, groups, targets):
        blocks = groups.shape[0]
        square = mesh.shape["row"] == 4 and mesh.shape["col"] % 2 == 0
        whole_field = blocks <= GATHER_LIMIT and blocks == mesh.size and square
        run = gathered_plan if whole_field else per_device
        return run(points, lengthscale, noise_var, groups, targets)

    return jax.shard_map(
        plan,
        mesh=mesh,
        in_specs=placed,
        out_specs=(P(("row", "col"), None), P(("row", "col"), None)),
        check_vma=False,
    )
```

```python
import functools

import functools

import jax
import jax.numpy as jnp
from jax import lax
from jax.experimental import pallas as pl
from jax.experimental.pallas import tpu as pltpu
from jax.sharding import PartitionSpec as P

TILE = 512
ITERS = 2
RHS = 128
CHUNK = 128
GATHER_LIMIT = 64
KEPT = 32
VMEM_LIMIT = 48 * 1024 * 1024
MESH = pl.DeviceIdType.MESH


def split3(value):
    first = value.astype(jnp.bfloat16).astype(jnp.float32)
    rest = value - first
    second = rest.astype(jnp.bfloat16).astype(jnp.float32)
    return first, second, rest - second


def lifted(coords, factor, norm_at, one_at):
    wide = coords.astype(jnp.float32)
    parts = split3(jnp.sum(wide * wide, axis=0, keepdims=True))
    row = lax.broadcasted_iota(jnp.int32, wide.shape, 0)
    tail = jnp.where((row >= one_at) & (row < one_at + 3), 1.0, 0.0)
    for place, part in enumerate(parts):
        tail = jnp.where(row == norm_at + place, part, tail)
    return jnp.concatenate([wide * factor, tail], axis=0).astype(jnp.bfloat16)


def wendland(squared):
    safe = jnp.maximum(squared, 1e-30)
    radius = safe * lax.rsqrt(safe)
    support = jnp.maximum(1.0 - radius, 0.0)
    second = support * support
    third = second * support
    fourth = second * second
    eighth = fourth * fourth
    return ((eighth * third) * (12.0 - 11.0 * support)).astype(jnp.bfloat16)


def place():
    row, col = lax.axis_index("row"), lax.axis_index("col")
    return row // 2, lax.rem(row, 2), col // 2, lax.rem(col, 2)


def greet(targets):
    barrier = pltpu.get_barrier_semaphore()
    for target in targets:
        pl.semaphore_signal(barrier, inc=1, device_id=target, device_id_type=MESH)
    pl.semaphore_wait(barrier, len(targets))


def device(y, core, z, x):
    return (2 * y + core, 2 * z + x)


class Plane:
    def __init__(self, n_col, out, send_sems, recv_sems):
        self.n_col, self.out, self.send_sems, self.recv_sems = n_col, out, send_sems, recv_sems
        self.y, self.core, self.z, self.x = place()
        self.depth = n_col // 2
        self.started = []
        y, core, z, x = self.y, self.core, self.z, self.x
        self.over_x, self.over_y = device(y, core, z, 1 - x), device(1 - y, core, z, x)
        self.over_core = device(y, 1 - core, z, x)

    def level(self, step):
        return lax.rem(self.z + step, self.depth)

    def over_z(self, step):
        return device(self.y, self.core, self.level(self.depth - step), self.x)

    def number(self, y, core, z, x):
        return (2 * y + core) * self.n_col + 2 * z + x

    def half(self, ref, part):
        lanes = TILE // 2
        return ref.at[:, pl.ds(part * lanes, lanes)]

    def launch(self, source, spot, recv_sem, target):
        copy = pltpu.make_async_remote_copy(
            src_ref=source,
            dst_ref=spot,
            send_sem=self.send_sems.at[len(self.started)],
            recv_sem=recv_sem,
            device_id=target,
            device_id_type=MESH,
        )
        copy.start()
        self.started.append(copy)

    def send(self, block, part, target, own=None):
        spot = self.half(self.out.at[block], part)
        source = spot if own is None else self.half(own, part)
        self.launch(source, spot, self.recv_sems.at[block, part], target)

    def arrived(self, block, part):
        spot = self.half(self.out.at[block], part)
        pltpu.make_async_copy(spot, spot, self.recv_sems.at[block, part]).wait()

    def pass_on(self, block, own=None):
        self.send(block, 0, self.over_x, own)
        self.send(block, 1, self.over_y, own)
        self.send(block, 0, self.over_y, own)
        self.send(block, 1, self.over_x, own)
        self.send(block, 0, self.over_core, own)
        self.send(block, 1, self.over_core, own)

    def second_hop(self, here):
        y, core, x = self.y, self.core, self.x
        block = self.number(y, core, here, 1 - x)
        self.arrived(block, 0)
        self.send(block, 0, self.over_y)
        self.send(block, 0, self.over_core)
        block = self.number(1 - y, core, here, x)
        self.arrived(block, 1)
        self.send(block, 1, self.over_x)
        self.send(block, 1, self.over_core)

    def last_hop(self, here):
        y, core, x = self.y, self.core, self.x
        for block, part in (
            (self.number(1 - y, core, here, x), 0),
            (self.number(y, core, here, 1 - x), 1),
            (self.number(1 - y, core, here, 1 - x), 0),
            (self.number(1 - y, core, here, 1 - x), 1),
        ):
            self.arrived(block, part)
            self.send(block, part, self.over_core)

    def finish(self):
        for step in range(self.depth):
            for other_y in (self.y, 1 - self.y):
                for other_x in (self.x, 1 - self.x):
                    block = self.number(other_y, 1 - self.core, self.level(step), other_x)
                    self.arrived(block, 0)
                    self.arrived(block, 1)
        for copy in self.started:
            copy.wait_send()


def first_gather(n_col, points, scale, targets, out, own, send_sems, recv_sems, own_sem):
    plane = Plane(n_col, out, send_sems, recv_sems)
    depth, dims = plane.depth, points.shape[0]
    width = targets.shape[1] // depth
    greet([plane.over_x, plane.over_y, plane.over_core] + [plane.over_z(step) for step in range(1, depth)])
    scaled = (points[...] / scale[...]).astype(jnp.bfloat16)
    turned = targets[...].T.astype(jnp.bfloat16)
    for part in range(depth):
        own[part, 0:width, :] = turned[part * width:(part + 1) * width, :]
        own[part, width:width + dims, :] = scaled
    me = plane.number(plane.y, plane.core, plane.z, plane.x)
    for step in range(1, depth):
        for part in range(2):
            plane.send(me, part, plane.over_z(step), own.at[plane.level(depth - step)])
    mine = own.at[plane.z]
    plane.pass_on(me, mine)
    keep = pltpu.make_async_copy(mine, out.at[me], own_sem)
    keep.start()
    for step in range(depth + 2):
        if 0 < step < depth:
            block = plane.number(plane.y, plane.core, plane.level(step), plane.x)
            plane.arrived(block, 0)
            plane.arrived(block, 1)
            plane.pass_on(block)
        if 0 < step <= depth:
            plane.second_hop(plane.level(step - 1))
        if step >= 2:
            plane.last_hop(plane.level(step - 2))
    keep.wait()
    plane.finish()


def second_gather(n_col, own, out, back, send_sems, recv_sems, back_sems, own_sems):
    plane = Plane(n_col, out, send_sems, recv_sems)
    depth = plane.depth
    greet([plane.over_x, plane.over_y, plane.over_core] + [plane.over_z(step) for step in range(1, depth)])
    keeps = []
    for step in range(depth):
        here = plane.level(step)
        block = plane.number(plane.y, plane.core, here, plane.x)
        plane.pass_on(block, own.at[here])
        if step > 0:
            there = plane.level(depth - step)
            plane.launch(own.at[there], back.at[plane.z], back_sems.at[step], plane.over_z(step))
        keep = pltpu.make_async_copy(own.at[here], out.at[block], own_sems.at[step])
        keep.start()
        keeps.append(keep)
    keep = pltpu.make_async_copy(own.at[plane.z], back.at[plane.z], own_sems.at[depth])
    keep.start()
    keeps.append(keep)
    for step in range(depth):
        plane.second_hop(plane.level(step))
    for step in range(depth):
        plane.last_hop(plane.level(step))
    for step in range(1, depth):
        spot = back.at[plane.level(step)]
        pltpu.make_async_copy(spot, spot, back_sems.at[step]).wait()
    for keep in keeps:
        keep.wait()
    plane.finish()


def finish_kernel(n_col, own, back, targets, total, once, twice,
                  land, line, wide, send_sems, recv_sems, line_sends, line_recvs, wide_sends, wide_recvs):
    y, core, z, x = place()
    depth = n_col // 2

    def level(step):
        return lax.rem(z + step, depth)

    column = [device(y, core, level(depth - step), x) for step in range(1, depth)]
    flips = [(a, b, c) for a in range(2) for b in range(2) for c in range(2)][1:]
    plane = [
        device(1 - y if a else y, 1 - core if b else core, z, 1 - x if c else x) for a, b, c in flips
    ]
    greet(column + plane)

    def remote(source, spot, send_sem, recv_sem, target):
        copy = pltpu.make_async_remote_copy(
            src_ref=source, dst_ref=spot, send_sem=send_sem, recv_sem=recv_sem,
            device_id=target, device_id_type=MESH,
        )
        copy.start()
        return copy

    copies = [
        remote(own.at[level(depth - step)], land.at[z], send_sems.at[step], recv_sems.at[step], column[step - 1])
        for step in range(1, depth)
    ]
    land[z] = own[z]
    rhs = targets.shape[1]
    target = targets[...]
    image = back[...].reshape(rhs, TILE).astype(jnp.float32).T
    once[...] = image

    def column_sum(value):
        return jnp.sum(value, axis=0, keepdims=True)

    line[0, 0:1, :] = column_sum(target * target)
    line[0, 1:2, :] = column_sum(target * image)
    line[0, 2:3, :] = column_sum(image * image)
    for copy in copies:
        copy.wait()
    again = land[...].reshape(rhs, TILE).astype(jnp.float32).T
    twice[...] = again
    line[0, 3:4, :] = column_sum(target * again)
    line[0, 4:5, :] = column_sum(image * again)
    line[0, 5:8, :] = jnp.zeros((3, rhs), jnp.float32)
    copies = [
        remote(line.at[0], line.at[step], line_sends.at[step], line_recvs.at[step], column[step - 1])
        for step in range(1, depth)
    ]
    for copy in copies:
        copy.wait()
    wide[0] = jnp.sum(line[...], axis=0)
    copies = [
        remote(wide.at[0], wide.at[step + 1], wide_sends.at[step], wide_recvs.at[step], peer)
        for step, peer in enumerate(plane)
    ]
    for copy in copies:
        copy.wait()
    total[...] = jnp.sum(wide[...], axis=0)


def find_tiles(n_col, blocks, groups, order, slices):
    y, core, _, x = place()

    def one_row(level, count):
        mine = groups[(2 * y + core) * n_col + 2 * level + x]

        def look(block, count):
            order[count] = block
            slices[count] = level
            return count + (groups[block] == mine).astype(jnp.int32)

        return lax.fori_loop(0, blocks, look, count)

    return lax.fori_loop(0, n_col // 2, one_row, 0)


def lift_rows(n_col, width, gathered, right):
    y, core, _, x = place()
    dims = gathered.shape[1] - width
    for level in range(n_col // 2):
        block = (2 * y + core) * n_col + 2 * level + x
        right[level] = lifted(gathered[block, pl.ds(width, dims), :], 1.0, 0, 3)


def build(width, gathered, block, level, left, right, spot):
    dims = gathered.shape[1] - width
    left[...] = lifted(gathered[block, pl.ds(width, dims), :], -2.0, 3, 0).T
    for start in range(0, TILE, CHUNK):
        rows = pl.ds(start, CHUNK)
        squared = jnp.dot(left[rows, :], right[level], preferred_element_type=jnp.float32)
        spot[rows, :] = wendland(squared)


def first_kernel(n_col, groups, gathered, tiles, narrow,
                 order, slices, left, right, built, image, tile_sems):
    width = narrow.shape[1]
    kept = tiles.shape[0]
    total = find_tiles(n_col, gathered.shape[0], groups, order, slices)
    lift_rows(n_col, width, gathered, right)
    image[...] = jnp.zeros_like(image)

    def tile_copy(slot):
        return pltpu.make_async_copy(built.at[slot], tiles.at[slot], tile_sems.at[slot])

    def one_tile(slot, carry):
        block, level = order[slot], slices[slot]
        spot = built.at[jnp.minimum(slot, kept)]
        build(width, gathered, block, level, left, right, spot)

        @pl.when(slot < kept)
        def _():
            tile_copy(slot).start()

        image[level] += jnp.dot(
            gathered[block, pl.ds(0, width), :], spot[...], preferred_element_type=jnp.float32
        )
        return carry

    lax.fori_loop(0, total, one_tile, 0)
    narrow[...] = image[...].astype(jnp.bfloat16)

    def finish(slot, carry):
        tile_copy(slot).wait()
        return carry

    lax.fori_loop(0, jnp.minimum(total, kept), finish, 0)


def second_kernel(n_col, groups, gathered, source, tiles, narrow,
                  order, slices, left, right, built, image, tile_sems):
    width = narrow.shape[1]
    kept = tiles.shape[0]
    total = find_tiles(n_col, gathered.shape[0], groups, order, slices)
    stored = jnp.minimum(total, kept)

    def tile_copy(slot):
        return pltpu.make_async_copy(tiles.at[slot], built.at[slot], tile_sems.at[slot])

    def begin(slot, carry):
        tile_copy(slot).start()
        return carry

    lax.fori_loop(0, stored, begin, 0)
    image[...] = jnp.zeros_like(image)

    def multiply(slot, spot):
        image[slices[slot]] += jnp.dot(source[order[slot]], spot[...], preferred_element_type=jnp.float32)

    def one_stored(slot, carry):
        tile_copy(slot).wait()
        multiply(slot, built.at[slot])
        return carry

    lax.fori_loop(0, stored, one_stored, 0)

    @pl.when(total > kept)
    def _():
        lift_rows(n_col, width, gathered, right)

    def one_more(slot, carry):
        build(width, gathered, order[slot], slices[slot], left, right, built.at[kept])
        multiply(slot, built.at[kept])
        return carry

    lax.fori_loop(stored, total, one_more, 0)
    narrow[...] = image[...].astype(jnp.bfloat16)


def gathered_plan(points, lengthscale, noise_var, groups, targets):
    n_col = lax.axis_size("col")
    depth = n_col // 2
    blocks = groups.shape[0]
    dims = points.shape[0]
    rhs = targets.shape[1]
    width = rhs // depth
    scale = lengthscale[:, None]
    variance = noise_var[None, :]
    first_sends = 2 * (depth - 1) + 14 * depth
    second_sends = depth - 1 + 14 * depth

    vmem = pl.BlockSpec(memory_space=pltpu.VMEM)
    smem = pl.BlockSpec(memory_space=pltpu.SMEM)
    anywhere = pl.BlockSpec(memory_space=pl.ANY)
    slices = jax.ShapeDtypeStruct((depth, width, TILE), jnp.bfloat16)
    whole = jax.ShapeDtypeStruct((TILE, rhs), jnp.float32)

    def remote(number):
        return pltpu.CompilerParams(
            collective_id=number, has_side_effects=True, vmem_limit_bytes=VMEM_LIMIT
        )

    gathered = pl.pallas_call(
        functools.partial(first_gather, n_col),
        out_shape=jax.ShapeDtypeStruct((blocks, width + dims, TILE), jnp.bfloat16),
        in_specs=[vmem, vmem, vmem],
        out_specs=vmem,
        scratch_shapes=[
            pltpu.VMEM((depth, width + dims, TILE), jnp.bfloat16),
            pltpu.SemaphoreType.DMA((first_sends,)),
            pltpu.SemaphoreType.DMA((blocks, 2)),
            pltpu.SemaphoreType.DMA,
        ],
        compiler_params=remote(0),
        name="first_gather",
    )(points, scale, targets)

    work = [
        pltpu.SMEM((depth * blocks,), jnp.int32),
        pltpu.SMEM((depth * blocks,), jnp.int32),
        pltpu.VMEM((TILE, 2 * dims), jnp.bfloat16),
        pltpu.VMEM((depth, 2 * dims, TILE), jnp.bfloat16),
        pltpu.VMEM((KEPT + 1, TILE, TILE), jnp.bfloat16),
        pltpu.VMEM((depth, width, TILE), jnp.float32),
        pltpu.SemaphoreType.DMA((KEPT,)),
    ]
    tiles, first = pl.pallas_call(
        functools.partial(first_kernel, n_col),
        out_shape=[jax.ShapeDtypeStruct((KEPT, TILE, TILE), jnp.bfloat16), slices],
        in_specs=[smem, vmem],
        out_specs=[anywhere, vmem],
        scratch_shapes=work,
        compiler_params=pltpu.CompilerParams(vmem_limit_bytes=VMEM_LIMIT),
        name="first_product",
    )(groups, gathered)

    source, back = pl.pallas_call(
        functools.partial(second_gather, n_col),
        out_shape=[jax.ShapeDtypeStruct((blocks, width, TILE), jnp.bfloat16), slices],
        in_specs=[vmem],
        out_specs=[vmem, vmem],
        scratch_shapes=[
            pltpu.SemaphoreType.DMA((second_sends,)),
            pltpu.SemaphoreType.DMA((blocks, 2)),
            pltpu.SemaphoreType.DMA((depth,)),
            pltpu.SemaphoreType.DMA((depth + 1,)),
        ],
        compiler_params=remote(1),
        name="second_gather",
    )(first)

    second = pl.pallas_call(
        functools.partial(second_kernel, n_col),
        out_shape=slices,
        in_specs=[smem, vmem, vmem, anywhere],
        out_specs=vmem,
        scratch_shapes=work,
        compiler_params=pltpu.CompilerParams(vmem_limit_bytes=VMEM_LIMIT),
        name="second_product",
    )(groups, gathered, source, tiles)

    total, image, again = pl.pallas_call(
        functools.partial(finish_kernel, n_col),
        out_shape=[jax.ShapeDtypeStruct((8, rhs), jnp.float32), whole, whole],
        in_specs=[vmem, vmem, vmem],
        out_specs=[vmem, vmem, vmem],
        scratch_shapes=[
            pltpu.VMEM((depth, width, TILE), jnp.bfloat16),
            pltpu.VMEM((depth, 8, rhs), jnp.float32),
            pltpu.VMEM((8, 8, rhs), jnp.float32),
        ]
        + [pltpu.SemaphoreType.DMA((depth,))] * 4
        + [pltpu.SemaphoreType.DMA((8,))] * 2,
        compiler_params=remote(2),
        name="finish",
    )(second, back, targets)

    tt, ty, yy, tz, yz = (total[place:place + 1] for place in range(5))
    step = tt / (variance * tt + ty)
    keep = 1.0 - step * variance
    after = keep * keep * tt - 2.0 * keep * step * ty + step * step * yy
    along = keep + after / tt
    squares = along * along * tt - 2.0 * along * step * ty + step * step * yy
    product = along * along * ty - along * step * (tz + yy) + step * step * yz
    second_step = after / (variance * squares + product)
    direction = along * targets - step * image
    applied = variance * direction + along * image - step * again
    solution_field = step * targets + second_step * direction
    residual = keep * targets - step * image - second_step * applied
    return (solution_field, residual)


def kernel_tile(row_coords, col_coords):
    row_norms = jnp.sum(row_coords * row_coords, axis=0)
    col_norms = jnp.sum(col_coords * col_coords, axis=0)
    crossed = lax.dot_general(
        row_coords,
        col_coords,
        (((0,), (0,)), ((), ())),
        precision=lax.Precision.HIGHEST,
        preferred_element_type=jnp.float32,
    )
    squared = jnp.maximum(row_norms[:, None] + col_norms[None, :] - 2.0 * crossed, 0.0)
    radius = jnp.sqrt(squared)
    support = jnp.maximum(1.0 - radius, 0.0)
    return (support**11 * (11.0 * radius + 1.0)).astype(jnp.bfloat16)


def per_device(points, lengthscale, noise_var, groups, targets):
    n_row = lax.axis_size("row")
    n_col = lax.axis_size("col")
    own_blocks = targets.shape[0] // TILE
    row_blocks = own_blocks * n_col
    col_blocks = own_blocks * n_row
    scaled = points / lengthscale[:, None]
    row_coords = lax.all_gather(scaled.astype(jnp.bfloat16), "col", axis=1, tiled=True).astype(
        scaled.dtype
    )
    col_coords = lax.all_gather(scaled.astype(jnp.bfloat16), "row", axis=1, tiled=True).astype(
        scaled.dtype
    )
    row_place = lax.axis_index("row")
    col_place = lax.axis_index("col")
    row_groups = lax.dynamic_slice_in_dim(groups, row_place * row_blocks, row_blocks, 0)
    col_groups = lax.dynamic_index_in_dim(
        groups.reshape(n_row, n_col, own_blocks), col_place, 1, keepdims=False
    ).reshape(col_blocks)
    flat_mask = (row_groups[:, None] == col_groups[None, :]).reshape(row_blocks * col_blocks)
    tile_count = jnp.sum(flat_mask.astype(jnp.int32))
    tile_order = jnp.nonzero(flat_mask, size=row_blocks * col_blocks, fill_value=0)[0].astype(
        jnp.int32
    )

    def square_sums(vector):
        return lax.psum(jnp.sum(vector * vector, axis=0), ("row", "col"))

    solution_field = jnp.zeros_like(targets)
    residual = targets
    direction = targets
    norm_now = square_sums(residual)
    for iteration in range(ITERS):
        narrow = direction.astype(jnp.bfloat16)
        operator_source = lax.all_gather(narrow, "row", axis=0, tiled=True)
        source = operator_source
        initial = jnp.zeros((row_blocks * TILE, RHS), jnp.float32)

        def one_tile(position, summed):
            flat_index = tile_order[position]
            row_slot = flat_index // col_blocks
            col_slot = flat_index % col_blocks
            left = lax.dynamic_slice_in_dim(row_coords, row_slot * TILE, TILE, 1)
            right = lax.dynamic_slice_in_dim(col_coords, col_slot * TILE, TILE, 1)
            values = kernel_tile(left, right)
            block_vec = lax.dynamic_slice_in_dim(source, col_slot * TILE, TILE, 0)
            product = jnp.dot(values, block_vec, preferred_element_type=jnp.float32)
            current = lax.dynamic_slice_in_dim(summed, row_slot * TILE, TILE, 0)
            return lax.dynamic_update_slice_in_dim(summed, current + product, row_slot * TILE, 0)

        partial_value = lax.fori_loop(0, tile_count, one_tile, initial)
        outgoing = partial_value.astype(jnp.bfloat16).reshape(n_col, own_blocks * TILE, RHS)
        incoming = lax.all_to_all(outgoing, "col", split_axis=0, concat_axis=0, tiled=True)
        operator_product = jnp.sum(incoming, axis=0, dtype=jnp.float32)
        image = noise_var[None, :] * direction + operator_product
        curve = lax.psum(jnp.sum(direction * image, axis=0), ("row", "col"))
        step_size = norm_now / curve
        solution_field = solution_field + step_size[None, :] * direction
        residual = residual - step_size[None, :] * image
        if iteration + 1 < ITERS:
            norm_next = square_sums(residual)
            direction = residual + (norm_next / norm_now)[None, :] * direction
            norm_now = norm_next
    return (solution_field, residual)


def solution(mesh):
    placed = (P(None, ("row", "col")), P(), P(), P(), P(("row", "col"), None))

    def plan(points, lengthscale, noise_var, groups, targets):
        blocks = groups.shape[0]
        square = mesh.shape["row"] == 4 and mesh.shape["col"] in (2, 4, 8, 16)
        whole_field = blocks <= GATHER_LIMIT and blocks == mesh.size and square
        run = gathered_plan if whole_field else per_device
        return run(points, lengthscale, noise_var, groups, targets)

    return jax.shard_map(
        plan,
        mesh=mesh,
        in_specs=placed,
        out_specs=(P(("row", "col"), None), P(("row", "col"), None)),
        check_vma=False,
    )
```

```python
import functools

import functools

import jax
import jax.numpy as jnp
from jax import lax
from jax.experimental import pallas as pl
from jax.experimental.pallas import tpu as pltpu
from jax.sharding import PartitionSpec as P

TILE = 512
ITERS = 2
RHS = 128
CHUNK = 128
GATHER_LIMIT = 64
KEPT = 32
VMEM_LIMIT = 48 * 1024 * 1024
MESH = pl.DeviceIdType.MESH


def split3(value):
    first = value.astype(jnp.bfloat16).astype(jnp.float32)
    rest = value - first
    second = rest.astype(jnp.bfloat16).astype(jnp.float32)
    return first, second, rest - second


def lifted(coords, factor, norm_at, one_at):
    wide = coords.astype(jnp.float32)
    parts = split3(jnp.sum(wide * wide, axis=0, keepdims=True))
    row = lax.broadcasted_iota(jnp.int32, wide.shape, 0)
    tail = jnp.where((row >= one_at) & (row < one_at + 3), 1.0, 0.0)
    for place, part in enumerate(parts):
        tail = jnp.where(row == norm_at + place, part, tail)
    return jnp.concatenate([wide * factor, tail], axis=0).astype(jnp.bfloat16)


def wendland(squared):
    safe = jnp.maximum(squared, 1e-30)
    radius = safe * lax.rsqrt(safe)
    support = jnp.maximum(1.0 - radius, 0.0)
    second = support * support
    third = second * support
    fourth = second * second
    eighth = fourth * fourth
    return ((eighth * third) * (12.0 - 11.0 * support)).astype(jnp.bfloat16)


def place():
    row, col = lax.axis_index("row"), lax.axis_index("col")
    return row // 2, lax.rem(row, 2), col // 2, lax.rem(col, 2)


def device(y, core, z, x):
    return (2 * y + core, 2 * z + x)


def greet(targets):
    barrier = pltpu.get_barrier_semaphore()
    for target in targets:
        pl.semaphore_signal(barrier, inc=1, device_id=target, device_id_type=MESH)


def greeted(targets):
    pl.semaphore_wait(pltpu.get_barrier_semaphore(), len(targets))


class Plane:
    def __init__(self, n_col, out, send_sems, recv_sems):
        self.out, self.send_sems, self.recv_sems = out, send_sems, recv_sems
        self.y, self.core, self.z, self.x = place()
        self.depth = n_col // 2
        self.started = []
        y, core, z, x = self.y, self.core, self.z, self.x
        self.over_x, self.over_y = device(y, core, z, 1 - x), device(1 - y, core, z, x)
        self.over_core = device(y, 1 - core, z, x)
        self.partners = [self.over_x, self.over_y, self.over_core]
        self.partners += [self.over_z(step) for step in range(1, self.depth)]

    def level(self, step):
        return lax.rem(self.z + step, self.depth)

    def over_z(self, step):
        return device(self.y, self.core, self.level(self.depth - step), self.x)

    def launch(self, source, spot, recv_sem, target):
        copy = pltpu.make_async_remote_copy(
            src_ref=source,
            dst_ref=spot,
            send_sem=self.send_sems.at[len(self.started)],
            recv_sem=recv_sem,
            device_id=target,
            device_id_type=MESH,
        )
        copy.start()
        self.started.append(copy)

    def half(self, ref, part):
        lanes = TILE // 2
        return ref.at[:, :, pl.ds(part * lanes, lanes)]

    def spot(self, peer, steps, part):
        return self.half(self.out.at[peer, pl.ds(steps[0], steps[1])], part)

    def send(self, group, steps, peer, part, target, flip, own=None):
        source = self.spot(peer, steps, part) if own is None else self.half(own, part)
        there = peer + flip
        self.launch(source, self.spot(there, steps, part), self.recv_sems.at[group, there, part], target)

    def arrived(self, group, steps, peer, part):
        spot = self.spot(peer, steps, part)
        pltpu.make_async_copy(spot, spot, self.recv_sems.at[group, peer, part]).wait()

    def first_hop(self, group, steps, own=None):
        self.send(group, steps, 0, 0, self.over_x, 1, own)
        self.send(group, steps, 0, 1, self.over_y, 4, own)
        self.send(group, steps, 0, 1, self.over_x, 1, own)
        self.send(group, steps, 0, 0, self.over_y, 4, own)
        self.send(group, steps, 0, 0, self.over_core, 2, own)
        self.send(group, steps, 0, 1, self.over_core, 2, own)

    def second_hop(self, group, steps):
        self.arrived(group, steps, 1, 0)
        self.send(group, steps, 1, 0, self.over_y, 4)
        self.arrived(group, steps, 4, 1)
        self.send(group, steps, 4, 1, self.over_x, 1)
        self.send(group, steps, 1, 0, self.over_core, 2)
        self.send(group, steps, 4, 1, self.over_core, 2)

    def last_hop(self, group, steps):
        for peer, part in ((1, 1), (4, 0), (5, 0), (5, 1)):
            self.arrived(group, steps, peer, part)
            self.send(group, steps, peer, part, self.over_core, 2)

    def finish(self, groups):
        for group, steps in enumerate(groups):
            for peer in (2, 3, 6, 7):
                self.arrived(group, steps, peer, 0)
                self.arrived(group, steps, peer, 1)
        for copy in self.started:
            copy.wait_send()


def first_gather(n_col, points_in, scale, targets_in, out, own, points, targets,
                 send_sems, recv_sems, z_sems, own_sems):
    plane = Plane(n_col, out, send_sems, recv_sems)
    depth, dims = plane.depth, points.shape[0]
    width = targets.shape[1] // depth
    fetches = [
        pltpu.make_async_copy(targets_in, targets, own_sems.at[0]),
        pltpu.make_async_copy(points_in, points, own_sems.at[1]),
    ]
    for fetch in fetches:
        fetch.start()
    greet(plane.partners)
    across = lax.broadcasted_iota(jnp.int32, (dims, dims), 1)
    down = lax.broadcasted_iota(jnp.int32, (dims, dims), 0)
    lengths = jnp.sum(jnp.where(across == down, scale[...], 0.0), axis=1, keepdims=True)
    for fetch in fetches:
        fetch.wait()
    scaled = (points[...] / lengths).astype(jnp.bfloat16)
    turned = targets[...].T.astype(jnp.bfloat16)
    for part in range(depth):
        own[part, 0:width, :] = turned[part * width:(part + 1) * width, :]
        own[part, width:width + dims, :] = scaled
    greeted(plane.partners)
    for step in range(1, depth):
        plane.launch(own.at[plane.level(depth - step)], out.at[0, step], z_sems.at[step], plane.over_z(step))
    groups = [(0, 1), (1, depth - 1)] if depth > 1 else [(0, 1)]
    mine = own.at[pl.ds(plane.z, 1)]
    plane.first_hop(0, groups[0], mine)
    keep = pltpu.make_async_copy(mine, out.at[0, pl.ds(0, 1)], own_sems.at[0])
    keep.start()
    plane.second_hop(0, groups[0])
    if depth > 1:
        for step in range(1, depth):
            spot = out.at[0, step]
            pltpu.make_async_copy(spot, spot, z_sems.at[step]).wait()
        plane.first_hop(1, groups[1])
    plane.last_hop(0, groups[0])
    if depth > 1:
        plane.second_hop(1, groups[1])
        plane.last_hop(1, groups[1])
    keep.wait()
    plane.finish(groups)


def second_gather(n_col, own, out, back, send_sems, recv_sems, back_sems, own_sems):
    plane = Plane(n_col, out, send_sems, recv_sems)
    depth = plane.depth
    greet(plane.partners)
    keeps = [
        pltpu.make_async_copy(own, out.at[0], own_sems.at[0]),
        pltpu.make_async_copy(own.at[0], back.at[plane.z], own_sems.at[1]),
    ]
    for keep in keeps:
        keep.start()
    greeted(plane.partners)
    steps = (0, depth)
    plane.first_hop(0, steps, own)
    for step in range(1, depth):
        plane.launch(own.at[depth - step], back.at[plane.z], back_sems.at[step], plane.over_z(step))
    plane.second_hop(0, steps)
    plane.last_hop(0, steps)
    for step in range(1, depth):
        spot = back.at[plane.level(step)]
        pltpu.make_async_copy(spot, spot, back_sems.at[step]).wait()
    for keep in keeps:
        keep.wait()
    plane.finish([steps])


def finish_kernel(n_col, own, back, targets, total, once, twice,
                  land, line, wide, send_sems, recv_sems, line_sends, line_recvs, wide_sends, wide_recvs):
    y, core, z, x = place()
    depth = n_col // 2

    def level(step):
        return lax.rem(z + step, depth)

    column = [device(y, core, level(depth - step), x) for step in range(1, depth)]
    flips = [(a, b, c) for a in range(2) for b in range(2) for c in range(2)][1:]
    plane = [
        device(1 - y if a else y, 1 - core if b else core, z, 1 - x if c else x) for a, b, c in flips
    ]
    greet(column + plane)
    rhs = targets.shape[1]
    target = targets[...]
    image = back[...].reshape(rhs, TILE).astype(jnp.float32).T
    once[...] = image

    def column_sum(value):
        return jnp.sum(value, axis=0, keepdims=True)

    line[0, 0:1, :] = column_sum(target * target)
    line[0, 1:2, :] = column_sum(target * image)
    line[0, 2:3, :] = column_sum(image * image)
    line[0, 5:8, :] = jnp.zeros((3, rhs), jnp.float32)
    greeted(column + plane)

    def remote(source, spot, send_sem, recv_sem, target):
        copy = pltpu.make_async_remote_copy(
            src_ref=source, dst_ref=spot, send_sem=send_sem, recv_sem=recv_sem,
            device_id=target, device_id_type=MESH,
        )
        copy.start()
        return copy

    copies = [
        remote(own.at[depth - step], land.at[z], send_sems.at[step], recv_sems.at[step], column[step - 1])
        for step in range(1, depth)
    ]
    land[z] = own[0]
    for copy in copies:
        copy.wait()
    again = land[...].reshape(rhs, TILE).astype(jnp.float32).T
    twice[...] = again
    line[0, 3:4, :] = column_sum(target * again)
    line[0, 4:5, :] = column_sum(image * again)
    copies = [
        remote(line.at[0], line.at[step], line_sends.at[step], line_recvs.at[step], column[step - 1])
        for step in range(1, depth)
    ]
    for copy in copies:
        copy.wait()
    wide[0] = jnp.sum(line[...], axis=0)
    copies = [
        remote(wide.at[0], wide.at[step + 1], wide_sends.at[step], wide_recvs.at[step], peer)
        for step, peer in enumerate(plane)
    ]
    for copy in copies:
        copy.wait()
    total[...] = jnp.sum(wide[...], axis=0)


def find_tiles(n_col, groups, order):
    y, core, z, x = place()
    depth = n_col // 2

    def label(peer, step):
        other_y = lax.rem(y + peer // 4, 2)
        other_core = lax.rem(core + peer // 2 % 2, 2)
        other_x = lax.rem(x + peer % 2, 2)
        return groups[(2 * other_y + other_core) * n_col + 2 * lax.rem(z + step, depth) + other_x]

    labels = [label(peer, step) for peer in range(8) for step in range(depth)]
    count = jnp.int32(0)
    for level in range(depth):
        for block, other in enumerate(labels):
            order[count] = block * depth + level
            count = count + (other == labels[level]).astype(jnp.int32)
    return count


def lift_rows(n_col, width, gathered, right):
    dims = gathered.shape[1] - width
    for level in range(n_col // 2):
        right[level] = lifted(gathered[level, pl.ds(width, dims), :], 1.0, 0, 3)


def build(width, gathered, block, level, left, right, spot):
    dims = gathered.shape[1] - width
    left[...] = lifted(gathered[block, pl.ds(width, dims), :], -2.0, 3, 0).T
    for start in range(0, TILE, CHUNK):
        rows = pl.ds(start, CHUNK)
        squared = jnp.dot(left[rows, :], right[level], preferred_element_type=jnp.float32)
        spot[rows, :] = wendland(squared)


def first_kernel(n_col, groups, gathered, tiles, narrow,
                 order, left, right, built, image, tile_sems):
    width = narrow.shape[1]
    depth, kept = n_col // 2, tiles.shape[0]
    total = find_tiles(n_col, groups, order)
    lift_rows(n_col, width, gathered, right)
    image[...] = jnp.zeros_like(image)

    def tile_copy(slot):
        return pltpu.make_async_copy(built.at[slot], tiles.at[slot], tile_sems.at[slot])

    def one_tile(slot, carry):
        block, level = order[slot] // depth, lax.rem(order[slot], depth)
        spot = built.at[jnp.minimum(slot, kept)]
        build(width, gathered, block, level, left, right, spot)

        @pl.when(slot < kept)
        def _():
            tile_copy(slot).start()

        image[level] += jnp.dot(
            gathered[block, pl.ds(0, width), :], spot[...], preferred_element_type=jnp.float32
        )
        return carry

    lax.fori_loop(0, total, one_tile, 0)
    narrow[...] = image[...].astype(jnp.bfloat16)

    def finish(slot, carry):
        tile_copy(slot).wait()
        return carry

    lax.fori_loop(0, jnp.minimum(total, kept), finish, 0)


def second_kernel(n_col, groups, gathered, source, tiles, narrow,
                  order, left, right, built, image, tile_sems):
    width = narrow.shape[1]
    depth, kept = n_col // 2, tiles.shape[0]
    total = find_tiles(n_col, groups, order)
    stored = jnp.minimum(total, kept)

    def tile_copy(slot):
        return pltpu.make_async_copy(tiles.at[slot], built.at[slot], tile_sems.at[slot])

    def begin(slot, carry):
        tile_copy(slot).start()
        return carry

    lax.fori_loop(0, stored, begin, 0)
    image[...] = jnp.zeros_like(image)

    def multiply(slot, spot):
        block, level = order[slot] // depth, lax.rem(order[slot], depth)
        image[level] += jnp.dot(source[block], spot[...], preferred_element_type=jnp.float32)

    def one_stored(slot, carry):
        tile_copy(slot).wait()
        multiply(slot, built.at[slot])
        return carry

    lax.fori_loop(0, stored, one_stored, 0)

    @pl.when(total > kept)
    def _():
        lift_rows(n_col, width, gathered, right)

    def one_more(slot, carry):
        block, level = order[slot] // depth, lax.rem(order[slot], depth)
        build(width, gathered, block, level, left, right, built.at[kept])
        multiply(slot, built.at[kept])
        return carry

    lax.fori_loop(stored, total, one_more, 0)
    narrow[...] = image[...].astype(jnp.bfloat16)


def gathered_plan(points, lengthscale, noise_var, groups, targets):
    n_col = lax.axis_size("col")
    depth = n_col // 2
    blocks = groups.shape[0]
    dims = points.shape[0]
    rhs = targets.shape[1]
    width = rhs // depth
    scale = lengthscale[None, :]
    variance = noise_var[None, :]
    parts = 2 if depth > 1 else 1

    vmem = pl.BlockSpec(memory_space=pltpu.VMEM)
    smem = pl.BlockSpec(memory_space=pltpu.SMEM)
    anywhere = pl.BlockSpec(memory_space=pl.ANY)
    slices = jax.ShapeDtypeStruct((depth, width, TILE), jnp.bfloat16)
    whole = jax.ShapeDtypeStruct((TILE, rhs), jnp.float32)

    def remote(number):
        return pltpu.CompilerParams(
            collective_id=number, has_side_effects=True, vmem_limit_bytes=VMEM_LIMIT
        )

    gathered = pl.pallas_call(
        functools.partial(first_gather, n_col),
        out_shape=jax.ShapeDtypeStruct((8, depth, width + dims, TILE), jnp.bfloat16),
        in_specs=[anywhere, vmem, anywhere],
        out_specs=vmem,
        scratch_shapes=[
            pltpu.VMEM((depth, width + dims, TILE), jnp.bfloat16),
            pltpu.VMEM((dims, TILE), jnp.float32),
            pltpu.VMEM((TILE, rhs), jnp.float32),
            pltpu.SemaphoreType.DMA((depth - 1 + 14 * parts,)),
            pltpu.SemaphoreType.DMA((parts, 8, 2)),
            pltpu.SemaphoreType.DMA((depth,)),
            pltpu.SemaphoreType.DMA((2,)),
        ],
        compiler_params=remote(0),
        name="first_gather",
    )(points, scale, targets).reshape(blocks, width + dims, TILE)

    work = [
        pltpu.SMEM((depth * blocks,), jnp.int32),
        pltpu.VMEM((TILE, 2 * dims), jnp.bfloat16),
        pltpu.VMEM((depth, 2 * dims, TILE), jnp.bfloat16),
        pltpu.VMEM((KEPT + 1, TILE, TILE), jnp.bfloat16),
        pltpu.VMEM((depth, width, TILE), jnp.float32),
        pltpu.SemaphoreType.DMA((KEPT,)),
    ]
    tiles, first = pl.pallas_call(
        functools.partial(first_kernel, n_col),
        out_shape=[jax.ShapeDtypeStruct((KEPT, TILE, TILE), jnp.bfloat16), slices],
        in_specs=[smem, vmem],
        out_specs=[anywhere, vmem],
        scratch_shapes=work,
        compiler_params=pltpu.CompilerParams(vmem_limit_bytes=VMEM_LIMIT),
        name="first_product",
    )(groups, gathered)

    source, back = pl.pallas_call(
        functools.partial(second_gather, n_col),
        out_shape=[jax.ShapeDtypeStruct((8, depth, width, TILE), jnp.bfloat16), slices],
        in_specs=[vmem],
        out_specs=[vmem, vmem],
        scratch_shapes=[
            pltpu.SemaphoreType.DMA((depth - 1 + 14,)),
            pltpu.SemaphoreType.DMA((1, 8, 2)),
            pltpu.SemaphoreType.DMA((depth,)),
            pltpu.SemaphoreType.DMA((2,)),
        ],
        compiler_params=remote(1),
        name="second_gather",
    )(first)

    second = pl.pallas_call(
        functools.partial(second_kernel, n_col),
        out_shape=slices,
        in_specs=[smem, vmem, vmem, anywhere],
        out_specs=vmem,
        scratch_shapes=work,
        compiler_params=pltpu.CompilerParams(vmem_limit_bytes=VMEM_LIMIT),
        name="second_product",
    )(groups, gathered, source.reshape(blocks, width, TILE), tiles)

    total, image, again = pl.pallas_call(
        functools.partial(finish_kernel, n_col),
        out_shape=[jax.ShapeDtypeStruct((8, rhs), jnp.float32), whole, whole],
        in_specs=[vmem, vmem, vmem],
        out_specs=[vmem, vmem, vmem],
        scratch_shapes=[
            pltpu.VMEM((depth, width, TILE), jnp.bfloat16),
            pltpu.VMEM((depth, 8, rhs), jnp.float32),
            pltpu.VMEM((8, 8, rhs), jnp.float32),
        ]
        + [pltpu.SemaphoreType.DMA((depth,))] * 4
        + [pltpu.SemaphoreType.DMA((8,))] * 2,
        compiler_params=remote(2),
        name="finish",
    )(second, back, targets)

    tt, ty, yy, tz, yz = (total[place:place + 1] for place in range(5))
    step = tt / (variance * tt + ty)
    keep = 1.0 - step * variance
    after = keep * keep * tt - 2.0 * keep * step * ty + step * step * yy
    along = keep + after / tt
    squares = along * along * tt - 2.0 * along * step * ty + step * step * yy
    product = along * along * ty - along * step * (tz + yy) + step * step * yz
    second_step = after / (variance * squares + product)
    direction = along * targets - step * image
    applied = variance * direction + along * image - step * again
    solution_field = step * targets + second_step * direction
    residual = keep * targets - step * image - second_step * applied
    return (solution_field, residual)


def kernel_tile(row_coords, col_coords):
    row_norms = jnp.sum(row_coords * row_coords, axis=0)
    col_norms = jnp.sum(col_coords * col_coords, axis=0)
    crossed = lax.dot_general(
        row_coords,
        col_coords,
        (((0,), (0,)), ((), ())),
        precision=lax.Precision.HIGHEST,
        preferred_element_type=jnp.float32,
    )
    squared = jnp.maximum(row_norms[:, None] + col_norms[None, :] - 2.0 * crossed, 0.0)
    radius = jnp.sqrt(squared)
    support = jnp.maximum(1.0 - radius, 0.0)
    return (support**11 * (11.0 * radius + 1.0)).astype(jnp.bfloat16)


def per_device(points, lengthscale, noise_var, groups, targets):
    n_row = lax.axis_size("row")
    n_col = lax.axis_size("col")
    own_blocks = targets.shape[0] // TILE
    row_blocks = own_blocks * n_col
    col_blocks = own_blocks * n_row
    scaled = points / lengthscale[:, None]
    row_coords = lax.all_gather(scaled.astype(jnp.bfloat16), "col", axis=1, tiled=True).astype(
        scaled.dtype
    )
    col_coords = lax.all_gather(scaled.astype(jnp.bfloat16), "row", axis=1, tiled=True).astype(
        scaled.dtype
    )
    row_place = lax.axis_index("row")
    col_place = lax.axis_index("col")
    row_groups = lax.dynamic_slice_in_dim(groups, row_place * row_blocks, row_blocks, 0)
    col_groups = lax.dynamic_index_in_dim(
        groups.reshape(n_row, n_col, own_blocks), col_place, 1, keepdims=False
    ).reshape(col_blocks)
    flat_mask = (row_groups[:, None] == col_groups[None, :]).reshape(row_blocks * col_blocks)
    tile_count = jnp.sum(flat_mask.astype(jnp.int32))
    tile_order = jnp.nonzero(flat_mask, size=row_blocks * col_blocks, fill_value=0)[0].astype(
        jnp.int32
    )

    def square_sums(vector):
        return lax.psum(jnp.sum(vector * vector, axis=0), ("row", "col"))

    solution_field = jnp.zeros_like(targets)
    residual = targets
    direction = targets
    norm_now = square_sums(residual)
    for iteration in range(ITERS):
        narrow = direction.astype(jnp.bfloat16)
        operator_source = lax.all_gather(narrow, "row", axis=0, tiled=True)
        source = operator_source
        initial = jnp.zeros((row_blocks * TILE, RHS), jnp.float32)

        def one_tile(position, summed):
            flat_index = tile_order[position]
            row_slot = flat_index // col_blocks
            col_slot = flat_index % col_blocks
            left = lax.dynamic_slice_in_dim(row_coords, row_slot * TILE, TILE, 1)
            right = lax.dynamic_slice_in_dim(col_coords, col_slot * TILE, TILE, 1)
            values = kernel_tile(left, right)
            block_vec = lax.dynamic_slice_in_dim(source, col_slot * TILE, TILE, 0)
            product = jnp.dot(values, block_vec, preferred_element_type=jnp.float32)
            current = lax.dynamic_slice_in_dim(summed, row_slot * TILE, TILE, 0)
            return lax.dynamic_update_slice_in_dim(summed, current + product, row_slot * TILE, 0)

        partial_value = lax.fori_loop(0, tile_count, one_tile, initial)
        outgoing = partial_value.astype(jnp.bfloat16).reshape(n_col, own_blocks * TILE, RHS)
        incoming = lax.all_to_all(outgoing, "col", split_axis=0, concat_axis=0, tiled=True)
        operator_product = jnp.sum(incoming, axis=0, dtype=jnp.float32)
        image = noise_var[None, :] * direction + operator_product
        curve = lax.psum(jnp.sum(direction * image, axis=0), ("row", "col"))
        step_size = norm_now / curve
        solution_field = solution_field + step_size[None, :] * direction
        residual = residual - step_size[None, :] * image
        if iteration + 1 < ITERS:
            norm_next = square_sums(residual)
            direction = residual + (norm_next / norm_now)[None, :] * direction
            norm_now = norm_next
    return (solution_field, residual)


def solution(mesh):
    placed = (P(None, ("row", "col")), P(), P(), P(), P(("row", "col"), None))

    def plan(points, lengthscale, noise_var, groups, targets):
        blocks = groups.shape[0]
        square = mesh.shape["row"] == 4 and mesh.shape["col"] in (2, 4, 8, 16)
        whole_field = blocks <= GATHER_LIMIT and blocks == mesh.size and square
        run = gathered_plan if whole_field else per_device
        return run(points, lengthscale, noise_var, groups, targets)

    return jax.shard_map(
        plan,
        mesh=mesh,
        in_specs=placed,
        out_specs=(P(("row", "col"), None), P(("row", "col"), None)),
        check_vma=False,
    )
```

```python
import functools

import functools

import jax
import jax.numpy as jnp
from jax import lax
from jax.experimental import pallas as pl
from jax.experimental.pallas import tpu as pltpu
from jax.sharding import PartitionSpec as P

TILE = 512
ITERS = 2
RHS = 128
CHUNK = 128
GATHER_LIMIT = 64
KEPT = 32
VMEM_LIMIT = 48 * 1024 * 1024
MESH = pl.DeviceIdType.MESH


def split3(value):
    first = value.astype(jnp.bfloat16).astype(jnp.float32)
    rest = value - first
    second = rest.astype(jnp.bfloat16).astype(jnp.float32)
    return first, second, rest - second


def lifted(coords, factor, norm_at, one_at):
    wide = coords.astype(jnp.float32)
    parts = split3(jnp.sum(wide * wide, axis=0, keepdims=True))
    row = lax.broadcasted_iota(jnp.int32, wide.shape, 0)
    tail = jnp.where((row >= one_at) & (row < one_at + 3), 1.0, 0.0)
    for place, part in enumerate(parts):
        tail = jnp.where(row == norm_at + place, part, tail)
    return jnp.concatenate([wide * factor, tail], axis=0).astype(jnp.bfloat16)


def wendland(squared):
    safe = jnp.maximum(squared, 1e-30)
    radius = safe * lax.rsqrt(safe)
    support = jnp.maximum(1.0 - radius, 0.0)
    second = support * support
    third = second * support
    fourth = second * second
    eighth = fourth * fourth
    return ((eighth * third) * (12.0 - 11.0 * support)).astype(jnp.bfloat16)


def place():
    row, col = lax.axis_index("row"), lax.axis_index("col")
    return row // 2, lax.rem(row, 2), col // 2, lax.rem(col, 2)


def device(y, core, z, x):
    return (2 * y + core, 2 * z + x)


def greet(targets):
    barrier = pltpu.get_barrier_semaphore()
    for target in targets:
        pl.semaphore_signal(barrier, inc=1, device_id=target, device_id_type=MESH)


def greeted(targets):
    pl.semaphore_wait(pltpu.get_barrier_semaphore(), len(targets))


class Plane:
    def __init__(self, n_col, out, send_sems, recv_sems):
        self.out, self.send_sems, self.recv_sems = out, send_sems, recv_sems
        self.y, self.core, self.z, self.x = place()
        self.depth = n_col // 2
        self.started = []
        y, core, z, x = self.y, self.core, self.z, self.x
        self.over_x, self.over_y = device(y, core, z, 1 - x), device(1 - y, core, z, x)
        self.over_core = device(y, 1 - core, z, x)
        self.partners = [self.over_x, self.over_y, self.over_core]
        self.partners += [self.over_z(step) for step in range(1, self.depth)]

    def level(self, step):
        return lax.rem(self.z + step, self.depth)

    def over_z(self, step):
        return device(self.y, self.core, self.level(self.depth - step), self.x)

    def launch(self, source, spot, recv_sem, target):
        copy = pltpu.make_async_remote_copy(
            src_ref=source,
            dst_ref=spot,
            send_sem=self.send_sems.at[len(self.started)],
            recv_sem=recv_sem,
            device_id=target,
            device_id_type=MESH,
        )
        copy.start()
        self.started.append(copy)

    def half(self, ref, part):
        lanes = TILE // 2
        return ref.at[:, :, pl.ds(part * lanes, lanes)]

    def spot(self, peer, steps, part):
        return self.half(self.out.at[peer, pl.ds(steps[0], steps[1])], part)

    def send(self, group, steps, peer, part, target, flip, own=None):
        source = self.spot(peer, steps, part) if own is None else self.half(own, part)
        there = peer + flip
        self.launch(source, self.spot(there, steps, part), self.recv_sems.at[group, there, part], target)

    def arrived(self, group, steps, peer, part):
        spot = self.spot(peer, steps, part)
        pltpu.make_async_copy(spot, spot, self.recv_sems.at[group, peer, part]).wait()

    def first_hop(self, group, steps, own=None):
        self.send(group, steps, 0, 0, self.over_x, 1, own)
        self.send(group, steps, 0, 1, self.over_y, 4, own)
        self.send(group, steps, 0, 1, self.over_x, 1, own)
        self.send(group, steps, 0, 0, self.over_y, 4, own)
        self.send(group, steps, 0, 0, self.over_core, 2, own)
        self.send(group, steps, 0, 1, self.over_core, 2, own)

    def second_hop(self, group, steps):
        self.arrived(group, steps, 1, 0)
        self.send(group, steps, 1, 0, self.over_y, 4)
        self.arrived(group, steps, 4, 1)
        self.send(group, steps, 4, 1, self.over_x, 1)
        self.send(group, steps, 1, 0, self.over_core, 2)
        self.send(group, steps, 4, 1, self.over_core, 2)

    def last_hop(self, group, steps):
        for peer, part in ((1, 1), (4, 0), (5, 0), (5, 1)):
            self.arrived(group, steps, peer, part)
            self.send(group, steps, peer, part, self.over_core, 2)

    def finish(self, groups):
        for group, steps in enumerate(groups):
            for peer in (2, 3, 6, 7):
                self.arrived(group, steps, peer, 0)
                self.arrived(group, steps, peer, 1)
        for copy in self.started:
            copy.wait_send()


def level_groups(depth):
    groups = [(step, 1) for step in range(min(depth, 2))]
    return groups + ([(2, depth - 2)] if depth > 2 else [])


def first_gather(n_col, points, scale, targets, out, own, send_sems, recv_sems, z_sems, own_sem):
    plane = Plane(n_col, out, send_sems, recv_sems)
    depth, dims = plane.depth, points.shape[0]
    width = targets.shape[1] // depth
    greet(plane.partners)
    across = lax.broadcasted_iota(jnp.int32, (dims, dims), 1)
    down = lax.broadcasted_iota(jnp.int32, (dims, dims), 0)
    lengths = jnp.sum(jnp.where(across == down, scale[...], 0.0), axis=1, keepdims=True)
    scaled = (points[...] / lengths).astype(jnp.bfloat16)
    turned = targets[...].T.astype(jnp.bfloat16)
    for part in range(depth):
        own[part, 0:width, :] = turned[part * width:(part + 1) * width, :]
        own[part, width:width + dims, :] = scaled
    greeted(plane.partners)
    for step in range(1, depth):
        plane.launch(own.at[plane.level(depth - step)], out.at[0, step], z_sems.at[step], plane.over_z(step))
    groups = level_groups(depth)
    for group, steps in enumerate(groups):
        if group == 0:
            mine = own.at[pl.ds(plane.z, 1)]
            plane.first_hop(0, steps, mine)
            keep = pltpu.make_async_copy(mine, out.at[0, pl.ds(0, 1)], own_sem)
            keep.start()
        else:
            for step in range(steps[0], steps[0] + steps[1]):
                spot = out.at[0, step]
                pltpu.make_async_copy(spot, spot, z_sems.at[step]).wait()
            plane.first_hop(group, steps)
            plane.second_hop(group - 1, groups[group - 1])
        if group >= 2:
            plane.last_hop(group - 2, groups[group - 2])
    last = len(groups) - 1
    plane.second_hop(last, groups[last])
    for group in range(max(last - 1, 0), last + 1):
        plane.last_hop(group, groups[group])
    keep.wait()
    plane.finish(groups)


def second_gather(n_col, own, out, back, send_sems, recv_sems, back_sems, own_sems):
    plane = Plane(n_col, out, send_sems, recv_sems)
    depth = plane.depth
    greet(plane.partners)
    keeps = [
        pltpu.make_async_copy(own, out.at[0], own_sems.at[0]),
        pltpu.make_async_copy(own.at[0], back.at[plane.z], own_sems.at[1]),
    ]
    for keep in keeps:
        keep.start()
    greeted(plane.partners)
    steps = (0, depth)
    plane.first_hop(0, steps, own)
    for step in range(1, depth):
        plane.launch(own.at[depth - step], back.at[plane.z], back_sems.at[step], plane.over_z(step))
    plane.second_hop(0, steps)
    plane.last_hop(0, steps)
    for step in range(1, depth):
        spot = back.at[plane.level(step)]
        pltpu.make_async_copy(spot, spot, back_sems.at[step]).wait()
    for keep in keeps:
        keep.wait()
    plane.finish([steps])


def finish_kernel(n_col, own, back, targets, total, once, twice,
                  land, line, wide, send_sems, recv_sems, line_sends, line_recvs, wide_sends, wide_recvs):
    y, core, z, x = place()
    depth = n_col // 2

    def level(step):
        return lax.rem(z + step, depth)

    column = [device(y, core, level(depth - step), x) for step in range(1, depth)]
    flips = [(a, b, c) for a in range(2) for b in range(2) for c in range(2)][1:]
    plane = [
        device(1 - y if a else y, 1 - core if b else core, z, 1 - x if c else x) for a, b, c in flips
    ]
    greet(column + plane)
    rhs = targets.shape[1]
    target = targets[...]
    image = back[...].reshape(rhs, TILE).astype(jnp.float32).T
    once[...] = image

    def column_sum(value):
        return jnp.sum(value, axis=0, keepdims=True)

    line[0, 0:1, :] = column_sum(target * target)
    line[0, 1:2, :] = column_sum(target * image)
    line[0, 2:3, :] = column_sum(image * image)
    line[0, 5:8, :] = jnp.zeros((3, rhs), jnp.float32)
    greeted(column + plane)

    def remote(source, spot, send_sem, recv_sem, target):
        copy = pltpu.make_async_remote_copy(
            src_ref=source, dst_ref=spot, send_sem=send_sem, recv_sem=recv_sem,
            device_id=target, device_id_type=MESH,
        )
        copy.start()
        return copy

    copies = [
        remote(own.at[depth - step], land.at[z], send_sems.at[step], recv_sems.at[step], column[step - 1])
        for step in range(1, depth)
    ]
    land[z] = own[0]
    for copy in copies:
        copy.wait()
    again = land[...].reshape(rhs, TILE).astype(jnp.float32).T
    twice[...] = again
    line[0, 3:4, :] = column_sum(target * again)
    line[0, 4:5, :] = column_sum(image * again)
    copies = [
        remote(line.at[0], line.at[step], line_sends.at[step], line_recvs.at[step], column[step - 1])
        for step in range(1, depth)
    ]
    for copy in copies:
        copy.wait()
    wide[0] = jnp.sum(line[...], axis=0)
    copies = [
        remote(wide.at[0], wide.at[step + 1], wide_sends.at[step], wide_recvs.at[step], peer)
        for step, peer in enumerate(plane)
    ]
    for copy in copies:
        copy.wait()
    total[...] = jnp.sum(wide[...], axis=0)


def find_tiles(n_col, groups, order):
    y, core, z, x = place()
    depth = n_col // 2

    def label(peer, step):
        other_y = lax.rem(y + peer // 4, 2)
        other_core = lax.rem(core + peer // 2 % 2, 2)
        other_x = lax.rem(x + peer % 2, 2)
        return groups[(2 * other_y + other_core) * n_col + 2 * lax.rem(z + step, depth) + other_x]

    labels = [label(peer, step) for peer in range(8) for step in range(depth)]
    count = jnp.int32(0)
    for level in range(depth):
        for block, other in enumerate(labels):
            order[count] = block * depth + level
            count = count + (other == labels[level]).astype(jnp.int32)
    return count


def lift_rows(n_col, width, gathered, right):
    dims = gathered.shape[1] - width
    for level in range(n_col // 2):
        right[level] = lifted(gathered[level, pl.ds(width, dims), :], 1.0, 0, 3)


def build(width, gathered, block, level, left, right, spot):
    dims = gathered.shape[1] - width
    left[...] = lifted(gathered[block, pl.ds(width, dims), :], -2.0, 3, 0).T
    for start in range(0, TILE, CHUNK):
        rows = pl.ds(start, CHUNK)
        squared = jnp.dot(left[rows, :], right[level], preferred_element_type=jnp.float32)
        spot[rows, :] = wendland(squared)


def first_kernel(n_col, groups, gathered, tiles, narrow,
                 order, left, right, built, image, tile_sems):
    width = narrow.shape[1]
    depth, kept = n_col // 2, tiles.shape[0]
    total = find_tiles(n_col, groups, order)
    lift_rows(n_col, width, gathered, right)
    def tile_copy(slot):
        return pltpu.make_async_copy(built.at[slot], tiles.at[slot], tile_sems.at[slot])

    def spot_of(slot):
        block, level = order[slot] // depth, lax.rem(order[slot], depth)
        return block, level

    def one_tile(slot, carry):
        block, level = spot_of(slot)
        build(width, gathered, block, level, left, right, built.at[slot])
        tile_copy(slot).start()
        return carry

    stored = jnp.minimum(total, kept)
    lax.fori_loop(0, stored, one_tile, 0)
    image[...] = jnp.zeros_like(image)

    def multiply(slot, spot):
        block, level = spot_of(slot)
        image[level] += jnp.dot(
            gathered[block, pl.ds(0, width), :], spot[...], preferred_element_type=jnp.float32
        )

    def one_stored(slot, carry):
        multiply(slot, built.at[slot])
        return carry

    lax.fori_loop(0, stored, one_stored, 0)

    def one_more(slot, carry):
        block, level = spot_of(slot)
        build(width, gathered, block, level, left, right, built.at[kept])
        multiply(slot, built.at[kept])
        return carry

    lax.fori_loop(stored, total, one_more, 0)
    narrow[...] = image[...].astype(jnp.bfloat16)

    def finish(slot, carry):
        tile_copy(slot).wait()
        return carry

    lax.fori_loop(0, stored, finish, 0)


def second_kernel(n_col, groups, gathered, source, tiles, narrow,
                  order, left, right, built, image, tile_sems):
    width = narrow.shape[1]
    depth, kept = n_col // 2, tiles.shape[0]
    total = find_tiles(n_col, groups, order)
    stored = jnp.minimum(total, kept)

    def tile_copy(slot):
        return pltpu.make_async_copy(tiles.at[slot], built.at[slot], tile_sems.at[slot])

    def begin(slot, carry):
        tile_copy(slot).start()
        return carry

    lax.fori_loop(0, stored, begin, 0)
    image[...] = jnp.zeros_like(image)

    def multiply(slot, spot):
        block, level = order[slot] // depth, lax.rem(order[slot], depth)
        image[level] += jnp.dot(source[block], spot[...], preferred_element_type=jnp.float32)

    def one_stored(slot, carry):
        tile_copy(slot).wait()
        multiply(slot, built.at[slot])
        return carry

    lax.fori_loop(0, stored, one_stored, 0)

    @pl.when(total > kept)
    def _():
        lift_rows(n_col, width, gathered, right)

    def one_more(slot, carry):
        block, level = order[slot] // depth, lax.rem(order[slot], depth)
        build(width, gathered, block, level, left, right, built.at[kept])
        multiply(slot, built.at[kept])
        return carry

    lax.fori_loop(stored, total, one_more, 0)
    narrow[...] = image[...].astype(jnp.bfloat16)


def gathered_plan(points, lengthscale, noise_var, groups, targets):
    n_col = lax.axis_size("col")
    depth = n_col // 2
    blocks = groups.shape[0]
    dims = points.shape[0]
    rhs = targets.shape[1]
    width = rhs // depth
    scale = lengthscale[None, :]
    variance = noise_var[None, :]
    parts = len(level_groups(depth))

    vmem = pl.BlockSpec(memory_space=pltpu.VMEM)
    smem = pl.BlockSpec(memory_space=pltpu.SMEM)
    anywhere = pl.BlockSpec(memory_space=pl.ANY)
    slices = jax.ShapeDtypeStruct((depth, width, TILE), jnp.bfloat16)
    whole = jax.ShapeDtypeStruct((TILE, rhs), jnp.float32)

    def remote(number):
        return pltpu.CompilerParams(
            collective_id=number, has_side_effects=True, vmem_limit_bytes=VMEM_LIMIT
        )

    gathered = pl.pallas_call(
        functools.partial(first_gather, n_col),
        out_shape=jax.ShapeDtypeStruct((8, depth, width + dims, TILE), jnp.bfloat16),
        in_specs=[vmem, vmem, vmem],
        out_specs=vmem,
        scratch_shapes=[
            pltpu.VMEM((depth, width + dims, TILE), jnp.bfloat16),
            pltpu.SemaphoreType.DMA((depth - 1 + 14 * parts,)),
            pltpu.SemaphoreType.DMA((parts, 8, 2)),
            pltpu.SemaphoreType.DMA((depth,)),
            pltpu.SemaphoreType.DMA,
        ],
        compiler_params=remote(0),
        name="first_gather",
    )(points, scale, targets).reshape(blocks, width + dims, TILE)

    work = [
        pltpu.SMEM((depth * blocks,), jnp.int32),
        pltpu.VMEM((TILE, 2 * dims), jnp.bfloat16),
        pltpu.VMEM((depth, 2 * dims, TILE), jnp.bfloat16),
        pltpu.VMEM((KEPT + 1, TILE, TILE), jnp.bfloat16),
        pltpu.VMEM((depth, width, TILE), jnp.float32),
        pltpu.SemaphoreType.DMA((KEPT,)),
    ]
    tiles, first = pl.pallas_call(
        functools.partial(first_kernel, n_col),
        out_shape=[jax.ShapeDtypeStruct((KEPT, TILE, TILE), jnp.bfloat16), slices],
        in_specs=[smem, vmem],
        out_specs=[anywhere, vmem],
        scratch_shapes=work,
        compiler_params=pltpu.CompilerParams(vmem_limit_bytes=VMEM_LIMIT),
        name="first_product",
    )(groups, gathered)

    source, back = pl.pallas_call(
        functools.partial(second_gather, n_col),
        out_shape=[jax.ShapeDtypeStruct((8, depth, width, TILE), jnp.bfloat16), slices],
        in_specs=[vmem],
        out_specs=[vmem, vmem],
        scratch_shapes=[
            pltpu.SemaphoreType.DMA((depth - 1 + 14,)),
            pltpu.SemaphoreType.DMA((1, 8, 2)),
            pltpu.SemaphoreType.DMA((depth,)),
            pltpu.SemaphoreType.DMA((2,)),
        ],
        compiler_params=remote(1),
        name="second_gather",
    )(first)

    second = pl.pallas_call(
        functools.partial(second_kernel, n_col),
        out_shape=slices,
        in_specs=[smem, vmem, vmem, anywhere],
        out_specs=vmem,
        scratch_shapes=work,
        compiler_params=pltpu.CompilerParams(vmem_limit_bytes=VMEM_LIMIT),
        name="second_product",
    )(groups, gathered, source.reshape(blocks, width, TILE), tiles)

    total, image, again = pl.pallas_call(
        functools.partial(finish_kernel, n_col),
        out_shape=[jax.ShapeDtypeStruct((8, rhs), jnp.float32), whole, whole],
        in_specs=[vmem, vmem, vmem],
        out_specs=[vmem, vmem, vmem],
        scratch_shapes=[
            pltpu.VMEM((depth, width, TILE), jnp.bfloat16),
            pltpu.VMEM((depth, 8, rhs), jnp.float32),
            pltpu.VMEM((8, 8, rhs), jnp.float32),
        ]
        + [pltpu.SemaphoreType.DMA((depth,))] * 4
        + [pltpu.SemaphoreType.DMA((8,))] * 2,
        compiler_params=remote(2),
        name="finish",
    )(second, back, targets)

    tt, ty, yy, tz, yz = (total[place:place + 1] for place in range(5))
    step = tt / (variance * tt + ty)
    keep = 1.0 - step * variance
    after = keep * keep * tt - 2.0 * keep * step * ty + step * step * yy
    along = keep + after / tt
    squares = along * along * tt - 2.0 * along * step * ty + step * step * yy
    product = along * along * ty - along * step * (tz + yy) + step * step * yz
    second_step = after / (variance * squares + product)
    direction = along * targets - step * image
    applied = variance * direction + along * image - step * again
    solution_field = step * targets + second_step * direction
    residual = keep * targets - step * image - second_step * applied
    return (solution_field, residual)


def kernel_tile(row_coords, col_coords):
    row_norms = jnp.sum(row_coords * row_coords, axis=0)
    col_norms = jnp.sum(col_coords * col_coords, axis=0)
    crossed = lax.dot_general(
        row_coords,
        col_coords,
        (((0,), (0,)), ((), ())),
        precision=lax.Precision.HIGHEST,
        preferred_element_type=jnp.float32,
    )
    squared = jnp.maximum(row_norms[:, None] + col_norms[None, :] - 2.0 * crossed, 0.0)
    radius = jnp.sqrt(squared)
    support = jnp.maximum(1.0 - radius, 0.0)
    return (support**11 * (11.0 * radius + 1.0)).astype(jnp.bfloat16)


def per_device(points, lengthscale, noise_var, groups, targets):
    n_row = lax.axis_size("row")
    n_col = lax.axis_size("col")
    own_blocks = targets.shape[0] // TILE
    row_blocks = own_blocks * n_col
    col_blocks = own_blocks * n_row
    scaled = points / lengthscale[:, None]
    row_coords = lax.all_gather(scaled.astype(jnp.bfloat16), "col", axis=1, tiled=True).astype(
        scaled.dtype
    )
    col_coords = lax.all_gather(scaled.astype(jnp.bfloat16), "row", axis=1, tiled=True).astype(
        scaled.dtype
    )
    row_place = lax.axis_index("row")
    col_place = lax.axis_index("col")
    row_groups = lax.dynamic_slice_in_dim(groups, row_place * row_blocks, row_blocks, 0)
    col_groups = lax.dynamic_index_in_dim(
        groups.reshape(n_row, n_col, own_blocks), col_place, 1, keepdims=False
    ).reshape(col_blocks)
    flat_mask = (row_groups[:, None] == col_groups[None, :]).reshape(row_blocks * col_blocks)
    tile_count = jnp.sum(flat_mask.astype(jnp.int32))
    tile_order = jnp.nonzero(flat_mask, size=row_blocks * col_blocks, fill_value=0)[0].astype(
        jnp.int32
    )

    def square_sums(vector):
        return lax.psum(jnp.sum(vector * vector, axis=0), ("row", "col"))

    solution_field = jnp.zeros_like(targets)
    residual = targets
    direction = targets
    norm_now = square_sums(residual)
    for iteration in range(ITERS):
        narrow = direction.astype(jnp.bfloat16)
        operator_source = lax.all_gather(narrow, "row", axis=0, tiled=True)
        source = operator_source
        initial = jnp.zeros((row_blocks * TILE, RHS), jnp.float32)

        def one_tile(position, summed):
            flat_index = tile_order[position]
            row_slot = flat_index // col_blocks
            col_slot = flat_index % col_blocks
            left = lax.dynamic_slice_in_dim(row_coords, row_slot * TILE, TILE, 1)
            right = lax.dynamic_slice_in_dim(col_coords, col_slot * TILE, TILE, 1)
            values = kernel_tile(left, right)
            block_vec = lax.dynamic_slice_in_dim(source, col_slot * TILE, TILE, 0)
            product = jnp.dot(values, block_vec, preferred_element_type=jnp.float32)
            current = lax.dynamic_slice_in_dim(summed, row_slot * TILE, TILE, 0)
            return lax.dynamic_update_slice_in_dim(summed, current + product, row_slot * TILE, 0)

        partial_value = lax.fori_loop(0, tile_count, one_tile, initial)
        outgoing = partial_value.astype(jnp.bfloat16).reshape(n_col, own_blocks * TILE, RHS)
        incoming = lax.all_to_all(outgoing, "col", split_axis=0, concat_axis=0, tiled=True)
        operator_product = jnp.sum(incoming, axis=0, dtype=jnp.float32)
        image = noise_var[None, :] * direction + operator_product
        curve = lax.psum(jnp.sum(direction * image, axis=0), ("row", "col"))
        step_size = norm_now / curve
        solution_field = solution_field + step_size[None, :] * direction
        residual = residual - step_size[None, :] * image
        if iteration + 1 < ITERS:
            norm_next = square_sums(residual)
            direction = residual + (norm_next / norm_now)[None, :] * direction
            norm_now = norm_next
    return (solution_field, residual)


def solution(mesh):
    placed = (P(None, ("row", "col")), P(), P(), P(), P(("row", "col"), None))

    def plan(points, lengthscale, noise_var, groups, targets):
        blocks = groups.shape[0]
        square = mesh.shape["row"] == 4 and mesh.shape["col"] in (2, 4, 8, 16)
        whole_field = blocks <= GATHER_LIMIT and blocks == mesh.size and square
        run = gathered_plan if whole_field else per_device
        return run(points, lengthscale, noise_var, groups, targets)

    return jax.shard_map(
        plan,
        mesh=mesh,
        in_specs=placed,
        out_specs=(P(("row", "col"), None), P(("row", "col"), None)),
        check_vma=False,
    )
```

```python
import functools

import functools

import jax
import jax.numpy as jnp
from jax import lax
from jax.experimental import pallas as pl
from jax.experimental.pallas import tpu as pltpu
from jax.sharding import PartitionSpec as P

TILE = 512
ITERS = 2
RHS = 128
CHUNK = 128
GATHER_LIMIT = 64
KEPT = 32
VMEM_LIMIT = 24 * 1024 * 1024
MESH = pl.DeviceIdType.MESH


def split3(value):
    first = value.astype(jnp.bfloat16).astype(jnp.float32)
    rest = value - first
    second = rest.astype(jnp.bfloat16).astype(jnp.float32)
    return first, second, rest - second


def lifted(coords, factor, norm_at, one_at):
    wide = coords.astype(jnp.float32)
    parts = split3(jnp.sum(wide * wide, axis=0, keepdims=True))
    row = lax.broadcasted_iota(jnp.int32, wide.shape, 0)
    tail = jnp.where((row >= one_at) & (row < one_at + 3), 1.0, 0.0)
    for place, part in enumerate(parts):
        tail = jnp.where(row == norm_at + place, part, tail)
    return jnp.concatenate([wide * factor, tail], axis=0).astype(jnp.bfloat16)


def wendland(squared):
    safe = jnp.maximum(squared, 1e-30)
    radius = safe * lax.rsqrt(safe)
    support = jnp.maximum(1.0 - radius, 0.0)
    second = support * support
    third = second * support
    fourth = second * second
    eighth = fourth * fourth
    return ((eighth * third) * (12.0 - 11.0 * support)).astype(jnp.bfloat16)


def place():
    row, col = lax.axis_index("row"), lax.axis_index("col")
    return row // 2, lax.rem(row, 2), col // 2, lax.rem(col, 2)


def device(y, core, z, x):
    return (2 * y + core, 2 * z + x)


def greet(targets):
    barrier = pltpu.get_barrier_semaphore()
    for target in targets:
        pl.semaphore_signal(barrier, inc=1, device_id=target, device_id_type=MESH)


def greeted(targets):
    pl.semaphore_wait(pltpu.get_barrier_semaphore(), len(targets))


class Plane:
    def __init__(self, n_col, out, send_sems, recv_sems):
        self.out, self.send_sems, self.recv_sems = out, send_sems, recv_sems
        self.y, self.core, self.z, self.x = place()
        self.depth = n_col // 2
        self.started = []
        y, core, z, x = self.y, self.core, self.z, self.x
        self.over_x, self.over_y = device(y, core, z, 1 - x), device(1 - y, core, z, x)
        self.over_core = device(y, 1 - core, z, x)
        self.partners = [self.over_x, self.over_y, self.over_core]
        self.partners += [self.over_z(step) for step in range(1, self.depth)]

    def level(self, step):
        return lax.rem(self.z + step, self.depth)

    def over_z(self, step):
        return device(self.y, self.core, self.level(self.depth - step), self.x)

    def launch(self, source, spot, recv_sem, target):
        copy = pltpu.make_async_remote_copy(
            src_ref=source,
            dst_ref=spot,
            send_sem=self.send_sems.at[len(self.started)],
            recv_sem=recv_sem,
            device_id=target,
            device_id_type=MESH,
        )
        copy.start()
        self.started.append(copy)

    def half(self, ref, part):
        lanes = TILE // 2
        return ref.at[:, :, pl.ds(part * lanes, lanes)]

    def spot(self, peer, steps, part):
        return self.half(self.out.at[peer, pl.ds(steps[0], steps[1])], part)

    def send(self, group, steps, peer, part, target, flip, own=None):
        source = self.spot(peer, steps, part) if own is None else self.half(own, part)
        there = peer + flip
        self.launch(source, self.spot(there, steps, part), self.recv_sems.at[group, there, part], target)

    def arrived(self, group, steps, peer, part):
        spot = self.spot(peer, steps, part)
        pltpu.make_async_copy(spot, spot, self.recv_sems.at[group, peer, part]).wait()

    def first_hop(self, group, steps, own=None):
        self.send(group, steps, 0, 0, self.over_x, 1, own)
        self.send(group, steps, 0, 1, self.over_y, 4, own)
        self.send(group, steps, 0, 1, self.over_x, 1, own)
        self.send(group, steps, 0, 0, self.over_y, 4, own)
        self.send(group, steps, 0, 0, self.over_core, 2, own)
        self.send(group, steps, 0, 1, self.over_core, 2, own)

    def second_hop(self, group, steps):
        self.arrived(group, steps, 1, 0)
        self.send(group, steps, 1, 0, self.over_y, 4)
        self.arrived(group, steps, 4, 1)
        self.send(group, steps, 4, 1, self.over_x, 1)
        self.send(group, steps, 1, 0, self.over_core, 2)
        self.send(group, steps, 4, 1, self.over_core, 2)

    def last_hop(self, group, steps):
        for peer, part in ((1, 1), (4, 0), (5, 0), (5, 1)):
            self.arrived(group, steps, peer, part)
            self.send(group, steps, peer, part, self.over_core, 2)

    def finish(self, groups):
        for group, steps in enumerate(groups):
            for peer in (2, 3, 6, 7):
                self.arrived(group, steps, peer, 0)
                self.arrived(group, steps, peer, 1)
        for copy in self.started:
            copy.wait_send()


def level_groups(depth):
    groups = [(step, 1) for step in range(min(depth, 2))]
    return groups + ([(2, depth - 2)] if depth > 2 else [])


def first_gather(n_col, points, scale, targets, out, own, send_sems, recv_sems, z_sems, own_sem):
    plane = Plane(n_col, out, send_sems, recv_sems)
    depth, dims = plane.depth, points.shape[0]
    width = targets.shape[1] // depth
    greet(plane.partners)
    across = lax.broadcasted_iota(jnp.int32, (dims, dims), 1)
    down = lax.broadcasted_iota(jnp.int32, (dims, dims), 0)
    lengths = jnp.sum(jnp.where(across == down, scale[...], 0.0), axis=1, keepdims=True)
    scaled = (points[...] / lengths).astype(jnp.bfloat16)
    turned = targets[...].T.astype(jnp.bfloat16)
    for part in range(depth):
        own[part, 0:width, :] = turned[part * width:(part + 1) * width, :]
        own[part, width:width + dims, :] = scaled
    greeted(plane.partners)
    for step in range(1, depth):
        plane.launch(own.at[plane.level(depth - step)], out.at[0, step], z_sems.at[step], plane.over_z(step))
    groups = level_groups(depth)
    for group, steps in enumerate(groups):
        if group == 0:
            mine = own.at[pl.ds(plane.z, 1)]
            plane.first_hop(0, steps, mine)
            keep = pltpu.make_async_copy(mine, out.at[0, pl.ds(0, 1)], own_sem)
            keep.start()
        else:
            for step in range(steps[0], steps[0] + steps[1]):
                spot = out.at[0, step]
                pltpu.make_async_copy(spot, spot, z_sems.at[step]).wait()
            plane.first_hop(group, steps)
            plane.second_hop(group - 1, groups[group - 1])
        if group >= 2:
            plane.last_hop(group - 2, groups[group - 2])
    last = len(groups) - 1
    plane.second_hop(last, groups[last])
    for group in range(max(last - 1, 0), last + 1):
        plane.last_hop(group, groups[group])
    keep.wait()
    plane.finish(groups)


def second_gather(n_col, own, out, back, send_sems, recv_sems, back_sems, own_sems):
    plane = Plane(n_col, out, send_sems, recv_sems)
    depth = plane.depth
    greet(plane.partners)
    keeps = [
        pltpu.make_async_copy(own, out.at[0], own_sems.at[0]),
        pltpu.make_async_copy(own.at[0], back.at[plane.z], own_sems.at[1]),
    ]
    for keep in keeps:
        keep.start()
    greeted(plane.partners)
    steps = (0, depth)
    plane.first_hop(0, steps, own)
    for step in range(1, depth):
        plane.launch(own.at[depth - step], back.at[plane.z], back_sems.at[step], plane.over_z(step))
    plane.second_hop(0, steps)
    plane.last_hop(0, steps)
    for step in range(1, depth):
        spot = back.at[plane.level(step)]
        pltpu.make_async_copy(spot, spot, back_sems.at[step]).wait()
    for keep in keeps:
        keep.wait()
    plane.finish([steps])


def finish_kernel(n_col, own, back, targets, total, once, twice,
                  land, line, wide, send_sems, recv_sems, line_sends, line_recvs, wide_sends, wide_recvs):
    y, core, z, x = place()
    depth = n_col // 2

    def level(step):
        return lax.rem(z + step, depth)

    column = [device(y, core, level(depth - step), x) for step in range(1, depth)]
    flips = [(a, b, c) for a in range(2) for b in range(2) for c in range(2)][1:]
    plane = [
        device(1 - y if a else y, 1 - core if b else core, z, 1 - x if c else x) for a, b, c in flips
    ]
    greet(column + plane)
    rhs = targets.shape[1]
    target = targets[...]
    image = back[...].reshape(rhs, TILE).astype(jnp.float32).T
    once[...] = image

    def column_sum(value):
        return jnp.sum(value, axis=0, keepdims=True)

    line[0, 0:1, :] = column_sum(target * target)
    line[0, 1:2, :] = column_sum(target * image)
    line[0, 2:3, :] = column_sum(image * image)
    line[0, 5:8, :] = jnp.zeros((3, rhs), jnp.float32)
    greeted(column + plane)

    def remote(source, spot, send_sem, recv_sem, target):
        copy = pltpu.make_async_remote_copy(
            src_ref=source, dst_ref=spot, send_sem=send_sem, recv_sem=recv_sem,
            device_id=target, device_id_type=MESH,
        )
        copy.start()
        return copy

    copies = [
        remote(own.at[depth - step], land.at[z], send_sems.at[step], recv_sems.at[step], column[step - 1])
        for step in range(1, depth)
    ]
    land[z] = own[0]
    for copy in copies:
        copy.wait()
    again = land[...].reshape(rhs, TILE).astype(jnp.float32).T
    twice[...] = again
    line[0, 3:4, :] = column_sum(target * again)
    line[0, 4:5, :] = column_sum(image * again)
    copies = [
        remote(line.at[0], line.at[step], line_sends.at[step], line_recvs.at[step], column[step - 1])
        for step in range(1, depth)
    ]
    for copy in copies:
        copy.wait()
    wide[0] = jnp.sum(line[...], axis=0)
    copies = [
        remote(wide.at[0], wide.at[step + 1], wide_sends.at[step], wide_recvs.at[step], peer)
        for step, peer in enumerate(plane)
    ]
    for copy in copies:
        copy.wait()
    total[...] = jnp.sum(wide[...], axis=0)


def find_tiles(n_col, groups, order):
    y, core, z, x = place()
    depth = n_col // 2

    def label(peer, step):
        other_y = lax.rem(y + peer // 4, 2)
        other_core = lax.rem(core + peer // 2 % 2, 2)
        other_x = lax.rem(x + peer % 2, 2)
        return groups[(2 * other_y + other_core) * n_col + 2 * lax.rem(z + step, depth) + other_x]

    labels = [label(peer, step) for peer in range(8) for step in range(depth)]
    count = jnp.int32(0)
    for level in range(depth):
        for block, other in enumerate(labels):
            order[count] = block * depth + level
            count = count + (other == labels[level]).astype(jnp.int32)
    return count


def lift_rows(n_col, width, gathered, right):
    dims = gathered.shape[1] - width
    for level in range(n_col // 2):
        right[level] = lifted(gathered[level, pl.ds(width, dims), :], 1.0, 0, 3)


def build(width, gathered, block, level, left, right, spot):
    dims = gathered.shape[1] - width
    left[...] = lifted(gathered[block, pl.ds(width, dims), :], -2.0, 3, 0).T
    for start in range(0, TILE, CHUNK):
        rows = pl.ds(start, CHUNK)
        squared = jnp.dot(left[rows, :], right[level], preferred_element_type=jnp.float32)
        spot[rows, :] = wendland(squared)


def spot_of(depth, order, slot):
    return order[slot] // depth, lax.rem(order[slot], depth)


def first_kernel(n_col, groups, gathered, tiles, narrow, order, left, right, spare, image):
    width = narrow.shape[1]
    depth, kept = n_col // 2, tiles.shape[0]
    total = find_tiles(n_col, groups, order)
    stored = jnp.minimum(total, kept)
    lift_rows(n_col, width, gathered, right)
    image[...] = jnp.zeros_like(image)

    def one_tile(slot, carry):
        block, level = spot_of(depth, order, slot)
        build(width, gathered, block, level, left, right, tiles.at[slot])
        return carry

    def multiply(slot, tile):
        block, level = spot_of(depth, order, slot)
        image[level] += jnp.dot(
            gathered[block, pl.ds(0, width), :], tile[...], preferred_element_type=jnp.float32
        )

    def one_stored(slot, carry):
        multiply(slot, tiles.at[slot])
        return carry

    def one_more(slot, carry):
        block, level = spot_of(depth, order, slot)
        build(width, gathered, block, level, left, right, spare)
        multiply(slot, spare)
        return carry

    lax.fori_loop(0, stored, one_tile, 0)
    lax.fori_loop(0, stored, one_stored, 0)
    lax.fori_loop(stored, total, one_more, 0)
    narrow[...] = image[...].astype(jnp.bfloat16)


def second_kernel(n_col, groups, gathered, source, tiles, narrow, order, left, right, spare, image):
    width = narrow.shape[1]
    depth, kept = n_col // 2, tiles.shape[0]
    total = find_tiles(n_col, groups, order)
    stored = jnp.minimum(total, kept)
    image[...] = jnp.zeros_like(image)

    def multiply(slot, tile):
        block, level = spot_of(depth, order, slot)
        image[level] += jnp.dot(source[block], tile[...], preferred_element_type=jnp.float32)

    def one_stored(slot, carry):
        multiply(slot, tiles.at[slot])
        return carry

    lax.fori_loop(0, stored, one_stored, 0)

    @pl.when(total > kept)
    def _():
        lift_rows(n_col, width, gathered, right)

    def one_more(slot, carry):
        block, level = spot_of(depth, order, slot)
        build(width, gathered, block, level, left, right, spare)
        multiply(slot, spare)
        return carry

    lax.fori_loop(stored, total, one_more, 0)
    narrow[...] = image[...].astype(jnp.bfloat16)


def gathered_plan(points, lengthscale, noise_var, groups, targets):
    n_col = lax.axis_size("col")
    depth = n_col // 2
    blocks = groups.shape[0]
    dims = points.shape[0]
    rhs = targets.shape[1]
    width = rhs // depth
    scale = lengthscale[None, :]
    variance = noise_var[None, :]
    parts = len(level_groups(depth))

    vmem = pl.BlockSpec(memory_space=pltpu.VMEM)
    smem = pl.BlockSpec(memory_space=pltpu.SMEM)
    slices = jax.ShapeDtypeStruct((depth, width, TILE), jnp.bfloat16)
    whole = jax.ShapeDtypeStruct((TILE, rhs), jnp.float32)

    def remote(number):
        return pltpu.CompilerParams(
            collective_id=number, has_side_effects=True, vmem_limit_bytes=VMEM_LIMIT
        )

    gathered = pl.pallas_call(
        functools.partial(first_gather, n_col),
        out_shape=jax.ShapeDtypeStruct((8, depth, width + dims, TILE), jnp.bfloat16),
        in_specs=[vmem, vmem, vmem],
        out_specs=vmem,
        scratch_shapes=[
            pltpu.VMEM((depth, width + dims, TILE), jnp.bfloat16),
            pltpu.SemaphoreType.DMA((depth - 1 + 14 * parts,)),
            pltpu.SemaphoreType.DMA((parts, 8, 2)),
            pltpu.SemaphoreType.DMA((depth,)),
            pltpu.SemaphoreType.DMA,
        ],
        compiler_params=remote(0),
        name="first_gather",
    )(points, scale, targets).reshape(blocks, width + dims, TILE)

    work = [
        pltpu.SMEM((depth * blocks,), jnp.int32),
        pltpu.VMEM((TILE, 2 * dims), jnp.bfloat16),
        pltpu.VMEM((depth, 2 * dims, TILE), jnp.bfloat16),
        pltpu.VMEM((TILE, TILE), jnp.bfloat16),
        pltpu.VMEM((depth, width, TILE), jnp.float32),
    ]
    tiles, first = pl.pallas_call(
        functools.partial(first_kernel, n_col),
        out_shape=[jax.ShapeDtypeStruct((KEPT, TILE, TILE), jnp.bfloat16), slices],
        in_specs=[smem, vmem],
        out_specs=[vmem, vmem],
        scratch_shapes=work,
        compiler_params=pltpu.CompilerParams(vmem_limit_bytes=VMEM_LIMIT),
        name="first_product",
    )(groups, gathered)

    source, back = pl.pallas_call(
        functools.partial(second_gather, n_col),
        out_shape=[jax.ShapeDtypeStruct((8, depth, width, TILE), jnp.bfloat16), slices],
        in_specs=[vmem],
        out_specs=[vmem, vmem],
        scratch_shapes=[
            pltpu.SemaphoreType.DMA((depth - 1 + 14,)),
            pltpu.SemaphoreType.DMA((1, 8, 2)),
            pltpu.SemaphoreType.DMA((depth,)),
            pltpu.SemaphoreType.DMA((2,)),
        ],
        compiler_params=remote(1),
        name="second_gather",
    )(first)

    second = pl.pallas_call(
        functools.partial(second_kernel, n_col),
        out_shape=slices,
        in_specs=[smem, vmem, vmem, vmem],
        out_specs=vmem,
        scratch_shapes=work,
        compiler_params=pltpu.CompilerParams(vmem_limit_bytes=VMEM_LIMIT),
        name="second_product",
    )(groups, gathered, source.reshape(blocks, width, TILE), tiles)

    total, image, again = pl.pallas_call(
        functools.partial(finish_kernel, n_col),
        out_shape=[jax.ShapeDtypeStruct((8, rhs), jnp.float32), whole, whole],
        in_specs=[vmem, vmem, vmem],
        out_specs=[vmem, vmem, vmem],
        scratch_shapes=[
            pltpu.VMEM((depth, width, TILE), jnp.bfloat16),
            pltpu.VMEM((depth, 8, rhs), jnp.float32),
            pltpu.VMEM((8, 8, rhs), jnp.float32),
        ]
        + [pltpu.SemaphoreType.DMA((depth,))] * 4
        + [pltpu.SemaphoreType.DMA((8,))] * 2,
        compiler_params=remote(2),
        name="finish",
    )(second, back, targets)

    tt, ty, yy, tz, yz = (total[place:place + 1] for place in range(5))
    step = tt / (variance * tt + ty)
    keep = 1.0 - step * variance
    after = keep * keep * tt - 2.0 * keep * step * ty + step * step * yy
    along = keep + after / tt
    squares = along * along * tt - 2.0 * along * step * ty + step * step * yy
    product = along * along * ty - along * step * (tz + yy) + step * step * yz
    second_step = after / (variance * squares + product)
    direction = along * targets - step * image
    applied = variance * direction + along * image - step * again
    solution_field = step * targets + second_step * direction
    residual = keep * targets - step * image - second_step * applied
    return (solution_field, residual)


def kernel_tile(row_coords, col_coords):
    row_norms = jnp.sum(row_coords * row_coords, axis=0)
    col_norms = jnp.sum(col_coords * col_coords, axis=0)
    crossed = lax.dot_general(
        row_coords,
        col_coords,
        (((0,), (0,)), ((), ())),
        precision=lax.Precision.HIGHEST,
        preferred_element_type=jnp.float32,
    )
    squared = jnp.maximum(row_norms[:, None] + col_norms[None, :] - 2.0 * crossed, 0.0)
    radius = jnp.sqrt(squared)
    support = jnp.maximum(1.0 - radius, 0.0)
    return (support**11 * (11.0 * radius + 1.0)).astype(jnp.bfloat16)


def per_device(points, lengthscale, noise_var, groups, targets):
    n_row = lax.axis_size("row")
    n_col = lax.axis_size("col")
    own_blocks = targets.shape[0] // TILE
    row_blocks = own_blocks * n_col
    col_blocks = own_blocks * n_row
    scaled = points / lengthscale[:, None]
    row_coords = lax.all_gather(scaled.astype(jnp.bfloat16), "col", axis=1, tiled=True).astype(
        scaled.dtype
    )
    col_coords = lax.all_gather(scaled.astype(jnp.bfloat16), "row", axis=1, tiled=True).astype(
        scaled.dtype
    )
    row_place = lax.axis_index("row")
    col_place = lax.axis_index("col")
    row_groups = lax.dynamic_slice_in_dim(groups, row_place * row_blocks, row_blocks, 0)
    col_groups = lax.dynamic_index_in_dim(
        groups.reshape(n_row, n_col, own_blocks), col_place, 1, keepdims=False
    ).reshape(col_blocks)
    flat_mask = (row_groups[:, None] == col_groups[None, :]).reshape(row_blocks * col_blocks)
    tile_count = jnp.sum(flat_mask.astype(jnp.int32))
    tile_order = jnp.nonzero(flat_mask, size=row_blocks * col_blocks, fill_value=0)[0].astype(
        jnp.int32
    )

    def square_sums(vector):
        return lax.psum(jnp.sum(vector * vector, axis=0), ("row", "col"))

    solution_field = jnp.zeros_like(targets)
    residual = targets
    direction = targets
    norm_now = square_sums(residual)
    for iteration in range(ITERS):
        narrow = direction.astype(jnp.bfloat16)
        operator_source = lax.all_gather(narrow, "row", axis=0, tiled=True)
        source = operator_source
        initial = jnp.zeros((row_blocks * TILE, RHS), jnp.float32)

        def one_tile(position, summed):
            flat_index = tile_order[position]
            row_slot = flat_index // col_blocks
            col_slot = flat_index % col_blocks
            left = lax.dynamic_slice_in_dim(row_coords, row_slot * TILE, TILE, 1)
            right = lax.dynamic_slice_in_dim(col_coords, col_slot * TILE, TILE, 1)
            values = kernel_tile(left, right)
            block_vec = lax.dynamic_slice_in_dim(source, col_slot * TILE, TILE, 0)
            product = jnp.dot(values, block_vec, preferred_element_type=jnp.float32)
            current = lax.dynamic_slice_in_dim(summed, row_slot * TILE, TILE, 0)
            return lax.dynamic_update_slice_in_dim(summed, current + product, row_slot * TILE, 0)

        partial_value = lax.fori_loop(0, tile_count, one_tile, initial)
        outgoing = partial_value.astype(jnp.bfloat16).reshape(n_col, own_blocks * TILE, RHS)
        incoming = lax.all_to_all(outgoing, "col", split_axis=0, concat_axis=0, tiled=True)
        operator_product = jnp.sum(incoming, axis=0, dtype=jnp.float32)
        image = noise_var[None, :] * direction + operator_product
        curve = lax.psum(jnp.sum(direction * image, axis=0), ("row", "col"))
        step_size = norm_now / curve
        solution_field = solution_field + step_size[None, :] * direction
        residual = residual - step_size[None, :] * image
        if iteration + 1 < ITERS:
            norm_next = square_sums(residual)
            direction = residual + (norm_next / norm_now)[None, :] * direction
            norm_now = norm_next
    return (solution_field, residual)


def solution(mesh):
    placed = (P(None, ("row", "col")), P(), P(), P(), P(("row", "col"), None))

    def plan(points, lengthscale, noise_var, groups, targets):
        blocks = groups.shape[0]
        square = mesh.shape["row"] == 4 and mesh.shape["col"] in (2, 4, 8, 16)
        whole_field = blocks <= GATHER_LIMIT and blocks == mesh.size and square
        run = gathered_plan if whole_field else per_device
        return run(points, lengthscale, noise_var, groups, targets)

    return jax.shard_map(
        plan,
        mesh=mesh,
        in_specs=placed,
        out_specs=(P(("row", "col"), None), P(("row", "col"), None)),
        check_vma=False,
    )
```

```python
import functools

import functools

import jax
import jax.numpy as jnp
from jax import lax
from jax.experimental import pallas as pl
from jax.experimental.pallas import tpu as pltpu
from jax.sharding import PartitionSpec as P

TILE = 512
ITERS = 2
RHS = 128
CHUNK = 128
GATHER_LIMIT = 64
KEPT = 32
VMEM_LIMIT = 24 * 1024 * 1024
MESH = pl.DeviceIdType.MESH


def split3(value):
    first = value.astype(jnp.bfloat16).astype(jnp.float32)
    rest = value - first
    second = rest.astype(jnp.bfloat16).astype(jnp.float32)
    return first, second, rest - second


def lifted(coords, factor, norm_at, one_at):
    wide = coords.astype(jnp.float32)
    parts = split3(jnp.sum(wide * wide, axis=0, keepdims=True))
    row = lax.broadcasted_iota(jnp.int32, wide.shape, 0)
    tail = jnp.where((row >= one_at) & (row < one_at + 3), 1.0, 0.0)
    for place, part in enumerate(parts):
        tail = jnp.where(row == norm_at + place, part, tail)
    return jnp.concatenate([wide * factor, tail], axis=0).astype(jnp.bfloat16)


def wendland(squared):
    safe = jnp.maximum(squared, 1e-30)
    radius = safe * lax.rsqrt(safe)
    support = jnp.maximum(1.0 - radius, 0.0)
    second = support * support
    third = second * support
    fourth = second * second
    eighth = fourth * fourth
    return ((eighth * third) * (12.0 - 11.0 * support)).astype(jnp.bfloat16)


def place():
    row, col = lax.axis_index("row"), lax.axis_index("col")
    return row // 2, lax.rem(row, 2), col // 2, lax.rem(col, 2)


def device(y, core, z, x):
    return (2 * y + core, 2 * z + x)


def greet(targets):
    barrier = pltpu.get_barrier_semaphore()
    for target in targets:
        pl.semaphore_signal(barrier, inc=1, device_id=target, device_id_type=MESH)


def greeted(targets):
    pl.semaphore_wait(pltpu.get_barrier_semaphore(), len(targets))


class Plane:
    def __init__(self, n_col, out, send_sems, recv_sems):
        self.out, self.send_sems, self.recv_sems = out, send_sems, recv_sems
        self.y, self.core, self.z, self.x = place()
        self.depth = n_col // 2
        self.started = []
        y, core, z, x = self.y, self.core, self.z, self.x
        self.over_x, self.over_y = device(y, core, z, 1 - x), device(1 - y, core, z, x)
        self.over_core = device(y, 1 - core, z, x)
        self.partners = [self.over_x, self.over_y, self.over_core]
        self.partners += [self.over_z(step) for step in range(1, self.depth)]

    def level(self, step):
        return lax.rem(self.z + step, self.depth)

    def over_z(self, step):
        return device(self.y, self.core, self.level(self.depth - step), self.x)

    def launch(self, source, spot, recv_sem, target):
        copy = pltpu.make_async_remote_copy(
            src_ref=source,
            dst_ref=spot,
            send_sem=self.send_sems.at[len(self.started)],
            recv_sem=recv_sem,
            device_id=target,
            device_id_type=MESH,
        )
        copy.start()
        self.started.append(copy)

    def half(self, ref, part):
        lanes = TILE // 2
        return ref.at[:, :, pl.ds(part * lanes, lanes)]

    def spot(self, peer, steps, part):
        return self.half(self.out.at[peer, pl.ds(steps[0], steps[1])], part)

    def send(self, group, steps, peer, part, target, flip, own=None):
        source = self.spot(peer, steps, part) if own is None else self.half(own, part)
        there = peer + flip
        self.launch(source, self.spot(there, steps, part), self.recv_sems.at[group, there, part], target)

    def arrived(self, group, steps, peer, part):
        spot = self.spot(peer, steps, part)
        pltpu.make_async_copy(spot, spot, self.recv_sems.at[group, peer, part]).wait()

    def first_hop(self, group, steps, own=None):
        self.send(group, steps, 0, 0, self.over_x, 1, own)
        self.send(group, steps, 0, 1, self.over_y, 4, own)
        self.send(group, steps, 0, 1, self.over_x, 1, own)
        self.send(group, steps, 0, 0, self.over_y, 4, own)
        self.send(group, steps, 0, 0, self.over_core, 2, own)
        self.send(group, steps, 0, 1, self.over_core, 2, own)

    def second_hop(self, group, steps):
        self.arrived(group, steps, 1, 0)
        self.send(group, steps, 1, 0, self.over_y, 4)
        self.arrived(group, steps, 4, 1)
        self.send(group, steps, 4, 1, self.over_x, 1)
        self.send(group, steps, 1, 0, self.over_core, 2)
        self.send(group, steps, 4, 1, self.over_core, 2)

    def last_hop(self, group, steps):
        for peer, part in ((1, 1), (4, 0), (5, 0), (5, 1)):
            self.arrived(group, steps, peer, part)
            self.send(group, steps, peer, part, self.over_core, 2)

    def finish(self, groups):
        for group, steps in enumerate(groups):
            for peer in (2, 3, 6, 7):
                self.arrived(group, steps, peer, 0)
                self.arrived(group, steps, peer, 1)
        for copy in self.started:
            copy.wait_send()


def level_groups(depth):
    groups = [(step, 1) for step in range(min(depth, 2))]
    return groups + ([(2, depth - 2)] if depth > 2 else [])


def build_own(coords, spot):
    left, right = lifted(coords, -2.0, 3, 0).T, lifted(coords, 1.0, 0, 3)
    for start in range(0, TILE, CHUNK):
        squared = jnp.dot(left[start:start + CHUNK, :], right, preferred_element_type=jnp.float32)
        spot[pl.ds(start, CHUNK), :] = wendland(squared)


def first_gather(n_col, points, scale, targets, out, diagonal, own, send_sems, recv_sems, z_sems, own_sem):
    plane = Plane(n_col, out, send_sems, recv_sems)
    depth, dims = plane.depth, points.shape[0]
    width = targets.shape[1] // depth
    greet(plane.partners)
    across = lax.broadcasted_iota(jnp.int32, (dims, dims), 1)
    down = lax.broadcasted_iota(jnp.int32, (dims, dims), 0)
    lengths = jnp.sum(jnp.where(across == down, scale[...], 0.0), axis=1, keepdims=True)
    scaled = (points[...] / lengths).astype(jnp.bfloat16)
    turned = targets[...].T.astype(jnp.bfloat16)
    for part in range(depth):
        own[part, 0:width, :] = turned[part * width:(part + 1) * width, :]
        own[part, width:width + dims, :] = scaled
    greeted(plane.partners)
    for step in range(1, depth):
        plane.launch(own.at[plane.level(depth - step)], out.at[0, step], z_sems.at[step], plane.over_z(step))
    groups = level_groups(depth)
    last = len(groups) - 1

    def build_group(group):
        steps = groups[group]
        for step in range(steps[0], steps[0] + steps[1]):
            build_own(scaled if step == 0 else out[0, step, pl.ds(width, dims), :], diagonal.at[step])

    for group, steps in enumerate(groups):
        if group == 0:
            mine = own.at[pl.ds(plane.z, 1)]
            plane.first_hop(0, steps, mine)
            keep = pltpu.make_async_copy(mine, out.at[0, pl.ds(0, 1)], own_sem)
            keep.start()
        else:
            for step in range(steps[0], steps[0] + steps[1]):
                spot = out.at[0, step]
                pltpu.make_async_copy(spot, spot, z_sems.at[step]).wait()
            plane.first_hop(group, steps)
            plane.second_hop(group - 1, groups[group - 1])
        if group >= 2:
            plane.last_hop(group - 2, groups[group - 2])
        if group < last:
            build_group(group)
    plane.second_hop(last, groups[last])
    build_group(last)
    for group in range(max(last - 1, 0), last + 1):
        plane.last_hop(group, groups[group])
    keep.wait()
    plane.finish(groups)


def second_gather(n_col, own, out, back, send_sems, recv_sems, back_sems, own_sems):
    plane = Plane(n_col, out, send_sems, recv_sems)
    depth = plane.depth
    greet(plane.partners)
    keeps = [
        pltpu.make_async_copy(own, out.at[0], own_sems.at[0]),
        pltpu.make_async_copy(own.at[0], back.at[plane.z], own_sems.at[1]),
    ]
    for keep in keeps:
        keep.start()
    greeted(plane.partners)
    steps = (0, depth)
    plane.first_hop(0, steps, own)
    for step in range(1, depth):
        plane.launch(own.at[depth - step], back.at[plane.z], back_sems.at[step], plane.over_z(step))
    plane.second_hop(0, steps)
    plane.last_hop(0, steps)
    for step in range(1, depth):
        spot = back.at[plane.level(step)]
        pltpu.make_async_copy(spot, spot, back_sems.at[step]).wait()
    for keep in keeps:
        keep.wait()
    plane.finish([steps])


def finish_kernel(n_col, own, back, targets, total, once, twice,
                  land, line, wide, send_sems, recv_sems, line_sends, line_recvs, wide_sends, wide_recvs):
    y, core, z, x = place()
    depth = n_col // 2

    def level(step):
        return lax.rem(z + step, depth)

    column = [device(y, core, level(depth - step), x) for step in range(1, depth)]
    flips = [(a, b, c) for a in range(2) for b in range(2) for c in range(2)][1:]
    plane = [
        device(1 - y if a else y, 1 - core if b else core, z, 1 - x if c else x) for a, b, c in flips
    ]
    greet(column + plane)
    rhs = targets.shape[1]
    target = targets[...]
    image = back[...].reshape(rhs, TILE).astype(jnp.float32).T
    once[...] = image

    def column_sum(value):
        return jnp.sum(value, axis=0, keepdims=True)

    line[0, 0:1, :] = column_sum(target * target)
    line[0, 1:2, :] = column_sum(target * image)
    line[0, 2:3, :] = column_sum(image * image)
    line[0, 5:8, :] = jnp.zeros((3, rhs), jnp.float32)
    greeted(column + plane)

    def remote(source, spot, send_sem, recv_sem, target):
        copy = pltpu.make_async_remote_copy(
            src_ref=source, dst_ref=spot, send_sem=send_sem, recv_sem=recv_sem,
            device_id=target, device_id_type=MESH,
        )
        copy.start()
        return copy

    copies = [
        remote(own.at[depth - step], land.at[z], send_sems.at[step], recv_sems.at[step], column[step - 1])
        for step in range(1, depth)
    ]
    land[z] = own[0]
    for copy in copies:
        copy.wait()
    again = land[...].reshape(rhs, TILE).astype(jnp.float32).T
    twice[...] = again
    line[0, 3:4, :] = column_sum(target * again)
    line[0, 4:5, :] = column_sum(image * again)
    copies = [
        remote(line.at[0], line.at[step], line_sends.at[step], line_recvs.at[step], column[step - 1])
        for step in range(1, depth)
    ]
    for copy in copies:
        copy.wait()
    wide[0] = jnp.sum(line[...], axis=0)
    copies = [
        remote(wide.at[0], wide.at[step + 1], wide_sends.at[step], wide_recvs.at[step], peer)
        for step, peer in enumerate(plane)
    ]
    for copy in copies:
        copy.wait()
    total[...] = jnp.sum(wide[...], axis=0)


def find_tiles(n_col, groups, order):
    y, core, z, x = place()
    depth = n_col // 2

    def label(peer, step):
        other_y = lax.rem(y + peer // 4, 2)
        other_core = lax.rem(core + peer // 2 % 2, 2)
        other_x = lax.rem(x + peer % 2, 2)
        return groups[(2 * other_y + other_core) * n_col + 2 * lax.rem(z + step, depth) + other_x]

    labels = [label(peer, step) for peer in range(8) for step in range(depth)]
    count = jnp.int32(0)
    for level in range(depth):
        for block, other in enumerate(labels):
            if block == level:
                continue
            order[count] = block * depth + level
            count = count + (other == labels[level]).astype(jnp.int32)
    return count


def lift_rows(n_col, width, gathered, right):
    dims = gathered.shape[1] - width
    for level in range(n_col // 2):
        right[level] = lifted(gathered[level, pl.ds(width, dims), :], 1.0, 0, 3)


def build(width, gathered, block, level, left, right, spot):
    dims = gathered.shape[1] - width
    left[...] = lifted(gathered[block, pl.ds(width, dims), :], -2.0, 3, 0).T
    for start in range(0, TILE, CHUNK):
        rows = pl.ds(start, CHUNK)
        squared = jnp.dot(left[rows, :], right[level], preferred_element_type=jnp.float32)
        spot[rows, :] = wendland(squared)


def spot_of(depth, order, slot):
    return order[slot] // depth, lax.rem(order[slot], depth)


def first_kernel(n_col, groups, gathered, diagonal, tiles, narrow, order, left, right, spare, image):
    width = narrow.shape[1]
    depth, kept = n_col // 2, tiles.shape[0]
    total = find_tiles(n_col, groups, order)
    stored = jnp.minimum(total, kept)
    lift_rows(n_col, width, gathered, right)
    for level in range(depth):
        image[level] = jnp.dot(
            gathered[level, pl.ds(0, width), :], diagonal[level], preferred_element_type=jnp.float32
        )

    def one_tile(slot, carry):
        block, level = spot_of(depth, order, slot)
        build(width, gathered, block, level, left, right, tiles.at[slot])
        return carry

    def multiply(slot, tile):
        block, level = spot_of(depth, order, slot)
        image[level] += jnp.dot(
            gathered[block, pl.ds(0, width), :], tile[...], preferred_element_type=jnp.float32
        )

    def one_stored(slot, carry):
        multiply(slot, tiles.at[slot])
        return carry

    def one_more(slot, carry):
        block, level = spot_of(depth, order, slot)
        build(width, gathered, block, level, left, right, spare)
        multiply(slot, spare)
        return carry

    lax.fori_loop(0, stored, one_tile, 0)
    lax.fori_loop(0, stored, one_stored, 0)
    lax.fori_loop(stored, total, one_more, 0)
    narrow[...] = image[...].astype(jnp.bfloat16)


def second_kernel(n_col, groups, gathered, diagonal, source, tiles, narrow, order, left, right, spare, image):
    width = narrow.shape[1]
    depth, kept = n_col // 2, tiles.shape[0]
    total = find_tiles(n_col, groups, order)
    stored = jnp.minimum(total, kept)
    for level in range(depth):
        image[level] = jnp.dot(source[level], diagonal[level], preferred_element_type=jnp.float32)

    def multiply(slot, tile):
        block, level = spot_of(depth, order, slot)
        image[level] += jnp.dot(source[block], tile[...], preferred_element_type=jnp.float32)

    def one_stored(slot, carry):
        multiply(slot, tiles.at[slot])
        return carry

    lax.fori_loop(0, stored, one_stored, 0)

    @pl.when(total > kept)
    def _():
        lift_rows(n_col, width, gathered, right)

    def one_more(slot, carry):
        block, level = spot_of(depth, order, slot)
        build(width, gathered, block, level, left, right, spare)
        multiply(slot, spare)
        return carry

    lax.fori_loop(stored, total, one_more, 0)
    narrow[...] = image[...].astype(jnp.bfloat16)


def gathered_plan(points, lengthscale, noise_var, groups, targets):
    n_col = lax.axis_size("col")
    depth = n_col // 2
    blocks = groups.shape[0]
    dims = points.shape[0]
    rhs = targets.shape[1]
    width = rhs // depth
    scale = lengthscale[None, :]
    variance = noise_var[None, :]
    parts = len(level_groups(depth))

    vmem = pl.BlockSpec(memory_space=pltpu.VMEM)
    smem = pl.BlockSpec(memory_space=pltpu.SMEM)
    slices = jax.ShapeDtypeStruct((depth, width, TILE), jnp.bfloat16)
    whole = jax.ShapeDtypeStruct((TILE, rhs), jnp.float32)

    def remote(number):
        return pltpu.CompilerParams(
            collective_id=number, has_side_effects=True, vmem_limit_bytes=VMEM_LIMIT
        )

    gathered, diagonal = pl.pallas_call(
        functools.partial(first_gather, n_col),
        out_shape=[
            jax.ShapeDtypeStruct((8, depth, width + dims, TILE), jnp.bfloat16),
            jax.ShapeDtypeStruct((depth, TILE, TILE), jnp.bfloat16),
        ],
        in_specs=[vmem, vmem, vmem],
        out_specs=[vmem, vmem],
        scratch_shapes=[
            pltpu.VMEM((depth, width + dims, TILE), jnp.bfloat16),
            pltpu.SemaphoreType.DMA((depth - 1 + 14 * parts,)),
            pltpu.SemaphoreType.DMA((parts, 8, 2)),
            pltpu.SemaphoreType.DMA((depth,)),
            pltpu.SemaphoreType.DMA,
        ],
        compiler_params=remote(0),
        name="first_gather",
    )(points, scale, targets)
    gathered = gathered.reshape(blocks, width + dims, TILE)

    work = [
        pltpu.SMEM((depth * blocks,), jnp.int32),
        pltpu.VMEM((TILE, 2 * dims), jnp.bfloat16),
        pltpu.VMEM((depth, 2 * dims, TILE), jnp.bfloat16),
        pltpu.VMEM((TILE, TILE), jnp.bfloat16),
        pltpu.VMEM((depth, width, TILE), jnp.float32),
    ]
    tiles, first = pl.pallas_call(
        functools.partial(first_kernel, n_col),
        out_shape=[jax.ShapeDtypeStruct((KEPT, TILE, TILE), jnp.bfloat16), slices],
        in_specs=[smem, vmem, vmem],
        out_specs=[vmem, vmem],
        scratch_shapes=work,
        compiler_params=pltpu.CompilerParams(vmem_limit_bytes=VMEM_LIMIT),
        name="first_product",
    )(groups, gathered, diagonal)

    source, back = pl.pallas_call(
        functools.partial(second_gather, n_col),
        out_shape=[jax.ShapeDtypeStruct((8, depth, width, TILE), jnp.bfloat16), slices],
        in_specs=[vmem],
        out_specs=[vmem, vmem],
        scratch_shapes=[
            pltpu.SemaphoreType.DMA((depth - 1 + 14,)),
            pltpu.SemaphoreType.DMA((1, 8, 2)),
            pltpu.SemaphoreType.DMA((depth,)),
            pltpu.SemaphoreType.DMA((2,)),
        ],
        compiler_params=remote(1),
        name="second_gather",
    )(first)

    second = pl.pallas_call(
        functools.partial(second_kernel, n_col),
        out_shape=slices,
        in_specs=[smem, vmem, vmem, vmem, vmem],
        out_specs=vmem,
        scratch_shapes=work,
        compiler_params=pltpu.CompilerParams(vmem_limit_bytes=VMEM_LIMIT),
        name="second_product",
    )(groups, gathered, diagonal, source.reshape(blocks, width, TILE), tiles)

    total, image, again = pl.pallas_call(
        functools.partial(finish_kernel, n_col),
        out_shape=[jax.ShapeDtypeStruct((8, rhs), jnp.float32), whole, whole],
        in_specs=[vmem, vmem, vmem],
        out_specs=[vmem, vmem, vmem],
        scratch_shapes=[
            pltpu.VMEM((depth, width, TILE), jnp.bfloat16),
            pltpu.VMEM((depth, 8, rhs), jnp.float32),
            pltpu.VMEM((8, 8, rhs), jnp.float32),
        ]
        + [pltpu.SemaphoreType.DMA((depth,))] * 4
        + [pltpu.SemaphoreType.DMA((8,))] * 2,
        compiler_params=remote(2),
        name="finish",
    )(second, back, targets)

    tt, ty, yy, tz, yz = (total[place:place + 1] for place in range(5))
    step = tt / (variance * tt + ty)
    keep = 1.0 - step * variance
    after = keep * keep * tt - 2.0 * keep * step * ty + step * step * yy
    along = keep + after / tt
    squares = along * along * tt - 2.0 * along * step * ty + step * step * yy
    product = along * along * ty - along * step * (tz + yy) + step * step * yz
    second_step = after / (variance * squares + product)
    direction = along * targets - step * image
    applied = variance * direction + along * image - step * again
    solution_field = step * targets + second_step * direction
    residual = keep * targets - step * image - second_step * applied
    return (solution_field, residual)


def kernel_tile(row_coords, col_coords):
    row_norms = jnp.sum(row_coords * row_coords, axis=0)
    col_norms = jnp.sum(col_coords * col_coords, axis=0)
    crossed = lax.dot_general(
        row_coords,
        col_coords,
        (((0,), (0,)), ((), ())),
        precision=lax.Precision.HIGHEST,
        preferred_element_type=jnp.float32,
    )
    squared = jnp.maximum(row_norms[:, None] + col_norms[None, :] - 2.0 * crossed, 0.0)
    radius = jnp.sqrt(squared)
    support = jnp.maximum(1.0 - radius, 0.0)
    return (support**11 * (11.0 * radius + 1.0)).astype(jnp.bfloat16)


def per_device(points, lengthscale, noise_var, groups, targets):
    n_row = lax.axis_size("row")
    n_col = lax.axis_size("col")
    own_blocks = targets.shape[0] // TILE
    row_blocks = own_blocks * n_col
    col_blocks = own_blocks * n_row
    scaled = points / lengthscale[:, None]
    row_coords = lax.all_gather(scaled.astype(jnp.bfloat16), "col", axis=1, tiled=True).astype(
        scaled.dtype
    )
    col_coords = lax.all_gather(scaled.astype(jnp.bfloat16), "row", axis=1, tiled=True).astype(
        scaled.dtype
    )
    row_place = lax.axis_index("row")
    col_place = lax.axis_index("col")
    row_groups = lax.dynamic_slice_in_dim(groups, row_place * row_blocks, row_blocks, 0)
    col_groups = lax.dynamic_index_in_dim(
        groups.reshape(n_row, n_col, own_blocks), col_place, 1, keepdims=False
    ).reshape(col_blocks)
    flat_mask = (row_groups[:, None] == col_groups[None, :]).reshape(row_blocks * col_blocks)
    tile_count = jnp.sum(flat_mask.astype(jnp.int32))
    tile_order = jnp.nonzero(flat_mask, size=row_blocks * col_blocks, fill_value=0)[0].astype(
        jnp.int32
    )

    def square_sums(vector):
        return lax.psum(jnp.sum(vector * vector, axis=0), ("row", "col"))

    solution_field = jnp.zeros_like(targets)
    residual = targets
    direction = targets
    norm_now = square_sums(residual)
    for iteration in range(ITERS):
        narrow = direction.astype(jnp.bfloat16)
        operator_source = lax.all_gather(narrow, "row", axis=0, tiled=True)
        source = operator_source
        initial = jnp.zeros((row_blocks * TILE, RHS), jnp.float32)

        def one_tile(position, summed):
            flat_index = tile_order[position]
            row_slot = flat_index // col_blocks
            col_slot = flat_index % col_blocks
            left = lax.dynamic_slice_in_dim(row_coords, row_slot * TILE, TILE, 1)
            right = lax.dynamic_slice_in_dim(col_coords, col_slot * TILE, TILE, 1)
            values = kernel_tile(left, right)
            block_vec = lax.dynamic_slice_in_dim(source, col_slot * TILE, TILE, 0)
            product = jnp.dot(values, block_vec, preferred_element_type=jnp.float32)
            current = lax.dynamic_slice_in_dim(summed, row_slot * TILE, TILE, 0)
            return lax.dynamic_update_slice_in_dim(summed, current + product, row_slot * TILE, 0)

        partial_value = lax.fori_loop(0, tile_count, one_tile, initial)
        outgoing = partial_value.astype(jnp.bfloat16).reshape(n_col, own_blocks * TILE, RHS)
        incoming = lax.all_to_all(outgoing, "col", split_axis=0, concat_axis=0, tiled=True)
        operator_product = jnp.sum(incoming, axis=0, dtype=jnp.float32)
        image = noise_var[None, :] * direction + operator_product
        curve = lax.psum(jnp.sum(direction * image, axis=0), ("row", "col"))
        step_size = norm_now / curve
        solution_field = solution_field + step_size[None, :] * direction
        residual = residual - step_size[None, :] * image
        if iteration + 1 < ITERS:
            norm_next = square_sums(residual)
            direction = residual + (norm_next / norm_now)[None, :] * direction
            norm_now = norm_next
    return (solution_field, residual)


def solution(mesh):
    placed = (P(None, ("row", "col")), P(), P(), P(), P(("row", "col"), None))

    def plan(points, lengthscale, noise_var, groups, targets):
        blocks = groups.shape[0]
        square = mesh.shape["row"] == 4 and mesh.shape["col"] in (2, 4, 8, 16)
        whole_field = blocks <= GATHER_LIMIT and blocks == mesh.size and square
        run = gathered_plan if whole_field else per_device
        return run(points, lengthscale, noise_var, groups, targets)

    return jax.shard_map(
        plan,
        mesh=mesh,
        in_specs=placed,
        out_specs=(P(("row", "col"), None), P(("row", "col"), None)),
        check_vma=False,
    )
```

```python
import functools

import functools

import jax
import jax.numpy as jnp
from jax import lax
from jax.experimental import pallas as pl
from jax.experimental.pallas import tpu as pltpu
from jax.sharding import PartitionSpec as P

TILE = 512
ITERS = 2
RHS = 128
CHUNK = 128
GATHER_LIMIT = 64
KEPT = 32
VMEM_LIMIT = 24 * 1024 * 1024
MESH = pl.DeviceIdType.MESH


def split3(value):
    first = value.astype(jnp.bfloat16).astype(jnp.float32)
    rest = value - first
    second = rest.astype(jnp.bfloat16).astype(jnp.float32)
    return first, second, rest - second


def lifted(coords, factor, norm_at, one_at):
    wide = coords.astype(jnp.float32)
    parts = split3(jnp.sum(wide * wide, axis=0, keepdims=True))
    row = lax.broadcasted_iota(jnp.int32, wide.shape, 0)
    tail = jnp.where((row >= one_at) & (row < one_at + 3), 1.0, 0.0)
    for place, part in enumerate(parts):
        tail = jnp.where(row == norm_at + place, part, tail)
    return jnp.concatenate([wide * factor, tail], axis=0).astype(jnp.bfloat16)


def wendland(squared):
    safe = jnp.maximum(squared, 1e-30)
    radius = safe * lax.rsqrt(safe)
    support = jnp.maximum(1.0 - radius, 0.0)
    second = support * support
    third = second * support
    fourth = second * second
    eighth = fourth * fourth
    return ((eighth * third) * (12.0 - 11.0 * support)).astype(jnp.bfloat16)


def place():
    row, col = lax.axis_index("row"), lax.axis_index("col")
    return row // 2, lax.rem(row, 2), col // 2, lax.rem(col, 2)


def device(y, core, z, x):
    return (2 * y + core, 2 * z + x)


def greet(targets):
    barrier = pltpu.get_barrier_semaphore()
    for target in targets:
        pl.semaphore_signal(barrier, inc=1, device_id=target, device_id_type=MESH)


def greeted(targets):
    pl.semaphore_wait(pltpu.get_barrier_semaphore(), len(targets))


class Plane:
    def __init__(self, n_col, out, send_sems, recv_sems):
        self.out, self.send_sems, self.recv_sems = out, send_sems, recv_sems
        self.y, self.core, self.z, self.x = place()
        self.depth = n_col // 2
        self.started = []
        y, core, z, x = self.y, self.core, self.z, self.x
        self.over_x, self.over_y = device(y, core, z, 1 - x), device(1 - y, core, z, x)
        self.over_core = device(y, 1 - core, z, x)
        self.partners = [self.over_x, self.over_y, self.over_core]
        self.partners += [self.over_z(step) for step in range(1, self.depth)]

    def level(self, step):
        return lax.rem(self.z + step, self.depth)

    def over_z(self, step):
        return device(self.y, self.core, self.level(self.depth - step), self.x)

    def launch(self, source, spot, recv_sem, target):
        copy = pltpu.make_async_remote_copy(
            src_ref=source,
            dst_ref=spot,
            send_sem=self.send_sems.at[len(self.started)],
            recv_sem=recv_sem,
            device_id=target,
            device_id_type=MESH,
        )
        copy.start()
        self.started.append(copy)

    def half(self, ref, part):
        lanes = TILE // 2
        return ref.at[:, :, pl.ds(part * lanes, lanes)]

    def spot(self, peer, steps, part):
        return self.half(self.out.at[peer, pl.ds(steps[0], steps[1])], part)

    def send(self, group, steps, peer, part, target, flip, own=None):
        source = self.spot(peer, steps, part) if own is None else self.half(own, part)
        there = peer + flip
        self.launch(source, self.spot(there, steps, part), self.recv_sems.at[group, there, part], target)

    def arrived(self, group, steps, peer, part):
        spot = self.spot(peer, steps, part)
        pltpu.make_async_copy(spot, spot, self.recv_sems.at[group, peer, part]).wait()

    def first_hop(self, group, steps, own=None):
        self.send(group, steps, 0, 0, self.over_x, 1, own)
        self.send(group, steps, 0, 1, self.over_y, 4, own)
        self.send(group, steps, 0, 1, self.over_x, 1, own)
        self.send(group, steps, 0, 0, self.over_y, 4, own)
        self.send(group, steps, 0, 0, self.over_core, 2, own)
        self.send(group, steps, 0, 1, self.over_core, 2, own)

    def second_hop(self, group, steps):
        self.arrived(group, steps, 1, 0)
        self.send(group, steps, 1, 0, self.over_y, 4)
        self.arrived(group, steps, 4, 1)
        self.send(group, steps, 4, 1, self.over_x, 1)
        self.send(group, steps, 1, 0, self.over_core, 2)
        self.send(group, steps, 4, 1, self.over_core, 2)

    def last_hop(self, group, steps):
        for peer, part in ((1, 1), (4, 0), (5, 0), (5, 1)):
            self.arrived(group, steps, peer, part)
            self.send(group, steps, peer, part, self.over_core, 2)

    def finish(self, groups):
        for group, steps in enumerate(groups):
            for peer in (2, 3, 6, 7):
                self.arrived(group, steps, peer, 0)
                self.arrived(group, steps, peer, 1)
        for copy in self.started:
            copy.wait_send()


def level_groups(depth):
    groups = [(step, 1) for step in range(min(depth, 2))]
    return groups + ([(2, depth - 2)] if depth > 2 else [])


def build_own(coords, spot):
    left, right = lifted(coords, -2.0, 3, 0).T, lifted(coords, 1.0, 0, 3)
    for start in range(0, TILE, CHUNK):
        squared = jnp.dot(left[start:start + CHUNK, :], right, preferred_element_type=jnp.float32)
        spot[pl.ds(start, CHUNK), :] = wendland(squared)


def first_gather(n_col, points, scale, targets, out, diagonal, own, send_sems, recv_sems, z_sems, own_sem):
    plane = Plane(n_col, out, send_sems, recv_sems)
    depth, dims = plane.depth, points.shape[0]
    width = targets.shape[1] // depth
    greet(plane.partners)
    across = lax.broadcasted_iota(jnp.int32, (dims, dims), 1)
    down = lax.broadcasted_iota(jnp.int32, (dims, dims), 0)
    lengths = jnp.sum(jnp.where(across == down, scale[...], 0.0), axis=1, keepdims=True)
    scaled = (points[...] / lengths).astype(jnp.bfloat16)
    turned = targets[...].T.astype(jnp.bfloat16)
    for part in range(depth):
        own[part, 0:width, :] = turned[part * width:(part + 1) * width, :]
        own[part, width:width + dims, :] = scaled
    greeted(plane.partners)
    for step in range(1, depth):
        plane.launch(own.at[plane.level(depth - step)], out.at[0, step], z_sems.at[step], plane.over_z(step))
    groups = level_groups(depth)
    last = len(groups) - 1

    def build_group(group):
        steps = groups[group]
        for step in range(steps[0], steps[0] + steps[1]):
            build_own(scaled if step == 0 else out[0, step, pl.ds(width, dims), :], diagonal.at[step])

    for group, steps in enumerate(groups):
        if group == 0:
            mine = own.at[pl.ds(plane.z, 1)]
            plane.first_hop(0, steps, mine)
            keep = pltpu.make_async_copy(mine, out.at[0, pl.ds(0, 1)], own_sem)
            keep.start()
        else:
            for step in range(steps[0], steps[0] + steps[1]):
                spot = out.at[0, step]
                pltpu.make_async_copy(spot, spot, z_sems.at[step]).wait()
            plane.first_hop(group, steps)
            plane.second_hop(group - 1, groups[group - 1])
        if group >= 2:
            plane.last_hop(group - 2, groups[group - 2])
        if group < last:
            build_group(group)
    plane.second_hop(last, groups[last])
    build_group(last)
    for group in range(max(last - 1, 0), last + 1):
        plane.last_hop(group, groups[group])
    keep.wait()
    plane.finish(groups)


def second_gather(n_col, own, out, back, send_sems, recv_sems, back_sems, own_sems):
    plane = Plane(n_col, out, send_sems, recv_sems)
    depth = plane.depth
    greet(plane.partners)
    keeps = [
        pltpu.make_async_copy(own, out.at[0], own_sems.at[0]),
        pltpu.make_async_copy(own.at[0], back.at[plane.z], own_sems.at[1]),
    ]
    for keep in keeps:
        keep.start()
    greeted(plane.partners)
    steps = (0, depth)
    plane.first_hop(0, steps, own)
    for step in range(1, depth):
        plane.launch(own.at[depth - step], back.at[plane.z], back_sems.at[step], plane.over_z(step))
    plane.second_hop(0, steps)
    plane.last_hop(0, steps)
    for step in range(1, depth):
        spot = back.at[plane.level(step)]
        pltpu.make_async_copy(spot, spot, back_sems.at[step]).wait()
    for keep in keeps:
        keep.wait()
    plane.finish([steps])


def finish_kernel(n_col, own, back, targets, total, once, twice,
                  land, line, wide, send_sems, recv_sems, line_sends, line_recvs, wide_sends, wide_recvs):
    y, core, z, x = place()
    depth = n_col // 2

    def level(step):
        return lax.rem(z + step, depth)

    column = [device(y, core, level(depth - step), x) for step in range(1, depth)]
    flips = [(a, b, c) for a in range(2) for b in range(2) for c in range(2)][1:]
    plane = [
        device(1 - y if a else y, 1 - core if b else core, z, 1 - x if c else x) for a, b, c in flips
    ]
    greet(column + plane)
    rhs = targets.shape[1]
    target = targets[...]
    image = back[...].reshape(rhs, TILE).astype(jnp.float32).T
    once[...] = image

    def column_sum(value):
        return jnp.sum(value, axis=0, keepdims=True)

    line[0, 0:1, :] = column_sum(target * target)
    line[0, 1:2, :] = column_sum(target * image)
    line[0, 2:3, :] = column_sum(image * image)
    line[0, 5:8, :] = jnp.zeros((3, rhs), jnp.float32)
    greeted(column + plane)

    def remote(source, spot, send_sem, recv_sem, target):
        copy = pltpu.make_async_remote_copy(
            src_ref=source, dst_ref=spot, send_sem=send_sem, recv_sem=recv_sem,
            device_id=target, device_id_type=MESH,
        )
        copy.start()
        return copy

    copies = [
        remote(own.at[depth - step], land.at[z], send_sems.at[step], recv_sems.at[step], column[step - 1])
        for step in range(1, depth)
    ]
    land[z] = own[0]
    for copy in copies:
        copy.wait()
    again = land[...].reshape(rhs, TILE).astype(jnp.float32).T
    twice[...] = again
    line[0, 3:4, :] = column_sum(target * again)
    line[0, 4:5, :] = column_sum(image * again)
    copies = [
        remote(line.at[0], line.at[step], line_sends.at[step], line_recvs.at[step], column[step - 1])
        for step in range(1, depth)
    ]
    for copy in copies:
        copy.wait()
    wide[0] = jnp.sum(line[...], axis=0)
    copies = [
        remote(wide.at[0], wide.at[step + 1], wide_sends.at[step], wide_recvs.at[step], peer)
        for step, peer in enumerate(plane)
    ]
    for copy in copies:
        copy.wait()
    total[...] = jnp.sum(wide[...], axis=0)


def find_tiles(n_col, groups, order):
    y, core, z, x = place()
    depth = n_col // 2

    def label(peer, step):
        other_y = lax.rem(y + peer // 4, 2)
        other_core = lax.rem(core + peer // 2 % 2, 2)
        other_x = lax.rem(x + peer % 2, 2)
        return groups[(2 * other_y + other_core) * n_col + 2 * lax.rem(z + step, depth) + other_x]

    labels = [label(peer, step) for peer in range(8) for step in range(depth)]
    count = jnp.int32(0)
    for level in range(depth):
        for block, other in enumerate(labels):
            if block == level:
                continue
            order[count] = block * depth + level
            count = count + (other == labels[level]).astype(jnp.int32)
    return count


def lift_rows(n_col, width, gathered, right):
    dims = gathered.shape[1] - width
    for level in range(n_col // 2):
        right[level] = lifted(gathered[level, pl.ds(width, dims), :], 1.0, 0, 3)


def build(width, gathered, block, level, left, right, spot):
    dims = gathered.shape[1] - width
    left[...] = lifted(gathered[block, pl.ds(width, dims), :], -2.0, 3, 0).T
    for start in range(0, TILE, CHUNK):
        rows = pl.ds(start, CHUNK)
        squared = jnp.dot(left[rows, :], right[level], preferred_element_type=jnp.float32)
        spot[rows, :] = wendland(squared)


def spot_of(depth, order, slot):
    return order[slot] // depth, lax.rem(order[slot], depth)


def first_kernel(n_col, groups, gathered, diagonal, evens, odds, narrow, order, left, right, spare, image):
    width = narrow.shape[1]
    depth, kept = n_col // 2, 2 * evens.shape[0]
    total = find_tiles(n_col, groups, order)
    stored = jnp.minimum(total, kept)
    pairs = stored // 2
    lift_rows(n_col, width, gathered, right)
    for level in range(depth):
        image[level] = jnp.dot(
            gathered[level, pl.ds(0, width), :], diagonal[level], preferred_element_type=jnp.float32
        )

    def make(slot, tile):
        block, level = spot_of(depth, order, slot)
        build(width, gathered, block, level, left, right, tile)

    def multiply(slot, tile):
        block, level = spot_of(depth, order, slot)
        image[level] += jnp.dot(
            gathered[block, pl.ds(0, width), :], tile[...], preferred_element_type=jnp.float32
        )

    odds[0] = jnp.zeros((TILE, TILE), jnp.bfloat16)

    def one_pair(pair, carry):
        before = jnp.maximum(pair - 1, 0)
        make(2 * pair, evens.at[pair])
        multiply(jnp.maximum(2 * pair - 1, 0), odds.at[before])
        make(2 * pair + 1, odds.at[pair])
        multiply(2 * pair, evens.at[pair])
        return carry

    def single(slot, carry):
        make(slot, evens.at[pairs])
        multiply(slot, evens.at[pairs])
        return carry

    def last_odd(slot, carry):
        multiply(slot, odds.at[pairs - 1])
        return carry

    def one_more(slot, carry):
        block, level = spot_of(depth, order, slot)
        build(width, gathered, block, level, left, right, spare)
        multiply(slot, spare)
        return carry

    lax.fori_loop(0, pairs, one_pair, 0)
    lax.fori_loop(jnp.maximum(2 * pairs - 1, 0), 2 * pairs, last_odd, 0)
    lax.fori_loop(2 * pairs, stored, single, 0)
    lax.fori_loop(stored, total, one_more, 0)
    narrow[...] = image[...].astype(jnp.bfloat16)


def second_kernel(n_col, groups, gathered, diagonal, source, evens, odds, narrow, order, left, right, spare, image):
    width = narrow.shape[1]
    depth, kept = n_col // 2, 2 * evens.shape[0]
    total = find_tiles(n_col, groups, order)
    stored = jnp.minimum(total, kept)
    pairs = stored // 2
    for level in range(depth):
        image[level] = jnp.dot(source[level], diagonal[level], preferred_element_type=jnp.float32)

    def multiply(slot, tile):
        block, level = spot_of(depth, order, slot)
        image[level] += jnp.dot(source[block], tile[...], preferred_element_type=jnp.float32)

    def one_pair(pair, carry):
        multiply(2 * pair, evens.at[pair])
        multiply(2 * pair + 1, odds.at[pair])
        return carry

    def single(slot, carry):
        multiply(slot, evens.at[pairs])
        return carry

    lax.fori_loop(0, pairs, one_pair, 0)
    lax.fori_loop(2 * pairs, stored, single, 0)

    @pl.when(total > kept)
    def _():
        lift_rows(n_col, width, gathered, right)

    def one_more(slot, carry):
        block, level = spot_of(depth, order, slot)
        build(width, gathered, block, level, left, right, spare)
        multiply(slot, spare)
        return carry

    lax.fori_loop(stored, total, one_more, 0)
    narrow[...] = image[...].astype(jnp.bfloat16)


def gathered_plan(points, lengthscale, noise_var, groups, targets):
    n_col = lax.axis_size("col")
    depth = n_col // 2
    blocks = groups.shape[0]
    dims = points.shape[0]
    rhs = targets.shape[1]
    width = rhs // depth
    scale = lengthscale[None, :]
    variance = noise_var[None, :]
    parts = len(level_groups(depth))

    vmem = pl.BlockSpec(memory_space=pltpu.VMEM)
    smem = pl.BlockSpec(memory_space=pltpu.SMEM)
    slices = jax.ShapeDtypeStruct((depth, width, TILE), jnp.bfloat16)
    whole = jax.ShapeDtypeStruct((TILE, rhs), jnp.float32)

    def remote(number):
        return pltpu.CompilerParams(
            collective_id=number, has_side_effects=True, vmem_limit_bytes=VMEM_LIMIT
        )

    gathered, diagonal = pl.pallas_call(
        functools.partial(first_gather, n_col),
        out_shape=[
            jax.ShapeDtypeStruct((8, depth, width + dims, TILE), jnp.bfloat16),
            jax.ShapeDtypeStruct((depth, TILE, TILE), jnp.bfloat16),
        ],
        in_specs=[vmem, vmem, vmem],
        out_specs=[vmem, vmem],
        scratch_shapes=[
            pltpu.VMEM((depth, width + dims, TILE), jnp.bfloat16),
            pltpu.SemaphoreType.DMA((depth - 1 + 14 * parts,)),
            pltpu.SemaphoreType.DMA((parts, 8, 2)),
            pltpu.SemaphoreType.DMA((depth,)),
            pltpu.SemaphoreType.DMA,
        ],
        compiler_params=remote(0),
        name="first_gather",
    )(points, scale, targets)
    gathered = gathered.reshape(blocks, width + dims, TILE)

    work = [
        pltpu.SMEM((depth * blocks,), jnp.int32),
        pltpu.VMEM((TILE, 2 * dims), jnp.bfloat16),
        pltpu.VMEM((depth, 2 * dims, TILE), jnp.bfloat16),
        pltpu.VMEM((TILE, TILE), jnp.bfloat16),
        pltpu.VMEM((depth, width, TILE), jnp.float32),
    ]
    evens, odds, first = pl.pallas_call(
        functools.partial(first_kernel, n_col),
        out_shape=[jax.ShapeDtypeStruct((KEPT // 2, TILE, TILE), jnp.bfloat16)] * 2 + [slices],
        in_specs=[smem, vmem, vmem],
        out_specs=[vmem, vmem, vmem],
        scratch_shapes=work,
        compiler_params=pltpu.CompilerParams(vmem_limit_bytes=VMEM_LIMIT),
        name="first_product",
    )(groups, gathered, diagonal)

    source, back = pl.pallas_call(
        functools.partial(second_gather, n_col),
        out_shape=[jax.ShapeDtypeStruct((8, depth, width, TILE), jnp.bfloat16), slices],
        in_specs=[vmem],
        out_specs=[vmem, vmem],
        scratch_shapes=[
            pltpu.SemaphoreType.DMA((depth - 1 + 14,)),
            pltpu.SemaphoreType.DMA((1, 8, 2)),
            pltpu.SemaphoreType.DMA((depth,)),
            pltpu.SemaphoreType.DMA((2,)),
        ],
        compiler_params=remote(1),
        name="second_gather",
    )(first)

    second = pl.pallas_call(
        functools.partial(second_kernel, n_col),
        out_shape=slices,
        in_specs=[smem, vmem, vmem, vmem, vmem, vmem],
        out_specs=vmem,
        scratch_shapes=work,
        compiler_params=pltpu.CompilerParams(vmem_limit_bytes=VMEM_LIMIT),
        name="second_product",
    )(groups, gathered, diagonal, source.reshape(blocks, width, TILE), evens, odds)

    total, image, again = pl.pallas_call(
        functools.partial(finish_kernel, n_col),
        out_shape=[jax.ShapeDtypeStruct((8, rhs), jnp.float32), whole, whole],
        in_specs=[vmem, vmem, vmem],
        out_specs=[vmem, vmem, vmem],
        scratch_shapes=[
            pltpu.VMEM((depth, width, TILE), jnp.bfloat16),
            pltpu.VMEM((depth, 8, rhs), jnp.float32),
            pltpu.VMEM((8, 8, rhs), jnp.float32),
        ]
        + [pltpu.SemaphoreType.DMA((depth,))] * 4
        + [pltpu.SemaphoreType.DMA((8,))] * 2,
        compiler_params=remote(2),
        name="finish",
    )(second, back, targets)

    tt, ty, yy, tz, yz = (total[place:place + 1] for place in range(5))
    step = tt / (variance * tt + ty)
    keep = 1.0 - step * variance
    after = keep * keep * tt - 2.0 * keep * step * ty + step * step * yy
    along = keep + after / tt
    squares = along * along * tt - 2.0 * along * step * ty + step * step * yy
    product = along * along * ty - along * step * (tz + yy) + step * step * yz
    second_step = after / (variance * squares + product)
    direction = along * targets - step * image
    applied = variance * direction + along * image - step * again
    solution_field = step * targets + second_step * direction
    residual = keep * targets - step * image - second_step * applied
    return (solution_field, residual)


def kernel_tile(row_coords, col_coords):
    row_norms = jnp.sum(row_coords * row_coords, axis=0)
    col_norms = jnp.sum(col_coords * col_coords, axis=0)
    crossed = lax.dot_general(
        row_coords,
        col_coords,
        (((0,), (0,)), ((), ())),
        precision=lax.Precision.HIGHEST,
        preferred_element_type=jnp.float32,
    )
    squared = jnp.maximum(row_norms[:, None] + col_norms[None, :] - 2.0 * crossed, 0.0)
    radius = jnp.sqrt(squared)
    support = jnp.maximum(1.0 - radius, 0.0)
    return (support**11 * (11.0 * radius + 1.0)).astype(jnp.bfloat16)


def per_device(points, lengthscale, noise_var, groups, targets):
    n_row = lax.axis_size("row")
    n_col = lax.axis_size("col")
    own_blocks = targets.shape[0] // TILE
    row_blocks = own_blocks * n_col
    col_blocks = own_blocks * n_row
    scaled = points / lengthscale[:, None]
    row_coords = lax.all_gather(scaled.astype(jnp.bfloat16), "col", axis=1, tiled=True).astype(
        scaled.dtype
    )
    col_coords = lax.all_gather(scaled.astype(jnp.bfloat16), "row", axis=1, tiled=True).astype(
        scaled.dtype
    )
    row_place = lax.axis_index("row")
    col_place = lax.axis_index("col")
    row_groups = lax.dynamic_slice_in_dim(groups, row_place * row_blocks, row_blocks, 0)
    col_groups = lax.dynamic_index_in_dim(
        groups.reshape(n_row, n_col, own_blocks), col_place, 1, keepdims=False
    ).reshape(col_blocks)
    flat_mask = (row_groups[:, None] == col_groups[None, :]).reshape(row_blocks * col_blocks)
    tile_count = jnp.sum(flat_mask.astype(jnp.int32))
    tile_order = jnp.nonzero(flat_mask, size=row_blocks * col_blocks, fill_value=0)[0].astype(
        jnp.int32
    )

    def square_sums(vector):
        return lax.psum(jnp.sum(vector * vector, axis=0), ("row", "col"))

    solution_field = jnp.zeros_like(targets)
    residual = targets
    direction = targets
    norm_now = square_sums(residual)
    for iteration in range(ITERS):
        narrow = direction.astype(jnp.bfloat16)
        operator_source = lax.all_gather(narrow, "row", axis=0, tiled=True)
        source = operator_source
        initial = jnp.zeros((row_blocks * TILE, RHS), jnp.float32)

        def one_tile(position, summed):
            flat_index = tile_order[position]
            row_slot = flat_index // col_blocks
            col_slot = flat_index % col_blocks
            left = lax.dynamic_slice_in_dim(row_coords, row_slot * TILE, TILE, 1)
            right = lax.dynamic_slice_in_dim(col_coords, col_slot * TILE, TILE, 1)
            values = kernel_tile(left, right)
            block_vec = lax.dynamic_slice_in_dim(source, col_slot * TILE, TILE, 0)
            product = jnp.dot(values, block_vec, preferred_element_type=jnp.float32)
            current = lax.dynamic_slice_in_dim(summed, row_slot * TILE, TILE, 0)
            return lax.dynamic_update_slice_in_dim(summed, current + product, row_slot * TILE, 0)

        partial_value = lax.fori_loop(0, tile_count, one_tile, initial)
        outgoing = partial_value.astype(jnp.bfloat16).reshape(n_col, own_blocks * TILE, RHS)
        incoming = lax.all_to_all(outgoing, "col", split_axis=0, concat_axis=0, tiled=True)
        operator_product = jnp.sum(incoming, axis=0, dtype=jnp.float32)
        image = noise_var[None, :] * direction + operator_product
        curve = lax.psum(jnp.sum(direction * image, axis=0), ("row", "col"))
        step_size = norm_now / curve
        solution_field = solution_field + step_size[None, :] * direction
        residual = residual - step_size[None, :] * image
        if iteration + 1 < ITERS:
            norm_next = square_sums(residual)
            direction = residual + (norm_next / norm_now)[None, :] * direction
            norm_now = norm_next
    return (solution_field, residual)


def solution(mesh):
    placed = (P(None, ("row", "col")), P(), P(), P(), P(("row", "col"), None))

    def plan(points, lengthscale, noise_var, groups, targets):
        blocks = groups.shape[0]
        square = mesh.shape["row"] == 4 and mesh.shape["col"] in (2, 4, 8, 16)
        whole_field = blocks <= GATHER_LIMIT and blocks == mesh.size and square
        run = gathered_plan if whole_field else per_device
        return run(points, lengthscale, noise_var, groups, targets)

    return jax.shard_map(
        plan,
        mesh=mesh,
        in_specs=placed,
        out_specs=(P(("row", "col"), None), P(("row", "col"), None)),
        check_vma=False,
    )
```

```python
import functools

import functools

import jax
import jax.numpy as jnp
from jax import lax
from jax.experimental import pallas as pl
from jax.experimental.pallas import tpu as pltpu
from jax.sharding import PartitionSpec as P

TILE = 512
ITERS = 2
RHS = 128
CHUNK = 128
GATHER_LIMIT = 64
KEPT = 32
VMEM_LIMIT = 24 * 1024 * 1024
MESH = pl.DeviceIdType.MESH


def split3(value):
    first = value.astype(jnp.bfloat16).astype(jnp.float32)
    rest = value - first
    second = rest.astype(jnp.bfloat16).astype(jnp.float32)
    return first, second, rest - second


def lifted(coords, factor, norm_at, one_at):
    wide = coords.astype(jnp.float32)
    parts = split3(jnp.sum(wide * wide, axis=0, keepdims=True))
    row = lax.broadcasted_iota(jnp.int32, wide.shape, 0)
    tail = jnp.where((row >= one_at) & (row < one_at + 3), 1.0, 0.0)
    for place, part in enumerate(parts):
        tail = jnp.where(row == norm_at + place, part, tail)
    return jnp.concatenate([wide * factor, tail], axis=0).astype(jnp.bfloat16)


def wendland(squared):
    safe = jnp.maximum(squared, 1e-30)
    radius = safe * lax.rsqrt(safe)
    support = jnp.maximum(1.0 - radius, 0.0)
    second = support * support
    third = second * support
    fourth = second * second
    eighth = fourth * fourth
    return ((eighth * third) * (12.0 - 11.0 * support)).astype(jnp.bfloat16)


def place():
    row, col = lax.axis_index("row"), lax.axis_index("col")
    return row // 2, lax.rem(row, 2), col // 2, lax.rem(col, 2)


def device(y, core, z, x):
    return (2 * y + core, 2 * z + x)


def greet(targets):
    barrier = pltpu.get_barrier_semaphore()
    for target in targets:
        pl.semaphore_signal(barrier, inc=1, device_id=target, device_id_type=MESH)


def greeted(targets):
    pl.semaphore_wait(pltpu.get_barrier_semaphore(), len(targets))


class Plane:
    def __init__(self, n_col, out, send_sems, recv_sems):
        self.out, self.send_sems, self.recv_sems = out, send_sems, recv_sems
        self.y, self.core, self.z, self.x = place()
        self.depth = n_col // 2
        self.started = []
        y, core, z, x = self.y, self.core, self.z, self.x
        self.over_x, self.over_y = device(y, core, z, 1 - x), device(1 - y, core, z, x)
        self.over_core = device(y, 1 - core, z, x)
        self.partners = [self.over_x, self.over_y, self.over_core]
        self.partners += [self.over_z(step) for step in range(1, self.depth)]

    def level(self, step):
        return lax.rem(self.z + step, self.depth)

    def over_z(self, step):
        return device(self.y, self.core, self.level(self.depth - step), self.x)

    def launch(self, source, spot, recv_sem, target):
        copy = pltpu.make_async_remote_copy(
            src_ref=source,
            dst_ref=spot,
            send_sem=self.send_sems.at[len(self.started)],
            recv_sem=recv_sem,
            device_id=target,
            device_id_type=MESH,
        )
        copy.start()
        self.started.append(copy)

    def half(self, ref, part):
        lanes = TILE // 2
        return ref.at[:, :, pl.ds(part * lanes, lanes)]

    def spot(self, peer, steps, part):
        return self.half(self.out.at[peer, pl.ds(steps[0], steps[1])], part)

    def send(self, group, steps, peer, part, target, flip, own=None):
        source = self.spot(peer, steps, part) if own is None else self.half(own, part)
        there = peer + flip
        self.launch(source, self.spot(there, steps, part), self.recv_sems.at[group, there, part], target)

    def arrived(self, group, steps, peer, part):
        spot = self.spot(peer, steps, part)
        pltpu.make_async_copy(spot, spot, self.recv_sems.at[group, peer, part]).wait()

    def first_hop(self, group, steps, own=None):
        self.send(group, steps, 0, 0, self.over_x, 1, own)
        self.send(group, steps, 0, 1, self.over_y, 4, own)
        self.send(group, steps, 0, 1, self.over_x, 1, own)
        self.send(group, steps, 0, 0, self.over_y, 4, own)
        self.send(group, steps, 0, 0, self.over_core, 2, own)
        self.send(group, steps, 0, 1, self.over_core, 2, own)

    def second_hop(self, group, steps):
        self.arrived(group, steps, 1, 0)
        self.send(group, steps, 1, 0, self.over_y, 4)
        self.arrived(group, steps, 4, 1)
        self.send(group, steps, 4, 1, self.over_x, 1)
        self.send(group, steps, 1, 0, self.over_core, 2)
        self.send(group, steps, 4, 1, self.over_core, 2)

    def last_hop(self, group, steps):
        for peer, part in ((1, 1), (4, 0), (5, 0), (5, 1)):
            self.arrived(group, steps, peer, part)
            self.send(group, steps, peer, part, self.over_core, 2)

    def finish(self, groups):
        for group, steps in enumerate(groups):
            for peer in (2, 3, 6, 7):
                self.arrived(group, steps, peer, 0)
                self.arrived(group, steps, peer, 1)
        for copy in self.started:
            copy.wait_send()


def level_groups(depth):
    groups = [(step, 1) for step in range(min(depth, 2))]
    return groups + ([(2, depth - 2)] if depth > 2 else [])


def build_own(coords, spot):
    left, right = lifted(coords, -2.0, 3, 0).T, lifted(coords, 1.0, 0, 3)
    for start in range(0, TILE, CHUNK):
        squared = jnp.dot(left[start:start + CHUNK, :], right, preferred_element_type=jnp.float32)
        spot[pl.ds(start, CHUNK), :] = wendland(squared)


def first_gather(n_col, points, scale, targets, out, diagonal, own, send_sems, recv_sems, z_sems, own_sem):
    plane = Plane(n_col, out, send_sems, recv_sems)
    depth, dims = plane.depth, points.shape[0]
    width = targets.shape[1] // depth
    greet(plane.partners)
    across = lax.broadcasted_iota(jnp.int32, (dims, dims), 1)
    down = lax.broadcasted_iota(jnp.int32, (dims, dims), 0)
    lengths = jnp.sum(jnp.where(across == down, scale[...], 0.0), axis=1, keepdims=True)
    scaled = (points[...] / lengths).astype(jnp.bfloat16)
    turned = targets[...].astype(jnp.bfloat16).T
    for part in range(depth):
        own[part, 0:width, :] = turned[part * width:(part + 1) * width, :]
        own[part, width:width + dims, :] = scaled
    greeted(plane.partners)
    for step in range(1, depth):
        plane.launch(own.at[plane.level(depth - step)], out.at[0, step], z_sems.at[step], plane.over_z(step))
    groups = level_groups(depth)
    last = len(groups) - 1

    def build_group(group):
        steps = groups[group]
        for step in range(steps[0], steps[0] + steps[1]):
            build_own(scaled if step == 0 else out[0, step, pl.ds(width, dims), :], diagonal.at[step])

    for group, steps in enumerate(groups):
        if group == 0:
            mine = own.at[pl.ds(plane.z, 1)]
            plane.first_hop(0, steps, mine)
            keep = pltpu.make_async_copy(mine, out.at[0, pl.ds(0, 1)], own_sem)
            keep.start()
        else:
            for step in range(steps[0], steps[0] + steps[1]):
                spot = out.at[0, step]
                pltpu.make_async_copy(spot, spot, z_sems.at[step]).wait()
            plane.first_hop(group, steps)
            plane.second_hop(group - 1, groups[group - 1])
        if group >= 2:
            plane.last_hop(group - 2, groups[group - 2])
        if group < last:
            build_group(group)
    plane.second_hop(last, groups[last])
    build_group(last)
    for group in range(max(last - 1, 0), last + 1):
        plane.last_hop(group, groups[group])
    keep.wait()
    plane.finish(groups)


def second_gather(n_col, own, out, back, send_sems, recv_sems, back_sems, own_sems):
    plane = Plane(n_col, out, send_sems, recv_sems)
    depth = plane.depth
    greet(plane.partners)
    keeps = [
        pltpu.make_async_copy(own, out.at[0], own_sems.at[0]),
        pltpu.make_async_copy(own.at[0], back.at[plane.z], own_sems.at[1]),
    ]
    for keep in keeps:
        keep.start()
    greeted(plane.partners)
    steps = (0, depth)
    plane.first_hop(0, steps, own)
    for step in range(1, depth):
        plane.launch(own.at[depth - step], back.at[plane.z], back_sems.at[step], plane.over_z(step))
    plane.second_hop(0, steps)
    plane.last_hop(0, steps)
    for step in range(1, depth):
        spot = back.at[plane.level(step)]
        pltpu.make_async_copy(spot, spot, back_sems.at[step]).wait()
    for keep in keeps:
        keep.wait()
    plane.finish([steps])


def finish_kernel(n_col, own, back, targets, total, once, twice,
                  land, line, wide, send_sems, recv_sems, line_sends, line_recvs, wide_sends, wide_recvs):
    y, core, z, x = place()
    depth = n_col // 2

    def level(step):
        return lax.rem(z + step, depth)

    column = [device(y, core, level(depth - step), x) for step in range(1, depth)]
    flips = [(a, b, c) for a in range(2) for b in range(2) for c in range(2)][1:]
    plane = [
        device(1 - y if a else y, 1 - core if b else core, z, 1 - x if c else x) for a, b, c in flips
    ]
    greet(column + plane)
    rhs = targets.shape[1]
    target = targets[...]
    image = back[...].reshape(rhs, TILE).T.astype(jnp.float32)
    once[...] = image

    def column_sum(value):
        return jnp.sum(value, axis=0, keepdims=True)

    line[0, 0:1, :] = column_sum(target * target)
    line[0, 1:2, :] = column_sum(target * image)
    line[0, 2:3, :] = column_sum(image * image)
    line[0, 5:8, :] = jnp.zeros((3, rhs), jnp.float32)
    greeted(column + plane)

    def remote(source, spot, send_sem, recv_sem, target):
        copy = pltpu.make_async_remote_copy(
            src_ref=source, dst_ref=spot, send_sem=send_sem, recv_sem=recv_sem,
            device_id=target, device_id_type=MESH,
        )
        copy.start()
        return copy

    copies = [
        remote(own.at[depth - step], land.at[z], send_sems.at[step], recv_sems.at[step], column[step - 1])
        for step in range(1, depth)
    ]
    land[z] = own[0]
    for copy in copies:
        copy.wait()
    again = land[...].reshape(rhs, TILE).T.astype(jnp.float32)
    twice[...] = again
    line[0, 3:4, :] = column_sum(target * again)
    line[0, 4:5, :] = column_sum(image * again)
    copies = [
        remote(line.at[0], line.at[step], line_sends.at[step], line_recvs.at[step], column[step - 1])
        for step in range(1, depth)
    ]
    for copy in copies:
        copy.wait()
    wide[0] = jnp.sum(line[...], axis=0)
    copies = [
        remote(wide.at[0], wide.at[step + 1], wide_sends.at[step], wide_recvs.at[step], peer)
        for step, peer in enumerate(plane)
    ]
    for copy in copies:
        copy.wait()
    total[...] = jnp.sum(wide[...], axis=0)


def find_tiles(n_col, groups, order):
    y, core, z, x = place()
    depth = n_col // 2

    def label(peer, step):
        other_y = lax.rem(y + peer // 4, 2)
        other_core = lax.rem(core + peer // 2 % 2, 2)
        other_x = lax.rem(x + peer % 2, 2)
        return groups[(2 * other_y + other_core) * n_col + 2 * lax.rem(z + step, depth) + other_x]

    labels = [label(peer, step) for peer in range(8) for step in range(depth)]
    count = jnp.int32(0)
    for level in range(depth):
        for block, other in enumerate(labels):
            if block == level:
                continue
            order[count] = block * depth + level
            count = count + (other == labels[level]).astype(jnp.int32)
    return count


def lift_rows(n_col, width, gathered, right):
    dims = gathered.shape[1] - width
    for level in range(n_col // 2):
        right[level] = lifted(gathered[level, pl.ds(width, dims), :], 1.0, 0, 3)


def build(width, gathered, block, level, left, right, spot):
    dims = gathered.shape[1] - width
    left[...] = lifted(gathered[block, pl.ds(width, dims), :], -2.0, 3, 0).T
    for start in range(0, TILE, CHUNK):
        rows = pl.ds(start, CHUNK)
        squared = jnp.dot(left[rows, :], right[level], preferred_element_type=jnp.float32)
        spot[rows, :] = wendland(squared)


def spot_of(depth, order, slot):
    return order[slot] // depth, lax.rem(order[slot], depth)


def first_kernel(n_col, groups, gathered, diagonal, evens, odds, narrow, order, left, right, spare, image):
    width = narrow.shape[1]
    depth, kept = n_col // 2, 2 * evens.shape[0]
    total = find_tiles(n_col, groups, order)
    stored = jnp.minimum(total, kept)
    pairs = stored // 2
    lift_rows(n_col, width, gathered, right)
    for level in range(depth):
        image[level] = jnp.dot(
            gathered[level, pl.ds(0, width), :], diagonal[level], preferred_element_type=jnp.float32
        )

    def make(slot, tile):
        block, level = spot_of(depth, order, slot)
        build(width, gathered, block, level, left, right, tile)

    def multiply(slot, tile):
        block, level = spot_of(depth, order, slot)
        image[level] += jnp.dot(
            gathered[block, pl.ds(0, width), :], tile[...], preferred_element_type=jnp.float32
        )

    odds[0] = jnp.zeros((TILE, TILE), jnp.bfloat16)

    def one_pair(pair, carry):
        before = jnp.maximum(pair - 1, 0)
        make(2 * pair, evens.at[pair])
        multiply(jnp.maximum(2 * pair - 1, 0), odds.at[before])
        make(2 * pair + 1, odds.at[pair])
        multiply(2 * pair, evens.at[pair])
        return carry

    def single(slot, carry):
        make(slot, evens.at[pairs])
        multiply(slot, evens.at[pairs])
        return carry

    def last_odd(slot, carry):
        multiply(slot, odds.at[pairs - 1])
        return carry

    def one_more(slot, carry):
        block, level = spot_of(depth, order, slot)
        build(width, gathered, block, level, left, right, spare)
        multiply(slot, spare)
        return carry

    lax.fori_loop(0, pairs, one_pair, 0)
    lax.fori_loop(jnp.maximum(2 * pairs - 1, 0), 2 * pairs, last_odd, 0)
    lax.fori_loop(2 * pairs, stored, single, 0)
    lax.fori_loop(stored, total, one_more, 0)
    narrow[...] = image[...].astype(jnp.bfloat16)


def second_kernel(n_col, groups, gathered, diagonal, source, evens, odds, narrow, order, left, right, spare, image):
    width = narrow.shape[1]
    depth, kept = n_col // 2, 2 * evens.shape[0]
    total = find_tiles(n_col, groups, order)
    stored = jnp.minimum(total, kept)
    pairs = stored // 2
    for level in range(depth):
        image[level] = jnp.dot(source[level], diagonal[level], preferred_element_type=jnp.float32)

    def multiply(slot, tile):
        block, level = spot_of(depth, order, slot)
        image[level] += jnp.dot(source[block], tile[...], preferred_element_type=jnp.float32)

    def one_pair(pair, carry):
        multiply(2 * pair, evens.at[pair])
        multiply(2 * pair + 1, odds.at[pair])
        return carry

    def single(slot, carry):
        multiply(slot, evens.at[pairs])
        return carry

    lax.fori_loop(0, pairs, one_pair, 0)
    lax.fori_loop(2 * pairs, stored, single, 0)

    @pl.when(total > kept)
    def _():
        lift_rows(n_col, width, gathered, right)

    def one_more(slot, carry):
        block, level = spot_of(depth, order, slot)
        build(width, gathered, block, level, left, right, spare)
        multiply(slot, spare)
        return carry

    lax.fori_loop(stored, total, one_more, 0)
    narrow[...] = image[...].astype(jnp.bfloat16)


def gathered_plan(points, lengthscale, noise_var, groups, targets):
    n_col = lax.axis_size("col")
    depth = n_col // 2
    blocks = groups.shape[0]
    dims = points.shape[0]
    rhs = targets.shape[1]
    width = rhs // depth
    scale = lengthscale[None, :]
    variance = noise_var[None, :]
    parts = len(level_groups(depth))

    vmem = pl.BlockSpec(memory_space=pltpu.VMEM)
    smem = pl.BlockSpec(memory_space=pltpu.SMEM)
    slices = jax.ShapeDtypeStruct((depth, width, TILE), jnp.bfloat16)
    whole = jax.ShapeDtypeStruct((TILE, rhs), jnp.float32)

    def remote(number):
        return pltpu.CompilerParams(
            collective_id=number, has_side_effects=True, vmem_limit_bytes=VMEM_LIMIT
        )

    gathered, diagonal = pl.pallas_call(
        functools.partial(first_gather, n_col),
        out_shape=[
            jax.ShapeDtypeStruct((8, depth, width + dims, TILE), jnp.bfloat16),
            jax.ShapeDtypeStruct((depth, TILE, TILE), jnp.bfloat16),
        ],
        in_specs=[vmem, vmem, vmem],
        out_specs=[vmem, vmem],
        scratch_shapes=[
            pltpu.VMEM((depth, width + dims, TILE), jnp.bfloat16),
            pltpu.SemaphoreType.DMA((depth - 1 + 14 * parts,)),
            pltpu.SemaphoreType.DMA((parts, 8, 2)),
            pltpu.SemaphoreType.DMA((depth,)),
            pltpu.SemaphoreType.DMA,
        ],
        compiler_params=remote(0),
        name="first_gather",
    )(points, scale, targets)
    gathered = gathered.reshape(blocks, width + dims, TILE)

    work = [
        pltpu.SMEM((depth * blocks,), jnp.int32),
        pltpu.VMEM((TILE, 2 * dims), jnp.bfloat16),
        pltpu.VMEM((depth, 2 * dims, TILE), jnp.bfloat16),
        pltpu.VMEM((TILE, TILE), jnp.bfloat16),
        pltpu.VMEM((depth, width, TILE), jnp.float32),
    ]
    evens, odds, first = pl.pallas_call(
        functools.partial(first_kernel, n_col),
        out_shape=[jax.ShapeDtypeStruct((KEPT // 2, TILE, TILE), jnp.bfloat16)] * 2 + [slices],
        in_specs=[smem, vmem, vmem],
        out_specs=[vmem, vmem, vmem],
        scratch_shapes=work,
        compiler_params=pltpu.CompilerParams(vmem_limit_bytes=VMEM_LIMIT),
        name="first_product",
    )(groups, gathered, diagonal)

    source, back = pl.pallas_call(
        functools.partial(second_gather, n_col),
        out_shape=[jax.ShapeDtypeStruct((8, depth, width, TILE), jnp.bfloat16), slices],
        in_specs=[vmem],
        out_specs=[vmem, vmem],
        scratch_shapes=[
            pltpu.SemaphoreType.DMA((depth - 1 + 14,)),
            pltpu.SemaphoreType.DMA((1, 8, 2)),
            pltpu.SemaphoreType.DMA((depth,)),
            pltpu.SemaphoreType.DMA((2,)),
        ],
        compiler_params=remote(1),
        name="second_gather",
    )(first)

    second = pl.pallas_call(
        functools.partial(second_kernel, n_col),
        out_shape=slices,
        in_specs=[smem, vmem, vmem, vmem, vmem, vmem],
        out_specs=vmem,
        scratch_shapes=work,
        compiler_params=pltpu.CompilerParams(vmem_limit_bytes=VMEM_LIMIT),
        name="second_product",
    )(groups, gathered, diagonal, source.reshape(blocks, width, TILE), evens, odds)

    total, image, again = pl.pallas_call(
        functools.partial(finish_kernel, n_col),
        out_shape=[jax.ShapeDtypeStruct((8, rhs), jnp.float32), whole, whole],
        in_specs=[vmem, vmem, vmem],
        out_specs=[vmem, vmem, vmem],
        scratch_shapes=[
            pltpu.VMEM((depth, width, TILE), jnp.bfloat16),
            pltpu.VMEM((depth, 8, rhs), jnp.float32),
            pltpu.VMEM((8, 8, rhs), jnp.float32),
        ]
        + [pltpu.SemaphoreType.DMA((depth,))] * 4
        + [pltpu.SemaphoreType.DMA((8,))] * 2,
        compiler_params=remote(2),
        name="finish",
    )(second, back, targets)

    tt, ty, yy, tz, yz = (total[place:place + 1] for place in range(5))
    step = tt / (variance * tt + ty)
    keep = 1.0 - step * variance
    after = keep * keep * tt - 2.0 * keep * step * ty + step * step * yy
    along = keep + after / tt
    squares = along * along * tt - 2.0 * along * step * ty + step * step * yy
    product = along * along * ty - along * step * (tz + yy) + step * step * yz
    second_step = after / (variance * squares + product)
    direction = along * targets - step * image
    applied = variance * direction + along * image - step * again
    solution_field = step * targets + second_step * direction
    residual = keep * targets - step * image - second_step * applied
    return (solution_field, residual)


def kernel_tile(row_coords, col_coords):
    row_norms = jnp.sum(row_coords * row_coords, axis=0)
    col_norms = jnp.sum(col_coords * col_coords, axis=0)
    crossed = lax.dot_general(
        row_coords,
        col_coords,
        (((0,), (0,)), ((), ())),
        precision=lax.Precision.HIGHEST,
        preferred_element_type=jnp.float32,
    )
    squared = jnp.maximum(row_norms[:, None] + col_norms[None, :] - 2.0 * crossed, 0.0)
    radius = jnp.sqrt(squared)
    support = jnp.maximum(1.0 - radius, 0.0)
    return (support**11 * (11.0 * radius + 1.0)).astype(jnp.bfloat16)


def per_device(points, lengthscale, noise_var, groups, targets):
    n_row = lax.axis_size("row")
    n_col = lax.axis_size("col")
    own_blocks = targets.shape[0] // TILE
    row_blocks = own_blocks * n_col
    col_blocks = own_blocks * n_row
    scaled = points / lengthscale[:, None]
    row_coords = lax.all_gather(scaled.astype(jnp.bfloat16), "col", axis=1, tiled=True).astype(
        scaled.dtype
    )
    col_coords = lax.all_gather(scaled.astype(jnp.bfloat16), "row", axis=1, tiled=True).astype(
        scaled.dtype
    )
    row_place = lax.axis_index("row")
    col_place = lax.axis_index("col")
    row_groups = lax.dynamic_slice_in_dim(groups, row_place * row_blocks, row_blocks, 0)
    col_groups = lax.dynamic_index_in_dim(
        groups.reshape(n_row, n_col, own_blocks), col_place, 1, keepdims=False
    ).reshape(col_blocks)
    flat_mask = (row_groups[:, None] == col_groups[None, :]).reshape(row_blocks * col_blocks)
    tile_count = jnp.sum(flat_mask.astype(jnp.int32))
    tile_order = jnp.nonzero(flat_mask, size=row_blocks * col_blocks, fill_value=0)[0].astype(
        jnp.int32
    )

    def square_sums(vector):
        return lax.psum(jnp.sum(vector * vector, axis=0), ("row", "col"))

    solution_field = jnp.zeros_like(targets)
    residual = targets
    direction = targets
    norm_now = square_sums(residual)
    for iteration in range(ITERS):
        narrow = direction.astype(jnp.bfloat16)
        operator_source = lax.all_gather(narrow, "row", axis=0, tiled=True)
        source = operator_source
        initial = jnp.zeros((row_blocks * TILE, RHS), jnp.float32)

        def one_tile(position, summed):
            flat_index = tile_order[position]
            row_slot = flat_index // col_blocks
            col_slot = flat_index % col_blocks
            left = lax.dynamic_slice_in_dim(row_coords, row_slot * TILE, TILE, 1)
            right = lax.dynamic_slice_in_dim(col_coords, col_slot * TILE, TILE, 1)
            values = kernel_tile(left, right)
            block_vec = lax.dynamic_slice_in_dim(source, col_slot * TILE, TILE, 0)
            product = jnp.dot(values, block_vec, preferred_element_type=jnp.float32)
            current = lax.dynamic_slice_in_dim(summed, row_slot * TILE, TILE, 0)
            return lax.dynamic_update_slice_in_dim(summed, current + product, row_slot * TILE, 0)

        partial_value = lax.fori_loop(0, tile_count, one_tile, initial)
        outgoing = partial_value.astype(jnp.bfloat16).reshape(n_col, own_blocks * TILE, RHS)
        incoming = lax.all_to_all(outgoing, "col", split_axis=0, concat_axis=0, tiled=True)
        operator_product = jnp.sum(incoming, axis=0, dtype=jnp.float32)
        image = noise_var[None, :] * direction + operator_product
        curve = lax.psum(jnp.sum(direction * image, axis=0), ("row", "col"))
        step_size = norm_now / curve
        solution_field = solution_field + step_size[None, :] * direction
        residual = residual - step_size[None, :] * image
        if iteration + 1 < ITERS:
            norm_next = square_sums(residual)
            direction = residual + (norm_next / norm_now)[None, :] * direction
            norm_now = norm_next
    return (solution_field, residual)


def solution(mesh):
    placed = (P(None, ("row", "col")), P(), P(), P(), P(("row", "col"), None))

    def plan(points, lengthscale, noise_var, groups, targets):
        blocks = groups.shape[0]
        square = mesh.shape["row"] == 4 and mesh.shape["col"] in (2, 4, 8, 16)
        whole_field = blocks <= GATHER_LIMIT and blocks == mesh.size and square
        run = gathered_plan if whole_field else per_device
        return run(points, lengthscale, noise_var, groups, targets)

    return jax.shard_map(
        plan,
        mesh=mesh,
        in_specs=placed,
        out_specs=(P(("row", "col"), None), P(("row", "col"), None)),
        check_vma=False,
    )
```
